32 devices in a mesh: grp: 2 (over x), gx: 16 (over z, y, core).
Axes of the slice: x: 2, y: 2, z: 4, core: 2. Of those that a mesh axis runs over, the one named last changes fastest.
Arguments:
- wave_state: float32 [4, 256, 96, 128], P('grp', 'gx'), parts along dimension 0, may hold values from -6 to 6
- layer_fields: float32 [8, 256, 96, 128], P('grp', 'gx'), parts along dimension 0, may hold values from -6 to 6
- source: float32 [512, 96, 128], P(('grp', 'gx')), parts along dimension 0, may hold values from -24 to 24
- filtered: float32 [512, 96, 128], P(('grp', 'gx')), parts along dimension 0, may hold values from -12 to 12
- frequency: float32 [2], P('grp'), parts along dimension 0, may hold values from 0.5 to 1.5
- start_time: float32 [2], P('grp'), parts along dimension 0, may hold values from 0 to 20
- speed_table: float32 [16], replicated, may hold values from 1.4 to 1.8
- speed_index: int32 [32, 12, 16], P('gx'), may hold values from 0 to 15
- pml_mask: int32 [32, 12, 16], P('gx'), may hold values from 0 to 7, as said below
Outputs:
- next_state: float32 [4, 256, 96, 128], P('grp', 'gx'), parts along dimension 0
- next_layer: float32 [8, 256, 96, 128], P('grp', 'gx'), parts along dimension 0
- next_filtered: float32 [512, 96, 128], P(('grp', 'gx')), parts along dimension 0
- filter_norm: float32 [2], P('grp'), parts along dimension 0
The draws below stay inside these ranges and needn't reach their ends.
There are 2 independent parts, one for each index of `grp`. The reference program is written for one: setup_inputs(seed, part) draws one part's arguments, and reference() takes and returns one part's arrays. A program takes and returns all parts, laid end to end along the dimension named above; an argument that names none is the same for every part. Nothing has to cross between parts.
Inputs may be any that keep to these rules, and one draw needn't show every extreme that they name: `pml_mask`: bit d of a block's value is 1 exactly where the block lies in the absorbing layer of a grid face normal to dimension d; the layer at each of the six faces is 2 to 4 blocks thick.
All inputs are finite; a program needn't handle non-finite values.
Results may differ from the reference program's by a relative error of at most 0.000068.
Values sent between devices are 32-bit elements; how exact they have to be, the bound alone decides.
No kernel may reach another device: no remote copies, remote signals or barrier semaphores. Data moves between devices by JAX's collectives and lax.ppermute only.
A program may use at most 64 MiB of HBM per device.

```python
import math
import jax
import jax.numpy as jnp
from jax import lax

CX = 16
NY = 96
NZ = 128
BLK = 8
PML = 32
NSPEED = 16
STEPS = 3
NX = 256
NBX = 32
NBY = 12
NBZ = 16


def brick_levels(key, extent, lowest, highest):
    return jnp.exp(jax.random.uniform(key, extent, jnp.float32, math.log(lowest), math.log(highest)))


def row_levels(levels):
    row_brick = jnp.arange(NX, dtype=jnp.int32) // CX
    return levels[..., row_brick]


def draw_wave_state(key, part):
    key = jax.random.fold_in(key, 14)
    level_key, value_key = jax.random.split(key)
    levels = row_levels(brick_levels(level_key, (2, NX // CX), 0.6, 4.8))
    x_pos = jnp.arange(NX, dtype=jnp.int32)[:, None, None]
    y_pos = jnp.arange(NY, dtype=jnp.int32)[None, :, None]
    z_pos = jnp.arange(NZ, dtype=jnp.int32)[None, None, :]
    parity = ((x_pos + y_pos + z_pos) % 2).astype(jnp.float32)
    signs = 1.0 - 2.0 * parity
    extent = (2, NX, NY, NZ)
    values = jax.random.normal(value_key, extent, jnp.float32)
    return jnp.clip(values * levels[:, :, None, None] * signs[None], -6.0, 6.0)


def draw_source(key, part):
    key = jax.random.fold_in(key, 11)
    level_key, value_key = jax.random.split(key)
    levels = row_levels(brick_levels(level_key, (NX // CX,), 0.5, 2.0))[:, None, None]
    extent = (NX, NY, NZ)
    values = 4.0 * jax.random.normal(value_key, extent, jnp.float32) * levels
    return jnp.clip(values, -24.0, 24.0)


def draw_filtered(key, part):
    key = jax.random.fold_in(key, 12)
    level_key, value_key = jax.random.split(key)
    levels = row_levels(brick_levels(level_key, (NX // CX,), 0.5, 2.0))[:, None, None]
    extent = (NX, NY, NZ)
    x_frac = jnp.arange(NX, dtype=jnp.float32)[:, None, None] / (NX - 1)
    y_frac = jnp.arange(NY, dtype=jnp.float32)[None, :, None] / (NY - 1)
    row_scale = jnp.exp(1.151293 * (x_frac + y_frac))
    values = jax.random.normal(value_key, extent, jnp.float32)
    return jnp.clip(0.2 * values * row_scale * levels, -12.0, 12.0)


def draw_pml_mask(key, part):
    key = jax.random.fold_in(key, 13)
    thinnest = PML // (2 * BLK)
    thickest = PML // BLK
    thickness = jax.random.randint(key, (6,), thinnest, thickest + 1)
    x_pos = jnp.arange(NBX, dtype=jnp.int32)[:, None, None]
    y_pos = jnp.arange(NBY, dtype=jnp.int32)[None, :, None]
    z_pos = jnp.arange(NBZ, dtype=jnp.int32)[None, None, :]
    in_first = ((x_pos < thickness[0]) | (x_pos >= NBX - thickness[1])).astype(jnp.int32)
    in_second = ((y_pos < thickness[2]) | (y_pos >= NBY - thickness[3])).astype(jnp.int32)
    in_third = ((z_pos < thickness[4]) | (z_pos >= NBZ - thickness[5])).astype(jnp.int32)
    return jnp.broadcast_to(in_first + 2 * in_second + 4 * in_third, (NBX, NBY, NBZ)).astype(jnp.int32)


def touch_ends(array, rng, least, top_value):
    spot = [jax.random.randint(jax.random.fold_in(rng, axis), (), 0, length) for axis, length in enumerate(array.shape)]
    longest = array.shape.index(max(array.shape))
    beside = spot[:longest] + [(spot[longest] + 1) % array.shape[longest]] + spot[longest + 1:]
    return array.at[tuple(spot)].set(least).at[tuple(beside)].set(top_value)


def block_levels(own_key, shape, cuts, low, largest):
    def one(position, parts):
        steps = jax.random.uniform(jax.random.fold_in(jax.random.fold_in(own_key, 6), position), (parts,), jnp.float32, low / len(cuts), largest / len(cuts))
        return jnp.repeat(jnp.exp(steps), shape[position] // parts).reshape((-1,) + (1,) * (len(shape) - position - 1))

    gain = one(*cuts[0])
    for cut in cuts[1:]:
        gain = gain * one(*cut)
    return gain


def normal_values(rng, shape, width, limit, cuts=(), kind=jnp.bfloat16):
    entries = jax.random.normal(rng, shape, jnp.float32) * width
    if len(cuts) > 0:
        entries = block_levels(rng, shape, cuts, -0.22, 0.18) * entries
    return jnp.clip(entries, min=-limit, max=limit).astype(kind)


def setup_inputs(seed: int = 0, part: int = 0) -> dict:
    arg_keys = jax.random.split(jax.random.key(seed), 10)
    part_keys = jax.random.split(jax.random.fold_in(arg_keys[9], part), 10)
    return {
        "wave_state": draw_wave_state(jax.random.fold_in(jax.random.fold_in(arg_keys[9], part), 71), part),
        "layer_fields": normal_values(part_keys[1], (4, NX, NY, NZ), 1.0, 6.0, ((1, 16),), jnp.float32),
        "source": draw_source(jax.random.fold_in(jax.random.fold_in(arg_keys[9], part), 71), part),
        "filtered": draw_filtered(jax.random.fold_in(jax.random.fold_in(arg_keys[9], part), 71), part),
        "frequency": jnp.clip(jax.random.uniform(part_keys[4], (1,), jnp.float32, 0.5, 1.5), 0.5, 1.5),
        "start_time": jnp.clip(jax.random.uniform(part_keys[5], (1,), jnp.float32, 0.0, 20.0), 0.0, 20.0),
        "speed_table": jnp.clip(jax.random.uniform(arg_keys[6], (NSPEED,), jnp.float32, 1.4, 1.8), 1.4, 1.8),
        "speed_index": touch_ends(jax.random.randint(arg_keys[7], (NBX, NBY, NBZ), 0, NSPEED), jax.random.fold_in(arg_keys[7], 1), 0, NSPEED - 1).astype(jnp.int32),
        "pml_mask": draw_pml_mask(jax.random.fold_in(arg_keys[9], 71), part),
    }


TIME_STEP = 0.25
DAMP_PEAK = 1.5
STENCIL = (-205.0 / 72.0, 8.0 / 5.0, -1.0 / 5.0, 8.0 / 315.0, -1.0 / 560.0)

def expand(blocks, factor):
    first_len, second_len, third_len = blocks.shape
    widened = jnp.broadcast_to(blocks[:, None, :, None, :, None], (first_len, factor, second_len, factor, third_len, factor))
    return widened.reshape(first_len * factor, second_len * factor, third_len * factor)

def speed_squares(speed_index, speed_table):
    levels = jnp.arange(speed_table.shape[0], dtype=jnp.int32)
    picked = jnp.where(speed_index[..., None] == levels, speed_table, jnp.zeros_like(speed_table))
    speeds = lax.optimization_barrier(jnp.sum(picked, axis=-1))
    return speeds * speeds

def layer_bits(pml_mask):
    return [expand((pml_mask // 2 ** direction % 2).astype(jnp.float32), BLK) for direction in range(3)]

def layer_terms(bits):
    damp_rates = [DAMP_PEAK * bit_field for bit_field in bits]
    damping = damp_rates[0] + damp_rates[1] + damp_rates[2]
    pairing = damp_rates[0] * damp_rates[1] + damp_rates[1] * damp_rates[2] + damp_rates[2] * damp_rates[0]
    retention = [jnp.exp(-TIME_STEP * rate_field) for rate_field in damp_rates]
    decay_factor = jnp.exp(-TIME_STEP * damping)
    return (damping, pairing, retention, decay_factor)

def pad_along(field, dimension):
    widths = [(0, 0), (0, 0), (0, 0)]
    widths[dimension] = (4, 4)
    return jnp.pad(field, widths)

def along_axis(padded, center_count, dimension):
    accumulated = STENCIL[0] * lax.slice_in_dim(padded, 4, 4 + center_count, axis=dimension)
    for offset in range(1, 5):
        upper = lax.slice_in_dim(padded, 4 + offset, 4 + offset + center_count, axis=dimension)
        lower = lax.slice_in_dim(padded, 4 - offset, 4 - offset + center_count, axis=dimension)
        accumulated = accumulated + STENCIL[offset] * (upper + lower)
    return accumulated

def advance(second_diffs, displace, previous, memory, stiff_memory, source, speed_square, bits, layer_consts, forcing_phase):
    damping, pairing, retention, decay_factor = layer_consts
    memory = [retention[direction] * memory[direction] + (1.0 - retention[direction]) * second_diffs[direction] for direction in range(3)]
    stiff_memory = decay_factor * stiff_memory + TIME_STEP * pairing * displace
    layered = bits[0] * memory[0] + bits[1] * memory[1] + bits[2] * memory[2]
    acceleration = speed_square * (second_diffs[0] + second_diffs[1] + second_diffs[2] - layered) - pairing * displace - damping * stiff_memory - source * forcing_phase
    half_damp = 0.5 * TIME_STEP * damping
    updated = (2.0 * displace - (1.0 - half_damp) * previous + TIME_STEP * TIME_STEP * acceleration) / (1.0 + half_damp)
    return (updated, memory, stiff_memory)

def filter_weight(angular, start_clock, count):
    return TIME_STEP * angular / math.pi * (jnp.cos(angular * (start_clock + count * TIME_STEP)) - 0.25)

def reference(wave_state, layer_fields, source, filtered, frequency, start_time, speed_table, speed_index, pml_mask):
    angular = frequency[0]
    start_clock = start_time[0]
    bits = layer_bits(pml_mask)
    speed_square = expand(speed_squares(speed_index, speed_table), BLK)
    layer_consts = layer_terms(bits)
    displace = wave_state[0]
    previous = wave_state[1]
    memory = [layer_fields[0], layer_fields[1], layer_fields[2]]
    stiff_memory = layer_fields[3]
    for step_number in range(STEPS):
        second_diffs = [along_axis(pad_along(displace, dimension), displace.shape[dimension], dimension) for dimension in range(3)]
        forcing_phase = jnp.cos(angular * (start_clock + step_number * TIME_STEP))
        updated, memory, stiff_memory = advance(second_diffs, displace, previous, memory, stiff_memory, source, speed_square, bits, layer_consts, forcing_phase)
        previous = displace
        displace = updated
        filtered = filtered + filter_weight(angular, start_clock, step_number + 1) * displace
    filter_norm = jnp.sqrt(jnp.sum(filtered * filtered) / filtered.size + 1e-06)
    return (jnp.stack([displace, previous]), jnp.stack(memory + [stiff_memory]), filtered, filter_norm.reshape(1))
```

```python
import functools
import math

import jax
import jax.numpy as jnp
from jax import lax
from jax.experimental import pallas as pl
from jax.experimental.pallas import tpu as pltpu
from jax.sharding import PartitionSpec as P

F32 = jnp.float32
BF16 = jnp.bfloat16
STEPS = 3
BLK = 8
REACH = 4
TIME_STEP = 0.25
DAMP_PEAK = 1.5
STENCIL = (-205.0 / 72.0, 8.0 / 5.0, -1.0 / 5.0, 8.0 / 315.0, -1.0 / 560.0)
SCALE = 5040.0
WHOLE = (-14336.0, 8064.0, -1008.0, 128.0, -9.0)
CENTRE_REST = 14.0 / SCALE
TAG_ROWS = 16
KAPPA, KAPPA_R, Q0, Q1, Q2, B0, B1, B2, DECAY, PAIR, AMP, BACK, STIFF, FORCE = range(14)
N_COEF = 14
VMEM_LIMIT = 30 * 1024 * 1024


def band(rows, cols, row_period, col_period):
    row = lax.broadcasted_iota(jnp.int32, (rows, cols), 0) % row_period
    col = lax.broadcasted_iota(jnp.int32, (rows, cols), 1) % col_period
    apart = jnp.abs(row - col)
    out = jnp.zeros((rows, cols), F32)
    for offset, value in enumerate(WHOLE):
        out = jnp.where(apart == offset, value, out)
    return out.astype(BF16)


def pieces(cells):
    high = cells.astype(BF16)
    return high, (cells - high.astype(F32)).astype(BF16)


def cross_diffs(planes, read, write_y, write_z, ny, nz):
    mat_y = band(ny, 2 * ny, ny, ny)
    mat_z = band(2 * nz, nz, nz, nz)
    for one, two in zip(planes[0::2], planes[1::2]):
        high_one, low_one = pieces(read(one))
        high_two, low_two = pieces(read(two))
        upper = jnp.concatenate([high_one, high_two], axis=1)
        lower = jnp.concatenate([low_one, low_two], axis=1)
        diff_y = jnp.dot(
            mat_y, jnp.concatenate([upper, lower], axis=0), preferred_element_type=F32
        )
        write_y(one, diff_y[:, :nz])
        write_y(two, diff_y[:, nz:])
        left = jnp.concatenate([high_one, low_one], axis=1)
        right = jnp.concatenate([high_two, low_two], axis=1)
        diff_z = jnp.dot(
            jnp.concatenate([left, right], axis=0), mat_z, preferred_element_type=F32
        )
        write_z(one, diff_z[:ny])
        write_z(two, diff_z[ny:])


def first_diff(cells, at):
    total = STENCIL[0] * cells[at]
    for offset in range(1, REACH + 1):
        above, below = cells.get(at + offset), cells.get(at - offset)
        if above is not None and below is not None:
            total = total + STENCIL[offset] * (above + below)
        elif above is not None:
            total = total + STENCIL[offset] * above
        elif below is not None:
            total = total + STENCIL[offset] * below
    return total


def outer_part(cells, at, positions):
    total = None
    for position in positions:
        offset = abs(position - at)
        if offset <= REACH:
            term = STENCIL[offset] * cells[position]
            total = term if total is None else total + term
    return total


def advance(cells, previous, memory, stiff, forcing, diffs, co, phase):
    rest = CENTRE_REST * cells
    diffs = [diffs[0], diffs[1] * (1.0 / SCALE) - rest, diffs[2] * (1.0 / SCALE) - rest]
    memory = [m + co(Q0 + d) * (diffs[d] - m) for d, m in enumerate(memory)]
    inner = sum(diffs[d] - co(B0 + d) * memory[d] for d in range(3))
    stiff = co(DECAY) * stiff + co(PAIR) * cells
    new = (
        co(AMP) * cells
        - co(BACK) * previous
        + co(KAPPA) * inner
        - co(STIFF) * stiff
        - (co(FORCE) * phase) * forcing
    )
    return new, memory, stiff


def coefficients(speed_square, bits):
    rates = [DAMP_PEAK * bit for bit in bits]
    damping = rates[0] + rates[1] + rates[2]
    pairing = rates[0] * rates[1] + rates[1] * rates[2] + rates[2] * rates[0]
    retention = [jnp.exp(-TIME_STEP * rate) for rate in rates]
    half = 0.5 * TIME_STEP * damping
    inverse = 1.0 / (1.0 + half)
    square = TIME_STEP * TIME_STEP
    kappa = square * speed_square * inverse
    return (
        kappa,
        kappa * retention[0],
        1.0 - retention[0],
        1.0 - retention[1],
        1.0 - retention[2],
        bits[0],
        bits[1],
        bits[2],
        jnp.exp(-TIME_STEP * damping),
        TIME_STEP * pairing,
        (2.0 - square * pairing) * inverse,
        (1.0 - half) * inverse,
        square * damping * inverse,
        square * inverse,
    )


def spread(tile, ny, nz):
    row = lax.broadcasted_iota(jnp.int32, (ny, TAG_ROWS), 0) // BLK
    col = lax.broadcasted_iota(jnp.int32, (ny, TAG_ROWS), 1)
    down = (row == col).astype(F32).astype(BF16)
    row = lax.broadcasted_iota(jnp.int32, (nz, nz), 0)
    col = lax.broadcasted_iota(jnp.int32, (nz, nz), 1) // BLK
    along = (row == col).astype(F32).astype(BF16)
    wide = jnp.dot(tile.astype(BF16), along, preferred_element_type=F32)
    return jnp.dot(down, wide.astype(BF16), preferred_element_type=F32)


def medium(index_tile, mask_tile, table, ny, nz):
    index = spread(index_tile, ny, nz)
    mask = spread(mask_tile, ny, nz).astype(jnp.int32)
    speed = jnp.zeros((ny, nz), F32)
    for entry in range(table.shape[0]):
        speed = jnp.where(index == float(entry), table[entry], speed)
    bits = [((mask >> direction) & 1).astype(F32) for direction in range(3)]
    return speed * speed, bits


def phase_at(freq, start, count):
    angle = freq[0] * (start[0] + count * TIME_STEP)
    return jnp.cos(jnp.full((BLK, 128), angle, F32))


def weight_at(freq, start, count):
    return (TIME_STEP * freq[0] / math.pi) * (phase_at(freq, start, count) - 0.25)


def over_rows(ny, step):
    def one(block, carry):
        step(pl.multiple_of(block * BLK, BLK))
        return carry

    lax.fori_loop(0, ny // BLK, one, 0)


def is_even():
    return lax.axis_index("gx") % 2 == 0


def send_kernel(
    wave, layer, source, freq, start, table, index, mask,
    inside, across, coef,
    u0, strips, diff_y, diff_z, tags, sems,
):
    nx, ny, nz = u0.shape
    n_block = nx // BLK
    edges = (0, nx - REACH)
    copies = [pltpu.make_async_copy(wave.at[0], u0, sems.at[0])]
    for side in range(2):
        at = pl.ds(edges[side], REACH)
        copies += [
            pltpu.make_async_copy(wave.at[1, at], strips.at[side, 0], sems.at[1 + 3 * side]),
            pltpu.make_async_copy(
                layer.at[:, at], strips.at[side, pl.ds(1, 4)], sems.at[2 + 3 * side]
            ),
            pltpu.make_async_copy(source.at[at], strips.at[side, 5], sems.at[3 + 3 * side]),
        ]
    for copy in copies:
        copy.start()
    even = is_even()
    tags[...] = jnp.zeros_like(tags)
    for block in range(n_block):
        tags[block, 0, : index.shape[1], : index.shape[2]] = index[block].astype(F32)
        tags[block, 1, : mask.shape[1], : mask.shape[2]] = mask[block].astype(F32)
    for block in range(n_block):
        square, bits = medium(tags[block, 0], tags[block, 1], table, ny, nz)
        for entry, value in enumerate(coefficients(square, bits)):
            coef[entry, block] = value
    phase = phase_at(freq, start, 0)
    copies[0].wait()
    edge_planes = [*range(REACH), *range(nx - REACH, nx)]
    slot = {plane: number for number, plane in enumerate(edge_planes)}

    def put_y(plane, value):
        diff_y[slot[plane]] = value

    def put_z(plane, value):
        diff_z[slot[plane]] = value

    cross_diffs(edge_planes, lambda plane: u0[plane], put_y, put_z, ny, nz)
    for copy in copies[1:]:
        copy.wait()

    def step(rows):
        at = pl.ds(rows, BLK)
        sides = []
        for side in range(2):
            block = side * (n_block - 1)
            reach = range(2 * REACH) if side == 0 else range(nx - 2 * REACH, nx)
            cells = {plane: u0[plane, at] for plane in reach}
            co = {}

            def get(entry):
                if entry not in co:
                    co[entry] = coef[entry, block, at]
                return co[entry]

            values = []
            for number in range(REACH):
                plane = edges[side] + number
                new, _, _ = advance(
                    cells[plane],
                    strips[side, 0, number, at],
                    [strips[side, 1 + d, number, at] for d in range(3)],
                    strips[side, 4, number, at],
                    strips[side, 5, number, at],
                    [
                        first_diff(cells, plane),
                        diff_y[slot[plane], at],
                        diff_z[slot[plane], at],
                    ],
                    get,
                    phase,
                )
                values.append((cells[plane], new))
            sides.append(values)
        for number in range(REACH):
            for part in range(2):
                to = pl.ds(pl.multiple_of((part * REACH + number) * ny + rows, BLK), BLK)
                left, right = sides[0][number][part], sides[1][number][part]
                inside[to] = jnp.where(even, right, left)
                across[to] = jnp.where(even, left, right)

    over_rows(ny, step)
    for part in range(2):
        to = pl.ds(2 * REACH * ny + part * TAG_ROWS, TAG_ROWS)
        left, right = tags[0, part], tags[n_block - 1, part]
        inside[to] = jnp.where(even, right, left)
        across[to] = jnp.where(even, left, right)


def local_kernel(
    wave, layer, source, filtered, freq, start, coef,
    inside, across, u0, forcing, running, state, memory, stiff,
    prev, mem_in, diff_y, diff_z, sems,
):
    nx, ny, nz = u0.shape
    copies = [
        pltpu.make_async_copy(wave.at[0], u0, sems.at[0]),
        pltpu.make_async_copy(wave.at[1], prev, sems.at[1]),
        pltpu.make_async_copy(layer, mem_in, sems.at[2]),
        pltpu.make_async_copy(source, forcing, sems.at[3]),
        pltpu.make_async_copy(filtered, running, sems.at[4]),
    ]
    for copy in copies:
        copy.start()
    even = is_even()
    phases = [phase_at(freq, start, count) for count in range(2)]
    copies[0].wait()

    def put_y(plane, value):
        diff_y[plane] = value

    def put_z(plane, value):
        diff_z[plane] = value

    cross_diffs(range(nx), lambda plane: u0[plane], put_y, put_z, ny, nz)
    for copy in copies[1:]:
        copy.wait()

    def first(rows):
        at = pl.ds(rows, BLK)
        cells = {plane: u0[plane, at] for plane in range(nx)}
        for plane in range(nx):
            new, mem, sti = advance(
                cells[plane],
                prev[plane, at],
                [mem_in[d, plane, at] for d in range(3)],
                mem_in[3, plane, at],
                forcing[plane, at],
                [first_diff(cells, plane), diff_y[plane, at], diff_z[plane, at]],
                lambda entry, block=plane // BLK: coef[entry, block, at],
                phases[0],
            )
            state[plane, at] = new
            for d in range(3):
                memory[d, plane, at] = mem[d]
            stiff[plane, at] = sti

    over_rows(ny, first)
    edge_planes = [*range(REACH), *range(nx - REACH, nx)]
    cross_diffs(edge_planes, lambda plane: state[plane], put_y, put_z, ny, nz)

    def second(rows):
        at = pl.ds(rows, BLK)
        cells = {plane: state[plane, at] for plane in range(nx)}
        values = {}
        for plane in edge_planes:
            values[plane], _, _ = advance(
                cells[plane],
                u0[plane, at],
                [memory[d, plane, at] for d in range(3)],
                stiff[plane, at],
                forcing[plane, at],
                [first_diff(cells, plane), diff_y[plane, at], diff_z[plane, at]],
                lambda entry, block=plane // BLK: coef[entry, block, at],
                phases[1],
            )
        for number in range(REACH):
            left, right = values[number], values[nx - REACH + number]
            inside[number, at] = jnp.where(even, right, left)
            across[number, at] = jnp.where(even, left, right)

    over_rows(ny, second)


def joint_kernel(
    freq, start, table, coef, inside, across, u0, forcing, running, state, memory, stiff,
    out_state, out_layer, out_filtered, edge_new, edge_memory, edge_running, ghost, partial,
    ext, bump, push, new, field, tail, ghost_coef, diff_y, diff_z, bump_y, bump_z, sems,
):
    nx, ny, nz = u0.shape
    count = lax.axis_size("gx")
    place = lax.axis_index("gx")
    even = is_even()
    n_block = nx // BLK
    present = (
        jnp.where(place > 0, 1.0, 0.0).astype(F32),
        jnp.where(place < count - 1, 1.0, 0.0).astype(F32),
    )
    phases = [phase_at(freq, start, number) for number in range(STEPS)]
    weights = [weight_at(freq, start, number + 1) for number in range(STEPS)]

    def received(to):
        one, two = inside[to], across[to]
        return jnp.where(even, two, one), jnp.where(even, one, two)

    tag_at = 2 * REACH * ny
    tiles = [received(pl.ds(tag_at + part * TAG_ROWS, TAG_ROWS)) for part in range(2)]
    for side in range(2):
        square, bits = medium(tiles[0][side], tiles[1][side], table, ny, nz)
        values = coefficients(square * present[side], bits)
        pairing, damping = values[PAIR] * (1.0 / TIME_STEP), DAMP_PEAK * (bits[0] + bits[1] + bits[2])
        inverse = values[FORCE] * (1.0 / (TIME_STEP * TIME_STEP))
        grown = (
            2.0 - TIME_STEP * TIME_STEP * pairing * (1.0 + TIME_STEP * damping)
        ) * inverse
        kappa = values[KAPPA]
        for entry, value in enumerate(
            (
                values[KAPPA_R],
                values[Q0],
                kappa * (1.0 - values[Q1]),
                kappa * (1.0 - values[Q2]),
                grown,
            )
        ):
            ghost_coef[side, entry] = value

    ghosts = (range(-REACH, 0), range(nx, nx + REACH))
    owned = (range(REACH), range(nx - REACH, nx))

    def exchange(rows):
        at = pl.ds(rows, BLK)
        halo = {}
        sent = {}
        for number in range(REACH):
            to = pl.ds(pl.multiple_of(number * ny + rows, BLK), BLK)
            halo[-REACH + number], halo[nx + number] = received(to)
            to = pl.ds(pl.multiple_of((REACH + number) * ny + rows, BLK), BLK)
            sent[-REACH + number], sent[nx + number] = received(to)
        for side in range(2):
            block = side * (n_block - 1)
            mine = {plane: u0[plane, at] for plane in owned[side]}
            kappa_r, q0 = coef[KAPPA_R, block, at], coef[Q0, block, at]
            for plane in owned[side]:
                outer = outer_part(halo, plane, ghosts[side])
                ext[plane + REACH, at] = state[plane, at] + kappa_r * outer
                number = plane - owned[side][0]
                edge_memory[side, number, at] = memory[0, plane, at] + q0 * outer
            kappa_r = ghost_coef[side, 0, at]
            for position in ghosts[side]:
                outer = outer_part(mine, position, owned[side])
                added = kappa_r * outer
                number = position - ghosts[side][0]
                bump[side * REACH + number, at] = added
                push[side, number, at] = outer
                ext[position + REACH, at] = sent[position] + added
        for plane in range(REACH, nx - REACH):
            ext[plane + REACH, at] = state[plane, at]

    over_rows(ny, exchange)

    def put_y(plane, value):
        diff_y[plane] = value

    def put_z(plane, value):
        diff_z[plane] = value

    cross_diffs(range(nx), lambda plane: ext[plane + REACH], put_y, put_z, ny, nz)

    def put_bump_y(plane, value):
        bump_y[plane] = value

    def put_bump_z(plane, value):
        bump_z[plane] = value

    cross_diffs(range(2 * REACH), lambda plane: bump[plane], put_bump_y, put_bump_z, ny, nz)

    def second(rows):
        at = pl.ds(rows, BLK)
        cells = {plane: ext[plane + REACH, at] for plane in range(-REACH, nx + REACH)}
        for plane in range(nx):
            if plane < REACH:
                mem0 = edge_memory[0, plane, at]
            elif plane >= nx - REACH:
                mem0 = edge_memory[1, plane - nx + REACH, at]
            else:
                mem0 = memory[0, plane, at]
            value, mem, sti = advance(
                cells[plane],
                u0[plane, at],
                [mem0, memory[1, plane, at], memory[2, plane, at]],
                stiff[plane, at],
                forcing[plane, at],
                [first_diff(cells, plane), diff_y[plane, at], diff_z[plane, at]],
                lambda entry, block=plane // BLK: coef[entry, block, at],
                phases[1],
            )
            new[plane, at] = value
            for d in range(3):
                field[d, plane, at] = mem[d]
            field[3, plane, at] = sti
            tail[plane, at] = running[plane, at] + weights[0] * cells[plane] + weights[1] * value
        for side in range(2):
            kappa_r, q0, kappa_1, kappa_2, grown = [
                ghost_coef[side, entry, at] for entry in range(5)
            ]
            added = {
                position: bump[side * REACH + position - ghosts[side][0], at]
                for position in ghosts[side]
            }
            for position in ghosts[side]:
                number = position - ghosts[side][0]
                value = added[position]
                rest = CENTRE_REST * value
                along = first_diff(added, position) + outer_part(cells, position, owned[side])
                side_y = bump_y[side * REACH + number, at] * (1.0 / SCALE) - rest
                side_z = bump_z[side * REACH + number, at] * (1.0 / SCALE) - rest
                ghost[side * REACH + number, at] = (
                    grown * value
                    + kappa_r * (along - q0 * push[side, number, at])
                    + kappa_1 * side_y
                    + kappa_2 * side_z
                )

    over_rows(ny, second)
    inner = pl.ds(REACH, nx - 2 * REACH)
    writes = [pltpu.make_async_copy(new, out_state.at[1], sems.at[0])]
    writes[0].start()
    cross_diffs(range(nx), lambda plane: new[plane], put_y, put_z, ny, nz)
    partial[...] = jnp.zeros_like(partial)

    def third(rows):
        at = pl.ds(rows, BLK)
        cells = {plane: new[plane, at] for plane in range(nx)}
        total = partial[...]
        for plane in range(nx):
            value, mem, sti = advance(
                cells[plane],
                ext[plane + REACH, at],
                [field[d, plane, at] for d in range(3)],
                field[3, plane, at],
                forcing[plane, at],
                [first_diff(cells, plane), diff_y[plane, at], diff_z[plane, at]],
                lambda entry, block=plane // BLK: coef[entry, block, at],
                phases[2],
            )
            done = tail[plane, at] + weights[2] * value
            for d in range(1, 3):
                field[d, plane, at] = mem[d]
            field[3, plane, at] = sti
            if REACH <= plane < nx - REACH:
                field[0, plane, at] = mem[0]
                bump_plane = plane
                ext[bump_plane + REACH, at] = value
                tail[plane, at] = done
                total = total + done * done
            else:
                side = 0 if plane < REACH else 1
                number = plane if side == 0 else plane - nx + REACH
                edge_new[side, number, at] = value
                edge_memory[side, number, at] = mem[0]
                edge_running[side, number, at] = done
        partial[...] = total

    over_rows(ny, third)
    own = pl.ds(2 * REACH, nx - 2 * REACH)
    writes += [
        pltpu.make_async_copy(ext.at[own], out_state.at[0, inner], sems.at[1]),
        pltpu.make_async_copy(field.at[0, inner], out_layer.at[0, inner], sems.at[2]),
        pltpu.make_async_copy(field.at[pl.ds(1, 3)], out_layer.at[pl.ds(1, 3)], sems.at[3]),
        pltpu.make_async_copy(tail.at[inner], out_filtered.at[inner], sems.at[4]),
    ]
    for write in writes[1:]:
        write.start()
    for write in writes:
        write.wait()


def finish_kernel(
    freq, start, coef, inside, across, edge_new, edge_memory, edge_running, ghost, partial,
    state_in, layer_in, filtered_in,
    out_state, out_layer, out_filtered, total_out,
    last, layer_last, tail, sems,
):
    del state_in, layer_in, filtered_in
    nx = out_state.shape[1]
    ny = out_state.shape[2]
    n_block = nx // BLK
    even = is_even()
    weight = weight_at(freq, start, STEPS)
    total_out[...] = partial[...]
    ghosts = (range(-REACH, 0), range(nx, nx + REACH))
    owned = (range(REACH), range(nx - REACH, nx))

    def step(rows):
        at = pl.ds(rows, BLK)
        halo = {}
        for number in range(REACH):
            one, two = inside[number, at], across[number, at]
            halo[-REACH + number] = jnp.where(even, two, one) + ghost[number, at]
            halo[nx + number] = jnp.where(even, one, two) + ghost[REACH + number, at]
        total = total_out[...]
        for side in range(2):
            block = side * (n_block - 1)
            kappa_r, q0 = coef[KAPPA_R, block, at], coef[Q0, block, at]
            for number, plane in enumerate(owned[side]):
                outer = outer_part(halo, plane, ghosts[side])
                added = kappa_r * outer
                last[side, number, at] = edge_new[side, number, at] + added
                layer_last[side, number, at] = edge_memory[side, number, at] + q0 * outer
                done = edge_running[side, number, at] + weight * added
                tail[side, number, at] = done
                total = total + done * done
        total_out[...] = total

    over_rows(ny, step)
    writes = []
    for side in range(2):
        at = pl.ds(owned[side][0], REACH)
        writes += [
            pltpu.make_async_copy(last.at[side], out_state.at[0, at], sems.at[3 * side]),
            pltpu.make_async_copy(layer_last.at[side], out_layer.at[0, at], sems.at[3 * side + 1]),
            pltpu.make_async_copy(tail.at[side], out_filtered.at[at], sems.at[3 * side + 2]),
        ]
    for write in writes:
        write.start()
    for write in writes:
        write.wait()


ANY = pl.BlockSpec(memory_space=pl.ANY)
VEC = pl.BlockSpec(memory_space=pltpu.VMEM)
SCALAR = pl.BlockSpec(memory_space=pltpu.SMEM)


def held(*shape):
    return pltpu.VMEM(shape, F32)


def in_vmem(*arrays):
    return [pltpu.with_memory_space_constraint(array, pltpu.VMEM) for array in arrays]


def call(kernel, name, in_specs, out_shape, out_specs, scratch, operands, micros, aliases=None):
    return pl.pallas_call(
        kernel,
        name=name,
        in_specs=in_specs,
        out_shape=out_shape,
        out_specs=out_specs,
        scratch_shapes=scratch,
        input_output_aliases=aliases or {},
        compiler_params=pltpu.CompilerParams(vmem_limit_bytes=VMEM_LIMIT),
        cost_estimate=pl.CostEstimate(
            flops=0, bytes_accessed=int(micros * 3.6e6), transcendentals=0
        ),
    )(*operands)


def swap_pairs(count):
    inside = [(i, i ^ 1) for i in range(count)]
    across = []
    for i in range(1, count - 1, 2):
        across += [(i, i + 1), (i + 1, i)]
    return inside, across


def total_over(values, axis):
    count = lax.axis_size(axis)
    if count & (count - 1):
        return lax.psum(values, axis)
    hop = 1
    while hop < count:
        values = values + lax.ppermute(values, axis, [(i, i ^ hop) for i in range(count)])
        hop *= 2
    return values


def body(
    wave_state, layer_fields, source, filtered, frequency, start_time, speed_table, speed_index,
    pml_mask,
):
    _, nx, ny, nz = wave_state.shape
    n_block = nx // BLK
    count = lax.axis_size("gx")
    pair_inside, pair_across = swap_pairs(count)
    brick = (nx, ny, nz)
    strip = (REACH, ny, nz)
    message = (2 * REACH * ny + 2 * TAG_ROWS, nz)
    dma = pltpu.SemaphoreType.DMA
    vec = lambda *shape: pltpu.VMEM(shape, F32)

    inside, across, coef = call(
        send_kernel,
        "strips",
        [ANY] * 3 + [SCALAR] * 3 + [VEC] * 2,
        [held(*message), held(*message), held(N_COEF, n_block, ny, nz)],
        [VEC] * 3,
        [
            vec(*brick),
            vec(2, 6, *strip),
            vec(2 * REACH, ny, nz),
            vec(2 * REACH, ny, nz),
            vec(n_block, 2, TAG_ROWS, 128),
            dma((7,)),
        ],
        (
            wave_state, layer_fields, source, frequency, start_time, speed_table, speed_index,
            pml_mask,
        ),
        2.5,
    )
    got_inside = lax.ppermute(inside, "gx", pair_inside)
    got_across = lax.ppermute(across, "gx", pair_across)

    later_inside, later_across, u0, forcing, running, state, memory, stiff = call(
        local_kernel,
        "local",
        [ANY] * 4 + [SCALAR] * 2 + [VEC],
        [
            held(*strip), held(*strip), held(*brick), held(*brick), held(*brick), held(*brick),
            held(3, *brick), held(*brick),
        ],
        [VEC] * 8,
        [vec(*brick), vec(4, *brick), vec(*brick), vec(*brick), dma((5,))],
        (
            wave_state, layer_fields, source, filtered, frequency, start_time, *in_vmem(coef),
        ),
        5,
    )
    last_inside = lax.ppermute(later_inside, "gx", pair_inside)
    last_across = lax.ppermute(later_across, "gx", pair_across)

    out_types = [
        jax.ShapeDtypeStruct(wave_state.shape, F32),
        jax.ShapeDtypeStruct(layer_fields.shape, F32),
        jax.ShapeDtypeStruct(filtered.shape, F32),
    ]
    (
        next_state, next_layer, next_filtered, edge_new, edge_memory, edge_running, ghost, partial,
    ) = call(
        joint_kernel,
        "joint",
        [SCALAR] * 3 + [VEC] * 9,
        out_types
        + [
            held(2, *strip), held(2, *strip), held(2, *strip), held(2 * REACH, ny, nz),
            held(BLK, nz),
        ],
        [ANY] * 3 + [VEC] * 5,
        [
            vec(nx + 2 * REACH, ny, nz),
            vec(2 * REACH, ny, nz),
            vec(2, *strip),
            vec(*brick),
            vec(4, *brick),
            vec(*brick),
            vec(2, 5, ny, nz),
            vec(*brick),
            vec(*brick),
            vec(2 * REACH, ny, nz),
            vec(2 * REACH, ny, nz),
            dma((5,)),
        ],
        (
            frequency, start_time, speed_table,
            *in_vmem(
                coef, got_inside, got_across, u0, forcing, running, state, memory, stiff
            ),
        ),
        5,
    )
    next_state, next_layer, next_filtered, total = call(
        finish_kernel,
        "finish",
        [SCALAR] * 2 + [VEC] * 8 + [ANY] * 3,
        out_types + [held(BLK, nz)],
        [ANY] * 3 + [VEC],
        [vec(2, *strip), vec(2, *strip), vec(2, *strip), dma((6,))],
        (
            frequency, start_time,
            *in_vmem(
                coef, last_inside, last_across, edge_new, edge_memory, edge_running, ghost, partial
            ),
            next_state, next_layer, next_filtered,
        ),
        1,
        {10: 0, 11: 1, 12: 2},
    )
    total = jnp.sum(total_over(total, "gx"))
    filter_norm = jnp.sqrt(total / (filtered.size * count) + 1e-06)
    return next_state, next_layer, next_filtered, filter_norm.reshape(1)


def solution(mesh):
    placed = (
        P("grp", "gx", None, None),
        P("grp", "gx", None, None),
        P(("grp", "gx"), None, None),
        P(("grp", "gx"), None, None),
        P("grp"),
        P("grp"),
        P(),
        P("gx", None, None),
        P("gx", None, None),
    )
    return jax.shard_map(
        body,
        mesh=mesh,
        in_specs=placed,
        out_specs=(
            P("grp", "gx", None, None),
            P("grp", "gx", None, None),
            P(("grp", "gx"), None, None),
            P("grp"),
        ),
        check_vma=False,
    )
```

```python
import functools
import math

import jax
import jax.numpy as jnp
from jax import lax
from jax.experimental import pallas as pl
from jax.experimental.pallas import tpu as pltpu
from jax.sharding import PartitionSpec as P

F32 = jnp.float32
BF16 = jnp.bfloat16
STEPS = 3
BLK = 8
REACH = 4
TIME_STEP = 0.25
DAMP_PEAK = 1.5
STENCIL = (-205.0 / 72.0, 8.0 / 5.0, -1.0 / 5.0, 8.0 / 315.0, -1.0 / 560.0)
SCALE = 5040.0
WHOLE = (-14336.0, 8064.0, -1008.0, 128.0, -9.0)
CENTRE_REST = 14.0 / SCALE
TAG_ROWS = 16
KAPPA, KAPPA_R, Q0, Q1, Q2, B0, B1, B2, DECAY, PAIR, AMP, BACK, STIFF, FORCE = range(14)
N_COEF = 14
VMEM_LIMIT = 30 * 1024 * 1024


def band(rows, cols, row_period, col_period):
    row = lax.broadcasted_iota(jnp.int32, (rows, cols), 0) % row_period
    col = lax.broadcasted_iota(jnp.int32, (rows, cols), 1) % col_period
    apart = jnp.abs(row - col)
    out = jnp.zeros((rows, cols), F32)
    for offset, value in enumerate(WHOLE):
        out = jnp.where(apart == offset, value, out)
    return out.astype(BF16)


def pieces(cells):
    high = cells.astype(BF16)
    return high, (cells - high.astype(F32)).astype(BF16)


def cross_diffs(planes, read, write_y, write_z, ny, nz):
    mat_y = band(ny, 2 * ny, ny, ny)
    mat_z = band(2 * nz, nz, nz, nz)
    for one, two in zip(planes[0::2], planes[1::2]):
        high_one, low_one = pieces(read(one))
        high_two, low_two = pieces(read(two))
        upper = jnp.concatenate([high_one, high_two], axis=1)
        lower = jnp.concatenate([low_one, low_two], axis=1)
        diff_y = jnp.dot(
            mat_y, jnp.concatenate([upper, lower], axis=0), preferred_element_type=F32
        )
        write_y(one, diff_y[:, :nz])
        write_y(two, diff_y[:, nz:])
        left = jnp.concatenate([high_one, low_one], axis=1)
        right = jnp.concatenate([high_two, low_two], axis=1)
        diff_z = jnp.dot(
            jnp.concatenate([left, right], axis=0), mat_z, preferred_element_type=F32
        )
        write_z(one, diff_z[:ny])
        write_z(two, diff_z[ny:])


def first_diff(cells, at):
    total = STENCIL[0] * cells[at]
    for offset in range(1, REACH + 1):
        above, below = cells.get(at + offset), cells.get(at - offset)
        if above is not None and below is not None:
            total = total + STENCIL[offset] * (above + below)
        elif above is not None:
            total = total + STENCIL[offset] * above
        elif below is not None:
            total = total + STENCIL[offset] * below
    return total


def outer_part(cells, at, positions):
    total = None
    for position in positions:
        offset = abs(position - at)
        if offset <= REACH:
            term = STENCIL[offset] * cells[position]
            total = term if total is None else total + term
    return total


def advance(cells, previous, memory, stiff, forcing, diffs, co, phase):
    rest = CENTRE_REST * cells
    diffs = [diffs[0], diffs[1] * (1.0 / SCALE) - rest, diffs[2] * (1.0 / SCALE) - rest]
    memory = [m + co(Q0 + d) * (diffs[d] - m) for d, m in enumerate(memory)]
    inner = sum(diffs[d] - co(B0 + d) * memory[d] for d in range(3))
    stiff = co(DECAY) * stiff + co(PAIR) * cells
    new = (
        co(AMP) * cells
        - co(BACK) * previous
        + co(KAPPA) * inner
        - co(STIFF) * stiff
        - (co(FORCE) * phase) * forcing
    )
    return new, memory, stiff


def coefficients(speed_square, bits):
    rates = [DAMP_PEAK * bit for bit in bits]
    damping = rates[0] + rates[1] + rates[2]
    pairing = rates[0] * rates[1] + rates[1] * rates[2] + rates[2] * rates[0]
    retention = [jnp.exp(-TIME_STEP * rate) for rate in rates]
    half = 0.5 * TIME_STEP * damping
    inverse = 1.0 / (1.0 + half)
    square = TIME_STEP * TIME_STEP
    kappa = square * speed_square * inverse
    return (
        kappa,
        kappa * retention[0],
        1.0 - retention[0],
        1.0 - retention[1],
        1.0 - retention[2],
        bits[0],
        bits[1],
        bits[2],
        jnp.exp(-TIME_STEP * damping),
        TIME_STEP * pairing,
        (2.0 - square * pairing) * inverse,
        (1.0 - half) * inverse,
        square * damping * inverse,
        square * inverse,
    )


def along_last(tiles, nz):
    row = lax.broadcasted_iota(jnp.int32, (nz, nz), 0)
    col = lax.broadcasted_iota(jnp.int32, (nz, nz), 1) // BLK
    along = (row == col).astype(F32).astype(BF16)
    return jnp.dot(tiles.astype(BF16), along, preferred_element_type=F32)


def squares(index, table):
    speed = jnp.zeros_like(index)
    for entry in range(table.shape[0]):
        speed = jnp.where(index == float(entry), table[entry], speed)
    return speed * speed


def bits_of(mask):
    mask = mask.astype(jnp.int32)
    return [((mask >> direction) & 1).astype(F32) for direction in range(3)]


def down_second(ref, lead, value, ny):
    for block in range(ny // BLK):
        rows = jnp.broadcast_to(value[block : block + 1], (BLK, value.shape[1]))
        ref[(*lead, pl.ds(block * BLK, BLK))] = rows


def fill_clock(clock, freq, start):
    steps = lax.broadcasted_iota(jnp.int32, clock.shape[1:], 0).astype(F32)
    cosine = jnp.cos(freq[0] * (start[0] + steps * TIME_STEP))
    weight = (TIME_STEP * freq[0] / math.pi) * (cosine - 0.25)
    for count in range(STEPS):
        clock[count] = jnp.broadcast_to(cosine[count : count + 1], cosine.shape)
        clock[STEPS + count] = jnp.broadcast_to(weight[count + 1 : count + 2], weight.shape)


def over_rows(ny, step):
    def one(block, carry):
        step(pl.multiple_of(block * BLK, BLK))
        return carry

    lax.fori_loop(0, ny // BLK, one, 0)


def is_even():
    return lax.axis_index("gx") % 2 == 0


def edge_planes(nx):
    return [*range(REACH), *range(nx - REACH, nx)]


def send_kernel(
    wave, layer, source, freq, start, table_in, index_in, mask_in,
    inside, across, coef, clock, edge,
    u0, strips, diff_y, diff_z, tags, index, mask, table, sems,
):
    nx, ny, nz = u0.shape
    n_block = nx // BLK
    edges = (0, nx - REACH)
    copies = [pltpu.make_async_copy(wave.at[0], u0, sems.at[0])]
    small = [
        pltpu.make_async_copy(one, to, sems.at[7 + number])
        for number, (one, to) in enumerate(
            ((index_in, index), (mask_in, mask), (table_in, table))
        )
    ]
    for side in range(2):
        at = pl.ds(edges[side], REACH)
        copies += [
            pltpu.make_async_copy(wave.at[1, at], strips.at[side, 0], sems.at[1 + 3 * side]),
            pltpu.make_async_copy(
                layer.at[:, at], strips.at[side, pl.ds(1, 4)], sems.at[2 + 3 * side]
            ),
            pltpu.make_async_copy(source.at[at], strips.at[side, 5], sems.at[3 + 3 * side]),
        ]
    for copy in small + copies:
        copy.start()
    even = is_even()
    tags[...] = jnp.zeros_like(tags)
    fill_clock(clock, freq, start)
    phase = clock[0]
    for copy in small:
        copy.wait()
    rows = n_block * TAG_ROWS
    for block in range(n_block):
        at = pl.ds(block * TAG_ROWS, index.shape[0])
        tags[0, at, : index.shape[2]] = index[:, block].astype(F32)
        tags[1, at, : mask.shape[2]] = mask[:, block].astype(F32)
    wide = along_last(tags[...].reshape(2 * rows, nz), nz)
    square = squares(wide[:rows], table)
    masks = wide[rows:]
    values = coefficients(square, bits_of(masks))
    for entry, value in enumerate(values):
        for block in range(n_block):
            down_second(coef, (entry, block), value[block * TAG_ROWS : (block + 1) * TAG_ROWS], ny)
    for part, value in enumerate((square, masks)):
        to = pl.ds(2 * REACH * ny + part * TAG_ROWS, TAG_ROWS)
        left, right = value[:TAG_ROWS], value[rows - TAG_ROWS :]
        inside[to] = jnp.where(even, right, left)
        across[to] = jnp.where(even, left, right)
    copies[0].wait()
    planes = edge_planes(nx)
    slot = {plane: number for number, plane in enumerate(planes)}

    def put_y(plane, value):
        diff_y[slot[plane]] = value

    def put_z(plane, value):
        diff_z[slot[plane]] = value

    cross_diffs(planes, lambda plane: u0[plane], put_y, put_z, ny, nz)
    for copy in copies[1:]:
        copy.wait()

    def step(rows):
        at = pl.ds(rows, BLK)
        sides = []
        for side in range(2):
            block = side * (n_block - 1)
            reach = range(2 * REACH) if side == 0 else range(nx - 2 * REACH, nx)
            cells = {plane: u0[plane, at] for plane in reach}
            values = []
            for number in range(REACH):
                plane = edges[side] + number
                new, memory, stiff = advance(
                    cells[plane],
                    strips[side, 0, number, at],
                    [strips[side, 1 + d, number, at] for d in range(3)],
                    strips[side, 4, number, at],
                    strips[side, 5, number, at],
                    [
                        first_diff(cells, plane),
                        diff_y[slot[plane], at],
                        diff_z[slot[plane], at],
                    ],
                    lambda entry, block=block: coef[entry, block, at],
                    phase,
                )
                for entry, value in enumerate((new, *memory, stiff)):
                    edge[side, entry, number, at] = value
                values.append((cells[plane], new))
            sides.append(values)
        for number in range(REACH):
            for part in range(2):
                to = pl.ds(pl.multiple_of((part * REACH + number) * ny + rows, BLK), BLK)
                left, right = sides[0][number][part], sides[1][number][part]
                inside[to] = jnp.where(even, right, left)
                across[to] = jnp.where(even, left, right)

    over_rows(ny, step)


def local_kernel(
    wave, layer, source, running, coef, clock, edge,
    inside, across, first_out, second_out, run_out,
    fields, diff_y, diff_z,
):
    _, nx, ny, nz = wave.shape
    even = is_even()

    def put_y(plane, value):
        diff_y[plane] = value

    def put_z(plane, value):
        diff_z[plane] = value

    middle = range(REACH, nx - REACH)
    cross_diffs(middle, lambda plane: wave[0, plane], put_y, put_z, ny, nz)

    def read(entry, plane, at=slice(None)):
        if plane < REACH:
            return edge[0, entry, plane, at]
        if plane >= nx - REACH:
            return edge[1, entry, plane - nx + REACH, at]
        if entry == 0:
            return first_out[plane - REACH, at]
        return fields[entry - 1, plane - REACH, at]

    def first(rows):
        at = pl.ds(rows, BLK)
        cells = {plane: wave[0, plane, at] for plane in range(nx)}
        for plane in middle:
            new, memory, stiff = advance(
                cells[plane],
                wave[1, plane, at],
                [layer[d, plane, at] for d in range(3)],
                layer[3, plane, at],
                source[plane, at],
                [first_diff(cells, plane), diff_y[plane, at], diff_z[plane, at]],
                lambda entry, block=plane // BLK: coef[entry, block, at],
                clock[0],
            )
            first_out[plane - REACH, at] = new
            for entry, value in enumerate((*memory, stiff)):
                fields[entry, plane - REACH, at] = value

    over_rows(ny, first)
    cross_diffs(range(nx), lambda plane: read(0, plane), put_y, put_z, ny, nz)

    def second(rows):
        at = pl.ds(rows, BLK)
        cells = {plane: read(0, plane, at) for plane in range(nx)}
        values = {}
        for plane in range(nx):
            new, memory, stiff = advance(
                cells[plane],
                wave[0, plane, at],
                [read(1 + d, plane, at) for d in range(3)],
                read(4, plane, at),
                source[plane, at],
                [first_diff(cells, plane), diff_y[plane, at], diff_z[plane, at]],
                lambda entry, block=plane // BLK: coef[entry, block, at],
                clock[1],
            )
            values[plane] = new
            for entry, value in enumerate((new, *memory, stiff)):
                second_out[entry, plane, at] = value
            run_out[plane, at] = (
                running[plane, at] + clock[STEPS] * cells[plane] + clock[STEPS + 1] * new
            )
        for number in range(REACH):
            left, right = values[number], values[nx - REACH + number]
            inside[number, at] = jnp.where(even, right, left)
            across[number, at] = jnp.where(even, left, right)

    over_rows(ny, second)


def joint_kernel(
    coef, clock, inside, across, wave, forcing, edge, first_in, second_in, run_in,
    out_state, out_layer, out_filtered, ghost, partial,
    ext, bump, push, ghost_coef, diff_y, diff_z, bump_y, bump_z,
):
    _, nx, ny, nz = wave.shape
    count = lax.axis_size("gx")
    place = lax.axis_index("gx")
    even = is_even()
    n_block = nx // BLK
    present = (
        jnp.where(place > 0, 1.0, 0.0).astype(F32),
        jnp.where(place < count - 1, 1.0, 0.0).astype(F32),
    )
    weights = [clock[STEPS + number] for number in range(STEPS)]
    ghosts = (range(-REACH, 0), range(nx, nx + REACH))
    owned = (range(REACH), range(nx - REACH, nx))
    nearby = (range(REACH, 2 * REACH), range(nx - 2 * REACH, nx - REACH))

    def slot(position):
        return position + REACH if position < nx // 2 else position - nx + 3 * REACH

    def received(to):
        one, two = inside[to], across[to]
        return jnp.where(even, two, one), jnp.where(even, one, two)

    tag_at = 2 * REACH * ny
    tiles = [received(pl.ds(tag_at + part * TAG_ROWS, TAG_ROWS)) for part in range(2)]
    for side in range(2):
        values = coefficients(tiles[0][side] * present[side], bits_of(tiles[1][side]))
        for entry, value in enumerate(
            (
                values[KAPPA_R],
                values[Q0],
                values[KAPPA] * (1.0 - values[Q1]),
                values[KAPPA] * (1.0 - values[Q2]),
                values[AMP] - values[STIFF] * values[PAIR],
            )
        ):
            down_second(ghost_coef, (side, entry), value, ny)

    def exchange(rows):
        at = pl.ds(rows, BLK)
        halo = {}
        sent = {}
        for number in range(REACH):
            to = pl.ds(pl.multiple_of(number * ny + rows, BLK), BLK)
            halo[-REACH + number], halo[nx + number] = received(to)
            to = pl.ds(pl.multiple_of((REACH + number) * ny + rows, BLK), BLK)
            sent[-REACH + number], sent[nx + number] = received(to)
        for side in range(2):
            mine = {plane: wave[0, plane, at] for plane in owned[side]}
            kappa_r = coef[KAPPA_R, side * (n_block - 1), at]
            for number, plane in enumerate(owned[side]):
                outer = outer_part(halo, plane, ghosts[side])
                added = kappa_r * outer
                push[slot(plane), at] = outer
                bump[slot(plane), at] = added
                ext[slot(plane), at] = edge[side, 0, number, at] + added
            kappa_r = ghost_coef[side, 0, at]
            for position in ghosts[side]:
                outer = outer_part(mine, position, owned[side])
                added = kappa_r * outer
                push[slot(position), at] = outer
                bump[slot(position), at] = added
                ext[slot(position), at] = sent[position] + added

    over_rows(ny, exchange)

    def put_bump_y(plane, value):
        bump_y[plane] = value

    def put_bump_z(plane, value):
        bump_z[plane] = value

    cross_diffs(range(4 * REACH), lambda plane: bump[plane], put_bump_y, put_bump_z, ny, nz)

    def respond(added, first, position, others, outer, q0, kappas, at):
        kappa_r, kappa_1, kappa_2, grown = kappas
        value = added[position]
        rest = CENTRE_REST * value
        along = first_diff(added, position) + outer_part(first, position, others)
        side_y = bump_y[slot(position), at] * (1.0 / SCALE) - rest
        side_z = bump_z[slot(position), at] * (1.0 / SCALE) - rest
        gain = (
            grown * value + kappa_r * (along - q0 * outer) + kappa_1 * side_y + kappa_2 * side_z
        )
        return gain, along, side_y, side_z

    def second(rows):
        at = pl.ds(rows, BLK)
        for side in range(2):
            block = side * (n_block - 1)
            first = {
                position: ext[slot(position), at] for position in (*ghosts[side], *owned[side])
            }
            added = {position: bump[slot(position), at] for position in ghosts[side]}
            kappa_r, q0, kappa_1, kappa_2, grown = [
                ghost_coef[side, entry, at] for entry in range(5)
            ]
            for number, position in enumerate(ghosts[side]):
                outer = push[slot(position), at]
                ghost[side * REACH + number, at], _, _, _ = respond(
                    added, first, position, owned[side], outer, q0,
                    (kappa_r, kappa_1, kappa_2, grown), at,
                )
            added = {position: bump[slot(position), at] for position in owned[side]}
            kappa_r, kappa = coef[KAPPA_R, block, at], coef[KAPPA, block, at]
            q0, q1, q2 = [coef[entry, block, at] for entry in (Q0, Q1, Q2)]
            pair = coef[PAIR, block, at]
            kappas = (
                kappa_r,
                kappa * (1.0 - q1),
                kappa * (1.0 - q2),
                coef[AMP, block, at] - coef[STIFF, block, at] * pair,
            )
            for plane in owned[side]:
                outer = push[slot(plane), at]
                gain, along, side_y, side_z = respond(
                    added, first, plane, ghosts[side], outer, q0, kappas, at
                )
                out_state[1, plane, at] = second_in[0, plane, at] + gain
                out_layer[0, plane, at] = second_in[1, plane, at] + q0 * (
                    along + (1.0 - q0) * outer
                )
                out_layer[1, plane, at] = second_in[2, plane, at] + q1 * side_y
                out_layer[2, plane, at] = second_in[3, plane, at] + q2 * side_z
                out_layer[3, plane, at] = second_in[4, plane, at] + pair * added[plane]
                out_filtered[plane, at] = (
                    run_in[plane, at] + weights[0] * added[plane] + weights[1] * gain
                )
            for plane in nearby[side]:
                along = outer_part(added, plane, owned[side])
                gain = kappa_r * along
                out_state[1, plane, at] = second_in[0, plane, at] + gain
                out_layer[0, plane, at] = second_in[1, plane, at] + q0 * along
                out_filtered[plane, at] = run_in[plane, at] + weights[1] * gain
        for plane in range(2 * REACH, nx - 2 * REACH):
            out_state[1, plane, at] = second_in[0, plane, at]
            out_layer[0, plane, at] = second_in[1, plane, at]
            out_filtered[plane, at] = run_in[plane, at]

    over_rows(ny, second)

    def put_y(plane, value):
        diff_y[plane] = value

    def put_z(plane, value):
        diff_z[plane] = value

    cross_diffs(range(nx), lambda plane: out_state[1, plane], put_y, put_z, ny, nz)
    partial[...] = jnp.zeros_like(partial)

    def third(rows):
        at = pl.ds(rows, BLK)
        cells = {plane: out_state[1, plane, at] for plane in range(nx)}
        total = partial[...]
        for plane in range(nx):
            at_edge = plane < REACH or plane >= nx - REACH
            if at_edge:
                previous = ext[slot(plane), at]
                fields = [out_layer[d, plane, at] for d in range(4)]
            else:
                previous = first_in[plane - REACH, at]
                fields = [out_layer[0, plane, at]]
                fields += [second_in[1 + d, plane, at] for d in range(1, 4)]
            value, memory, stiff = advance(
                cells[plane],
                previous,
                fields[:3],
                fields[3],
                forcing[plane, at],
                [first_diff(cells, plane), diff_y[plane, at], diff_z[plane, at]],
                lambda entry, block=plane // BLK: coef[entry, block, at],
                clock[2],
            )
            done = out_filtered[plane, at] + weights[2] * value
            for d in range(3):
                out_layer[d, plane, at] = memory[d]
            out_layer[3, plane, at] = stiff
            out_state[0, plane, at] = value
            out_filtered[plane, at] = done
            if not at_edge:
                total = total + done * done
        partial[...] = total

    over_rows(ny, third)


def finish_kernel(
    coef, clock, inside, across, ghost, partial, state_in, layer_in, filtered_in,
    out_state, out_layer, out_filtered, total_out,
):
    _, nx, ny, _ = state_in.shape
    n_block = nx // BLK
    even = is_even()
    weight = clock[2 * STEPS - 1]
    total_out[...] = partial[...]
    ghosts = (range(-REACH, 0), range(nx, nx + REACH))
    owned = (range(REACH), range(nx - REACH, nx))

    def step(rows):
        at = pl.ds(rows, BLK)
        halo = {}
        for number in range(REACH):
            one, two = inside[number, at], across[number, at]
            halo[-REACH + number] = jnp.where(even, two, one) + ghost[number, at]
            halo[nx + number] = jnp.where(even, one, two) + ghost[REACH + number, at]
        total = total_out[...]
        for side in range(2):
            block = side * (n_block - 1)
            kappa_r, q0 = coef[KAPPA_R, block, at], coef[Q0, block, at]
            for plane in owned[side]:
                outer = outer_part(halo, plane, ghosts[side])
                added = kappa_r * outer
                out_state[0, plane, at] = state_in[0, plane, at] + added
                out_layer[0, plane, at] = layer_in[0, plane, at] + q0 * outer
                done = filtered_in[plane, at] + weight * added
                out_filtered[plane, at] = done
                total = total + done * done
        total_out[...] = total

    over_rows(ny, step)


def store_kernel(values, held_array, out, values_out, sem):
    copy = pltpu.make_async_copy(held_array, out, sem)
    copy.start()
    values_out[...] = values[...]
    copy.wait()


SCALAR = pl.BlockSpec(memory_space=pltpu.SMEM)
HBM = pl.BlockSpec(memory_space=pltpu.HBM)
VEC = pl.BlockSpec(memory_space=pltpu.VMEM)


def held(*shape):
    return pltpu.VMEM(shape, F32)


def in_vmem(*arrays):
    return [pltpu.with_memory_space_constraint(array, pltpu.VMEM) for array in arrays]


def in_hbm(*arrays):
    return [pltpu.with_memory_space_constraint(array, pltpu.HBM) for array in arrays]


def call(kernel, name, in_specs, out_shape, out_specs, scratch, operands, micros, aliases=None):
    return pl.pallas_call(
        kernel,
        name=name,
        in_specs=in_specs,
        out_shape=out_shape,
        out_specs=out_specs,
        scratch_shapes=scratch,
        input_output_aliases=aliases or {},
        compiler_params=pltpu.CompilerParams(vmem_limit_bytes=VMEM_LIMIT),
        cost_estimate=pl.CostEstimate(
            flops=0, bytes_accessed=int(micros * 3.6e6), transcendentals=0
        ),
    )(*operands)


def swap_pairs(count):
    inside = [(i, i ^ 1) for i in range(count)]
    across = []
    for i in range(1, count - 1, 2):
        across += [(i, i + 1), (i + 1, i)]
    return inside, across


def store(values, array):
    return call(
        store_kernel,
        "store",
        [VEC] * 2,
        [jax.ShapeDtypeStruct(array.shape, F32), held(*values.shape)],
        [HBM, VEC],
        [pltpu.SemaphoreType.DMA],
        in_vmem(values, array),
        1,
    )


def total_and_stores(values, arrays, axis):
    count = lax.axis_size(axis)
    stored = []
    if count & (count - 1):
        for array in arrays:
            stored.append(store(values, array)[0])
        return lax.psum(values, axis), stored
    hop = 1
    while hop < count:
        got = lax.ppermute(values, axis, [(i, i ^ hop) for i in range(count)])
        if len(stored) < len(arrays):
            done, values = store(values, arrays[len(stored)])
            stored.append(done)
        values = values + got
        hop *= 2
    for array in arrays[len(stored) :]:
        stored.append(store(values, array)[0])
    return values, stored


def body(
    wave_state, layer_fields, source, filtered, frequency, start_time, speed_table, speed_index,
    pml_mask,
):
    _, nx, ny, nz = wave_state.shape
    n_block = nx // BLK
    count = lax.axis_size("gx")
    pair_inside, pair_across = swap_pairs(count)
    brick = (nx, ny, nz)
    strip = (REACH, ny, nz)
    message = (2 * REACH * ny + 2 * TAG_ROWS, nz)
    dma = pltpu.SemaphoreType.DMA
    vec = lambda *shape: pltpu.VMEM(shape, F32)

    blocks = (speed_index.shape[1], n_block, speed_index.shape[2])
    index, mask = in_hbm(*(jnp.transpose(one, (1, 0, 2)) for one in (speed_index, pml_mask)))

    inside, across, coef, clock, edge = call(
        send_kernel,
        "strips",
        [HBM] * 3 + [SCALAR] * 2 + [HBM] * 3,
        [
            held(*message), held(*message), held(N_COEF, n_block, ny, nz),
            held(2 * STEPS, BLK, nz), held(2, 5, *strip),
        ],
        [VEC] * 5,
        [
            vec(*brick),
            vec(2, 6, *strip),
            vec(2 * REACH, ny, nz),
            vec(2 * REACH, ny, nz),
            vec(2, n_block * TAG_ROWS, nz),
            pltpu.VMEM(blocks, jnp.int32),
            pltpu.VMEM(blocks, jnp.int32),
            pltpu.SMEM(speed_table.shape, F32),
            dma((10,)),
        ],
        (
            *in_hbm(wave_state, layer_fields, source), frequency, start_time,
            *in_hbm(speed_table), index, mask,
        ),
        2.5,
    )
    got_inside = lax.ppermute(inside, "gx", pair_inside)
    got_across = lax.ppermute(across, "gx", pair_across)
    coef, clock, edge, wave, layer, forcing, running = in_vmem(
        coef, clock, edge, wave_state, layer_fields, source, filtered
    )

    later_inside, later_across, first, second, run = call(
        local_kernel,
        "local",
        [VEC] * 7,
        [
            held(*strip), held(*strip), held(nx - 2 * REACH, ny, nz), held(5, *brick),
            held(*brick),
        ],
        [VEC] * 5,
        [vec(4, nx - 2 * REACH, ny, nz), vec(*brick), vec(*brick)],
        (wave, layer, forcing, running, coef, clock, edge),
        4,
    )
    last_inside = lax.ppermute(later_inside, "gx", pair_inside)
    last_across = lax.ppermute(later_across, "gx", pair_across)

    out_types = [
        held(*wave_state.shape), held(*layer_fields.shape), held(*filtered.shape)
    ]
    next_state, next_layer, next_filtered, ghost, partial = call(
        joint_kernel,
        "joint",
        [VEC] * 10,
        out_types + [held(2 * REACH, ny, nz), held(BLK, nz)],
        [VEC] * 5,
        [
            vec(4 * REACH, ny, nz),
            vec(4 * REACH, ny, nz),
            vec(4 * REACH, ny, nz),
            vec(2, 5, ny, nz),
            vec(*brick),
            vec(*brick),
            vec(4 * REACH, ny, nz),
            vec(4 * REACH, ny, nz),
        ],
        (
            coef, clock, *in_vmem(got_inside, got_across), wave, forcing, edge,
            *in_vmem(first, second, run),
        ),
        5,
    )
    next_state, next_layer, next_filtered, total = call(
        finish_kernel,
        "finish",
        [VEC] * 9,
        out_types + [held(BLK, nz)],
        [VEC] * 4,
        [],
        (
            coef, clock,
            *in_vmem(
                last_inside, last_across, ghost, partial, next_state, next_layer, next_filtered
            ),
        ),
        1,
        {6: 0, 7: 1, 8: 2},
    )
    total, (next_filtered, next_state, next_layer) = total_and_stores(
        total, [next_filtered, next_state, next_layer], "gx"
    )
    total = jnp.sum(total)
    filter_norm = jnp.sqrt(total / (filtered.size * count) + 1e-06)
    return next_state, next_layer, next_filtered, filter_norm.reshape(1)


def solution(mesh):
    placed = (
        P("grp", "gx", None, None),
        P("grp", "gx", None, None),
        P(("grp", "gx"), None, None),
        P(("grp", "gx"), None, None),
        P("grp"),
        P("grp"),
        P(),
        P("gx", None, None),
        P("gx", None, None),
    )
    return jax.shard_map(
        body,
        mesh=mesh,
        in_specs=placed,
        out_specs=(
            P("grp", "gx", None, None),
            P("grp", "gx", None, None),
            P(("grp", "gx"), None, None),
            P("grp"),
        ),
        check_vma=False,
    )
```

```python
import functools
import math

import jax
import jax.numpy as jnp
from jax import lax
from jax.experimental import pallas as pl
from jax.experimental.pallas import tpu as pltpu
from jax.sharding import PartitionSpec as P

F32 = jnp.float32
BF16 = jnp.bfloat16
STEPS = 3
BLK = 8
REACH = 4
TIME_STEP = 0.25
DAMP_PEAK = 1.5
STENCIL = (-205.0 / 72.0, 8.0 / 5.0, -1.0 / 5.0, 8.0 / 315.0, -1.0 / 560.0)
SCALE = 5040.0
WHOLE = (-14336.0, 8064.0, -1008.0, 128.0, -9.0)
CENTRE_REST = 14.0 / SCALE
TAG_ROWS = 16
KAPPA, KAPPA_R, Q0, Q1, Q2, B0, B1, B2, DECAY, PAIR, AMP, BACK, STIFF, FORCE = range(14)
N_COEF = 14
VMEM_LIMIT = 30 * 1024 * 1024


def band(rows, cols, row_period, col_period):
    row = lax.broadcasted_iota(jnp.int32, (rows, cols), 0) % row_period
    col = lax.broadcasted_iota(jnp.int32, (rows, cols), 1) % col_period
    apart = jnp.abs(row - col)
    out = jnp.zeros((rows, cols), F32)
    for offset, value in enumerate(WHOLE):
        out = jnp.where(apart == offset, value, out)
    return out.astype(BF16)


def pieces(cells):
    high = cells.astype(BF16)
    return high, (cells - high.astype(F32)).astype(BF16)


def cross_diffs(planes, read, write_y, write_z, ny, nz):
    mat_y = band(ny, 2 * ny, ny, ny)
    mat_z = band(2 * nz, nz, nz, nz)
    for one, two in zip(planes[0::2], planes[1::2]):
        high_one, low_one = pieces(read(one))
        high_two, low_two = pieces(read(two))
        upper = jnp.concatenate([high_one, high_two], axis=1)
        lower = jnp.concatenate([low_one, low_two], axis=1)
        diff_y = jnp.dot(
            mat_y, jnp.concatenate([upper, lower], axis=0), preferred_element_type=F32
        )
        write_y(one, diff_y[:, :nz])
        write_y(two, diff_y[:, nz:])
        left = jnp.concatenate([high_one, low_one], axis=1)
        right = jnp.concatenate([high_two, low_two], axis=1)
        diff_z = jnp.dot(
            jnp.concatenate([left, right], axis=0), mat_z, preferred_element_type=F32
        )
        write_z(one, diff_z[:ny])
        write_z(two, diff_z[ny:])


def first_diff(cells, at):
    total = STENCIL[0] * cells[at]
    for offset in range(1, REACH + 1):
        above, below = cells.get(at + offset), cells.get(at - offset)
        if above is not None and below is not None:
            total = total + STENCIL[offset] * (above + below)
        elif above is not None:
            total = total + STENCIL[offset] * above
        elif below is not None:
            total = total + STENCIL[offset] * below
    return total


def outer_part(cells, at, positions):
    total = None
    for position in positions:
        offset = abs(position - at)
        if offset <= REACH:
            term = STENCIL[offset] * cells[position]
            total = term if total is None else total + term
    return total


def advance(cells, previous, memory, stiff, forcing, diffs, co, phase):
    rest = CENTRE_REST * cells
    diffs = [diffs[0], diffs[1] * (1.0 / SCALE) - rest, diffs[2] * (1.0 / SCALE) - rest]
    memory = [m + co(Q0 + d) * (diffs[d] - m) for d, m in enumerate(memory)]
    inner = sum(diffs[d] - co(B0 + d) * memory[d] for d in range(3))
    stiff = co(DECAY) * stiff + co(PAIR) * cells
    new = (
        co(AMP) * cells
        - co(BACK) * previous
        + co(KAPPA) * inner
        - co(STIFF) * stiff
        - (co(FORCE) * phase) * forcing
    )
    return new, memory, stiff


def coefficients(speed_square, bits):
    rates = [DAMP_PEAK * bit for bit in bits]
    damping = rates[0] + rates[1] + rates[2]
    pairing = rates[0] * rates[1] + rates[1] * rates[2] + rates[2] * rates[0]
    retention = [jnp.exp(-TIME_STEP * rate) for rate in rates]
    half = 0.5 * TIME_STEP * damping
    inverse = 1.0 / (1.0 + half)
    square = TIME_STEP * TIME_STEP
    kappa = square * speed_square * inverse
    return (
        kappa,
        kappa * retention[0],
        1.0 - retention[0],
        1.0 - retention[1],
        1.0 - retention[2],
        bits[0],
        bits[1],
        bits[2],
        jnp.exp(-TIME_STEP * damping),
        TIME_STEP * pairing,
        (2.0 - square * pairing) * inverse,
        (1.0 - half) * inverse,
        square * damping * inverse,
        square * inverse,
    )


def along_last(tiles, nz):
    row = lax.broadcasted_iota(jnp.int32, (nz, nz), 0)
    col = lax.broadcasted_iota(jnp.int32, (nz, nz), 1) // BLK
    along = (row == col).astype(F32).astype(BF16)
    return jnp.dot(tiles.astype(BF16), along, preferred_element_type=F32)


def squares(index, table):
    speed = jnp.zeros_like(index)
    for entry in range(table.shape[0]):
        speed = jnp.where(index == float(entry), table[entry], speed)
    return speed * speed


def bits_of(mask):
    mask = mask.astype(jnp.int32)
    return [((mask >> direction) & 1).astype(F32) for direction in range(3)]


def down_second(ref, lead, value, ny):
    for block in range(ny // BLK):
        rows = jnp.broadcast_to(value[block : block + 1], (BLK, value.shape[1]))
        ref[(*lead, pl.ds(block * BLK, BLK))] = rows


def fill_clock(clock, freq, start):
    steps = lax.broadcasted_iota(jnp.int32, clock.shape[1:], 0).astype(F32)
    cosine = jnp.cos(freq[0] * (start[0] + steps * TIME_STEP))
    weight = (TIME_STEP * freq[0] / math.pi) * (cosine - 0.25)
    for count in range(STEPS):
        clock[count] = jnp.broadcast_to(cosine[count : count + 1], cosine.shape)
        clock[STEPS + count] = jnp.broadcast_to(weight[count + 1 : count + 2], weight.shape)


def over_rows(ny, step):
    def one(block, carry):
        step(pl.multiple_of(block * BLK, BLK))
        return carry

    lax.fori_loop(0, ny // BLK, one, 0)


def is_even():
    return lax.axis_index("gx") % 2 == 0


def edge_planes(nx):
    return [*range(REACH), *range(nx - REACH, nx)]


def send_kernel(
    wave_in, layer_in, source_in, freq, start, table_in, index_in, mask_in,
    inside, across, coef, clock, edge, wave, layer, source,
    diff_y, diff_z, tags, index, mask, table, sems,
):
    _, nx, ny, nz = wave.shape
    n_block = nx // BLK
    edges = (0, nx - REACH)
    pieces_of = [(wave_in.at[0], wave.at[0])]
    for first, length in ((0, REACH), (nx - REACH, REACH), (REACH, nx - 2 * REACH)):
        at = pl.ds(first, length)
        pieces_of += [
            (wave_in.at[1, at], wave.at[1, at]),
            (layer_in.at[:, at], layer.at[:, at]),
            (source_in.at[at], source.at[at]),
        ]
    copies = [
        pltpu.make_async_copy(one, to, sems.at[number])
        for number, (one, to) in enumerate(pieces_of)
    ]
    small = [
        pltpu.make_async_copy(one, to, sems.at[len(copies) + number])
        for number, (one, to) in enumerate(
            ((index_in, index), (mask_in, mask), (table_in, table))
        )
    ]
    for copy in small + copies:
        copy.start()
    even = is_even()
    tags[...] = jnp.zeros_like(tags)
    fill_clock(clock, freq, start)
    phase = clock[0]
    for copy in small:
        copy.wait()
    rows = n_block * TAG_ROWS
    for block in range(n_block):
        at = pl.ds(block * TAG_ROWS, index.shape[0])
        tags[0, at, : index.shape[2]] = index[:, block].astype(F32)
        tags[1, at, : mask.shape[2]] = mask[:, block].astype(F32)
    wide = along_last(tags[...].reshape(2 * rows, nz), nz)
    square = squares(wide[:rows], table)
    masks = wide[rows:]
    values = coefficients(square, bits_of(masks))
    for entry, value in enumerate(values):
        for block in range(n_block):
            down_second(coef, (entry, block), value[block * TAG_ROWS : (block + 1) * TAG_ROWS], ny)
    for part, value in enumerate((square, masks)):
        to = pl.ds(2 * REACH * ny + part * TAG_ROWS, TAG_ROWS)
        left, right = value[:TAG_ROWS], value[rows - TAG_ROWS :]
        inside[to] = jnp.where(even, right, left)
        across[to] = jnp.where(even, left, right)
    copies[0].wait()
    planes = edge_planes(nx)
    slot = {plane: number for number, plane in enumerate(planes)}

    def put_y(plane, value):
        diff_y[slot[plane]] = value

    def put_z(plane, value):
        diff_z[slot[plane]] = value

    cross_diffs(planes, lambda plane: wave[0, plane], put_y, put_z, ny, nz)
    for copy in copies[1:7]:
        copy.wait()

    def step(rows):
        at = pl.ds(rows, BLK)
        sides = []
        for side in range(2):
            block = side * (n_block - 1)
            reach = range(2 * REACH) if side == 0 else range(nx - 2 * REACH, nx)
            cells = {plane: wave[0, plane, at] for plane in reach}
            values = []
            for number in range(REACH):
                plane = edges[side] + number
                new, memory, stiff = advance(
                    cells[plane],
                    wave[1, plane, at],
                    [layer[d, plane, at] for d in range(3)],
                    layer[3, plane, at],
                    source[plane, at],
                    [
                        first_diff(cells, plane),
                        diff_y[slot[plane], at],
                        diff_z[slot[plane], at],
                    ],
                    lambda entry, block=block: coef[entry, block, at],
                    phase,
                )
                for entry, value in enumerate((new, *memory, stiff)):
                    edge[side, entry, number, at] = value
                values.append((cells[plane], new))
            sides.append(values)
        for number in range(REACH):
            for part in range(2):
                to = pl.ds(pl.multiple_of((part * REACH + number) * ny + rows, BLK), BLK)
                left, right = sides[0][number][part], sides[1][number][part]
                inside[to] = jnp.where(even, right, left)
                across[to] = jnp.where(even, left, right)

    over_rows(ny, step)
    for copy in copies[7:]:
        copy.wait()


def local_kernel(
    wave, layer, source, coef, clock, edge,
    inside, across, first_out, second_out, run_out,
    fields, diff_y, diff_z,
):
    _, nx, ny, nz = wave.shape
    even = is_even()

    def put_y(plane, value):
        diff_y[plane] = value

    def put_z(plane, value):
        diff_z[plane] = value

    middle = range(REACH, nx - REACH)
    cross_diffs(middle, lambda plane: wave[0, plane], put_y, put_z, ny, nz)

    def read(entry, plane, at=slice(None)):
        if plane < REACH:
            return edge[0, entry, plane, at]
        if plane >= nx - REACH:
            return edge[1, entry, plane - nx + REACH, at]
        if entry == 0:
            return first_out[plane - REACH, at]
        return fields[entry - 1, plane - REACH, at]

    def first(rows):
        at = pl.ds(rows, BLK)
        cells = {plane: wave[0, plane, at] for plane in range(nx)}
        for plane in middle:
            new, memory, stiff = advance(
                cells[plane],
                wave[1, plane, at],
                [layer[d, plane, at] for d in range(3)],
                layer[3, plane, at],
                source[plane, at],
                [first_diff(cells, plane), diff_y[plane, at], diff_z[plane, at]],
                lambda entry, block=plane // BLK: coef[entry, block, at],
                clock[0],
            )
            first_out[plane - REACH, at] = new
            for entry, value in enumerate((*memory, stiff)):
                fields[entry, plane - REACH, at] = value

    over_rows(ny, first)
    cross_diffs(range(nx), lambda plane: read(0, plane), put_y, put_z, ny, nz)

    def second(rows):
        at = pl.ds(rows, BLK)
        cells = {plane: read(0, plane, at) for plane in range(nx)}
        values = {}
        for plane in range(nx):
            new, memory, stiff = advance(
                cells[plane],
                wave[0, plane, at],
                [read(1 + d, plane, at) for d in range(3)],
                read(4, plane, at),
                source[plane, at],
                [first_diff(cells, plane), diff_y[plane, at], diff_z[plane, at]],
                lambda entry, block=plane // BLK: coef[entry, block, at],
                clock[1],
            )
            values[plane] = new
            for entry, value in enumerate((new, *memory, stiff)):
                second_out[entry, plane, at] = value
            run_out[plane, at] = clock[STEPS] * cells[plane] + clock[STEPS + 1] * new
        for number in range(REACH):
            left, right = values[number], values[nx - REACH + number]
            inside[number, at] = jnp.where(even, right, left)
            across[number, at] = jnp.where(even, left, right)

    over_rows(ny, second)


def joint_kernel(
    coef, clock, inside, across, wave, forcing, running, edge, first_in, second_in, run_in,
    out_state, out_layer, out_filtered, ghost, partial,
    ext, bump, push, ghost_coef, diff_y, diff_z, bump_y, bump_z,
):
    _, nx, ny, nz = wave.shape
    count = lax.axis_size("gx")
    place = lax.axis_index("gx")
    even = is_even()
    n_block = nx // BLK
    present = (
        jnp.where(place > 0, 1.0, 0.0).astype(F32),
        jnp.where(place < count - 1, 1.0, 0.0).astype(F32),
    )
    weights = [clock[STEPS + number] for number in range(STEPS)]
    ghosts = (range(-REACH, 0), range(nx, nx + REACH))
    owned = (range(REACH), range(nx - REACH, nx))
    nearby = (range(REACH, 2 * REACH), range(nx - 2 * REACH, nx - REACH))

    def slot(position):
        return position + REACH if position < nx // 2 else position - nx + 3 * REACH

    def received(to):
        one, two = inside[to], across[to]
        return jnp.where(even, two, one), jnp.where(even, one, two)

    tag_at = 2 * REACH * ny
    tiles = [received(pl.ds(tag_at + part * TAG_ROWS, TAG_ROWS)) for part in range(2)]
    for side in range(2):
        values = coefficients(tiles[0][side] * present[side], bits_of(tiles[1][side]))
        for entry, value in enumerate(
            (
                values[KAPPA_R],
                values[Q0],
                values[KAPPA] * (1.0 - values[Q1]),
                values[KAPPA] * (1.0 - values[Q2]),
                values[AMP] - values[STIFF] * values[PAIR],
            )
        ):
            down_second(ghost_coef, (side, entry), value, ny)

    def exchange(rows):
        at = pl.ds(rows, BLK)
        halo = {}
        sent = {}
        for number in range(REACH):
            to = pl.ds(pl.multiple_of(number * ny + rows, BLK), BLK)
            halo[-REACH + number], halo[nx + number] = received(to)
            to = pl.ds(pl.multiple_of((REACH + number) * ny + rows, BLK), BLK)
            sent[-REACH + number], sent[nx + number] = received(to)
        for side in range(2):
            mine = {plane: wave[0, plane, at] for plane in owned[side]}
            kappa_r = coef[KAPPA_R, side * (n_block - 1), at]
            for number, plane in enumerate(owned[side]):
                outer = outer_part(halo, plane, ghosts[side])
                added = kappa_r * outer
                push[slot(plane), at] = outer
                bump[slot(plane), at] = added
                ext[slot(plane), at] = edge[side, 0, number, at] + added
            kappa_r = ghost_coef[side, 0, at]
            for position in ghosts[side]:
                outer = outer_part(mine, position, owned[side])
                added = kappa_r * outer
                push[slot(position), at] = outer
                bump[slot(position), at] = added
                ext[slot(position), at] = sent[position] + added

    over_rows(ny, exchange)

    def put_bump_y(plane, value):
        bump_y[plane] = value

    def put_bump_z(plane, value):
        bump_z[plane] = value

    cross_diffs(range(4 * REACH), lambda plane: bump[plane], put_bump_y, put_bump_z, ny, nz)

    def respond(added, first, position, others, outer, q0, kappas, at):
        kappa_r, kappa_1, kappa_2, grown = kappas
        value = added[position]
        rest = CENTRE_REST * value
        along = first_diff(added, position) + outer_part(first, position, others)
        side_y = bump_y[slot(position), at] * (1.0 / SCALE) - rest
        side_z = bump_z[slot(position), at] * (1.0 / SCALE) - rest
        gain = (
            grown * value + kappa_r * (along - q0 * outer) + kappa_1 * side_y + kappa_2 * side_z
        )
        return gain, along, side_y, side_z

    def second(rows):
        at = pl.ds(rows, BLK)
        for side in range(2):
            block = side * (n_block - 1)
            first = {
                position: ext[slot(position), at] for position in (*ghosts[side], *owned[side])
            }
            added = {position: bump[slot(position), at] for position in ghosts[side]}
            kappa_r, q0, kappa_1, kappa_2, grown = [
                ghost_coef[side, entry, at] for entry in range(5)
            ]
            for number, position in enumerate(ghosts[side]):
                outer = push[slot(position), at]
                ghost[side * REACH + number, at], _, _, _ = respond(
                    added, first, position, owned[side], outer, q0,
                    (kappa_r, kappa_1, kappa_2, grown), at,
                )
            added = {position: bump[slot(position), at] for position in owned[side]}
            kappa_r, kappa = coef[KAPPA_R, block, at], coef[KAPPA, block, at]
            q0, q1, q2 = [coef[entry, block, at] for entry in (Q0, Q1, Q2)]
            pair = coef[PAIR, block, at]
            kappas = (
                kappa_r,
                kappa * (1.0 - q1),
                kappa * (1.0 - q2),
                coef[AMP, block, at] - coef[STIFF, block, at] * pair,
            )
            for plane in owned[side]:
                outer = push[slot(plane), at]
                gain, along, side_y, side_z = respond(
                    added, first, plane, ghosts[side], outer, q0, kappas, at
                )
                out_state[1, plane, at] = second_in[0, plane, at] + gain
                out_layer[0, plane, at] = second_in[1, plane, at] + q0 * (
                    along + (1.0 - q0) * outer
                )
                out_layer[1, plane, at] = second_in[2, plane, at] + q1 * side_y
                out_layer[2, plane, at] = second_in[3, plane, at] + q2 * side_z
                out_layer[3, plane, at] = second_in[4, plane, at] + pair * added[plane]
                out_filtered[plane, at] = (
                    running[plane, at]
                    + run_in[plane, at]
                    + weights[0] * added[plane]
                    + weights[1] * gain
                )
            for plane in nearby[side]:
                along = outer_part(added, plane, owned[side])
                gain = kappa_r * along
                out_state[1, plane, at] = second_in[0, plane, at] + gain
                out_layer[0, plane, at] = second_in[1, plane, at] + q0 * along
                out_filtered[plane, at] = running[plane, at] + run_in[plane, at] + weights[1] * gain
        for plane in range(2 * REACH, nx - 2 * REACH):
            out_state[1, plane, at] = second_in[0, plane, at]
            out_layer[0, plane, at] = second_in[1, plane, at]
            out_filtered[plane, at] = running[plane, at] + run_in[plane, at]

    over_rows(ny, second)

    def put_y(plane, value):
        diff_y[plane] = value

    def put_z(plane, value):
        diff_z[plane] = value

    cross_diffs(range(nx), lambda plane: out_state[1, plane], put_y, put_z, ny, nz)
    partial[...] = jnp.zeros_like(partial)

    def third(rows):
        at = pl.ds(rows, BLK)
        cells = {plane: out_state[1, plane, at] for plane in range(nx)}
        total = partial[...]
        for plane in range(nx):
            at_edge = plane < REACH or plane >= nx - REACH
            if at_edge:
                previous = ext[slot(plane), at]
                fields = [out_layer[d, plane, at] for d in range(4)]
            else:
                previous = first_in[plane - REACH, at]
                fields = [out_layer[0, plane, at]]
                fields += [second_in[1 + d, plane, at] for d in range(1, 4)]
            value, memory, stiff = advance(
                cells[plane],
                previous,
                fields[:3],
                fields[3],
                forcing[plane, at],
                [first_diff(cells, plane), diff_y[plane, at], diff_z[plane, at]],
                lambda entry, block=plane // BLK: coef[entry, block, at],
                clock[2],
            )
            done = out_filtered[plane, at] + weights[2] * value
            for d in range(3):
                out_layer[d, plane, at] = memory[d]
            out_layer[3, plane, at] = stiff
            out_state[0, plane, at] = value
            out_filtered[plane, at] = done
            if not at_edge:
                total = total + done * done
        partial[...] = total

    over_rows(ny, third)


def finish_kernel(
    coef, clock, inside, across, across_late, ghost, partial, state_in, layer_in, filtered_in,
    out_state, out_layer, out_filtered, total_out,
):
    _, nx, ny, _ = state_in.shape
    n_block = nx // BLK
    even = is_even()
    weight = clock[2 * STEPS - 1]
    total_out[...] = partial[...]
    ghosts = (range(-REACH, 0), range(nx, nx + REACH))
    owned = (range(REACH), range(nx - REACH, nx))

    def step(rows):
        at = pl.ds(rows, BLK)
        halo = {}
        for number in range(REACH):
            one = inside[number, at]
            two = across[number, at] + across_late[number, at]
            halo[-REACH + number] = jnp.where(even, two, one) + ghost[number, at]
            halo[nx + number] = jnp.where(even, one, two) + ghost[REACH + number, at]
        total = total_out[...]
        for side in range(2):
            block = side * (n_block - 1)
            kappa_r, q0 = coef[KAPPA_R, block, at], coef[Q0, block, at]
            for plane in owned[side]:
                outer = outer_part(halo, plane, ghosts[side])
                added = kappa_r * outer
                out_state[0, plane, at] = state_in[0, plane, at] + added
                out_layer[0, plane, at] = layer_in[0, plane, at] + q0 * outer
                done = filtered_in[plane, at] + weight * added
                out_filtered[plane, at] = done
                total = total + done * done
        total_out[...] = total

    over_rows(ny, step)


def store_kernel(parts, values, *refs):
    n = len(parts)
    arrays, outs, values_out, sems = refs[:n], refs[-n - 2 : -2], refs[-2], refs[-1]
    copies = [
        pltpu.make_async_copy(
            *((array, out) if at is None else (array.at[at], out.at[at])), sems.at[number]
        )
        for number, (at, array, out) in enumerate(zip(parts, arrays, outs))
    ]
    for copy in copies:
        copy.start()
    values_out[...] = values[...]
    for copy in copies:
        copy.wait()


SCALAR = pl.BlockSpec(memory_space=pltpu.SMEM)
HBM = pl.BlockSpec(memory_space=pltpu.HBM)
VEC = pl.BlockSpec(memory_space=pltpu.VMEM)


def held(*shape):
    return pltpu.VMEM(shape, F32)


def in_vmem(*arrays):
    return [pltpu.with_memory_space_constraint(array, pltpu.VMEM) for array in arrays]


def in_hbm(*arrays):
    return [pltpu.with_memory_space_constraint(array, pltpu.HBM) for array in arrays]


def call(kernel, name, in_specs, out_shape, out_specs, scratch, operands, micros, aliases=None):
    return pl.pallas_call(
        kernel,
        name=name,
        in_specs=in_specs,
        out_shape=out_shape,
        out_specs=out_specs,
        scratch_shapes=scratch,
        input_output_aliases=aliases or {},
        compiler_params=pltpu.CompilerParams(vmem_limit_bytes=VMEM_LIMIT),
        cost_estimate=pl.CostEstimate(
            flops=0, bytes_accessed=int(micros * 3.6e6), transcendentals=0
        ),
    )(*operands)


def swap_pairs(count):
    inside = [(i, i ^ 1) for i in range(count)]
    across = []
    for i in range(1, count - 1, 2):
        across += [(i, i + 1), (i + 1, i)]
    return inside, across


def halves(pairs):
    return [[pair for pair in pairs if min(pair) % 4 == first] for first in (1, 3)]


def store(values, parts, arrays, begun=()):
    n = len(arrays)
    outs = [jax.ShapeDtypeStruct(array.shape, F32) for array in arrays]
    *stored, values = call(
        functools.partial(store_kernel, parts),
        "store",
        [VEC] * (1 + n) + [HBM] * len(begun),
        [*outs, held(*values.shape)],
        [HBM] * n + [VEC],
        [pltpu.SemaphoreType.DMA((n,))],
        (*in_vmem(values, *arrays), *begun),
        1,
        {1 + n + number: n - len(begun) + number for number in range(len(begun))},
    )
    return values, stored


def total_and_stores(values, state, layer, running, axis):
    count = lax.axis_size(axis)
    half = layer.shape[0] // 2
    stored = {}

    def first(values):
        values, (stored["state"],) = store(values, [None], [state])
        return values

    def second(values):
        values, (stored["layer"],) = store(values, [pl.ds(0, half)], [layer])
        return values

    def third(values):
        values, (stored["running"], stored["layer"]) = store(
            values, [None, pl.ds(half, half)], [running, layer], [stored["layer"]]
        )
        return values

    waiting = [first, second, third]
    hops = [] if count & (count - 1) else [1 << k for k in range(count.bit_length() - 1)]
    for number, hop in enumerate(hops):
        got = lax.ppermute(values, axis, [(i, i ^ hop) for i in range(count)])
        if waiting and number >= 1:
            values = waiting.pop(0)(values)
        values = values + got
    for step in waiting:
        values = step(values)
    if not hops:
        values = lax.psum(values, axis)
    return values, stored["state"], stored["layer"], stored["running"]


def body(
    wave_state, layer_fields, source, filtered, frequency, start_time, speed_table, speed_index,
    pml_mask,
):
    _, nx, ny, nz = wave_state.shape
    n_block = nx // BLK
    count = lax.axis_size("gx")
    pair_inside, pair_across = swap_pairs(count)
    brick = (nx, ny, nz)
    strip = (REACH, ny, nz)
    message = (2 * REACH * ny + 2 * TAG_ROWS, nz)
    dma = pltpu.SemaphoreType.DMA
    vec = lambda *shape: pltpu.VMEM(shape, F32)

    blocks = (speed_index.shape[1], n_block, speed_index.shape[2])
    index, mask = in_hbm(*(jnp.transpose(one, (1, 0, 2)) for one in (speed_index, pml_mask)))

    inside, across, coef, clock, edge, wave, layer, forcing = call(
        send_kernel,
        "strips",
        [HBM] * 3 + [SCALAR] * 2 + [HBM] * 3,
        [
            held(*message), held(*message), held(N_COEF, n_block, ny, nz),
            held(2 * STEPS, BLK, nz), held(2, 5, *strip), held(*wave_state.shape),
            held(*layer_fields.shape), held(*brick),
        ],
        [VEC] * 8,
        [
            vec(2 * REACH, ny, nz),
            vec(2 * REACH, ny, nz),
            vec(2, n_block * TAG_ROWS, nz),
            pltpu.VMEM(blocks, jnp.int32),
            pltpu.VMEM(blocks, jnp.int32),
            pltpu.SMEM(speed_table.shape, F32),
            dma((13,)),
        ],
        (
            *in_hbm(wave_state, layer_fields, source), frequency, start_time,
            *in_hbm(speed_table), index, mask,
        ),
        2.5,
    )
    got_inside = lax.ppermute(inside, "gx", pair_inside)
    got_across = lax.ppermute(across, "gx", pair_across)
    coef, clock, edge, wave, layer, forcing, running = in_vmem(
        coef, clock, edge, wave, layer, forcing, filtered
    )

    later_inside, later_across, first, second, run = call(
        local_kernel,
        "local",
        [VEC] * 6,
        [
            held(*strip), held(*strip), held(nx - 2 * REACH, ny, nz), held(5, *brick),
            held(*brick),
        ],
        [VEC] * 5,
        [vec(4, nx - 2 * REACH, ny, nz), vec(*brick), vec(*brick)],
        (wave, layer, forcing, coef, clock, edge),
        4,
    )
    last_inside = lax.ppermute(later_inside, "gx", pair_inside)
    early_pairs, late_pairs = halves(pair_across)
    last_across = lax.ppermute(later_across, "gx", early_pairs)
    later_across, got_across = lax.optimization_barrier((later_across, got_across))
    last_late = lax.ppermute(later_across, "gx", late_pairs)

    out_types = [
        held(*wave_state.shape), held(*layer_fields.shape), held(*filtered.shape)
    ]
    next_state, next_layer, next_filtered, ghost, partial = call(
        joint_kernel,
        "joint",
        [VEC] * 11,
        out_types + [held(2 * REACH, ny, nz), held(BLK, nz)],
        [VEC] * 5,
        [
            vec(4 * REACH, ny, nz),
            vec(4 * REACH, ny, nz),
            vec(4 * REACH, ny, nz),
            vec(2, 5, ny, nz),
            vec(*brick),
            vec(*brick),
            vec(4 * REACH, ny, nz),
            vec(4 * REACH, ny, nz),
        ],
        (
            coef, clock, *in_vmem(got_inside, got_across), wave, forcing, running, edge,
            *in_vmem(first, second, run),
        ),
        5,
    )
    next_state, next_layer, next_filtered, total = call(
        finish_kernel,
        "finish",
        [VEC] * 10,
        out_types + [held(BLK, nz)],
        [VEC] * 4,
        [],
        (
            coef, clock,
            *in_vmem(
                last_inside, last_across, last_late, ghost, partial,
                next_state, next_layer, next_filtered,
            ),
        ),
        1,
        {7: 0, 8: 1, 9: 2},
    )
    total, next_state, next_layer, next_filtered = total_and_stores(
        total, next_state, next_layer, next_filtered, "gx"
    )
    total = jnp.sum(total)
    filter_norm = jnp.sqrt(total / (filtered.size * count) + 1e-06)
    return next_state, next_layer, next_filtered, filter_norm.reshape(1)


def solution(mesh):
    placed = (
        P("grp", "gx", None, None),
        P("grp", "gx", None, None),
        P(("grp", "gx"), None, None),
        P(("grp", "gx"), None, None),
        P("grp"),
        P("grp"),
        P(),
        P("gx", None, None),
        P("gx", None, None),
    )
    return jax.shard_map(
        body,
        mesh=mesh,
        in_specs=placed,
        out_specs=(
            P("grp", "gx", None, None),
            P("grp", "gx", None, None),
            P(("grp", "gx"), None, None),
            P("grp"),
        ),
        check_vma=False,
    )
```

```python
import functools
import math

import jax
import jax.numpy as jnp
from jax import lax
from jax.experimental import pallas as pl
from jax.experimental.pallas import tpu as pltpu
from jax.sharding import PartitionSpec as P

F32 = jnp.float32
BF16 = jnp.bfloat16
STEPS = 3
BLK = 8
REACH = 4
TIME_STEP = 0.25
DAMP_PEAK = 1.5
STENCIL = (-205.0 / 72.0, 8.0 / 5.0, -1.0 / 5.0, 8.0 / 315.0, -1.0 / 560.0)
SCALE = 5040.0
WHOLE = (-14336.0, 8064.0, -1008.0, 128.0, -9.0)
CENTRE_REST = 14.0 / SCALE
TAG_ROWS = 16
KAPPA, KAPPA_R, Q0, Q1, Q2, B0, B1, B2, DECAY, PAIR, AMP, BACK, STIFF, FORCE = range(14)
N_COEF = 14
VMEM_LIMIT = 30 * 1024 * 1024


def band(rows, cols, row_period, col_period):
    row = lax.broadcasted_iota(jnp.int32, (rows, cols), 0) % row_period
    col = lax.broadcasted_iota(jnp.int32, (rows, cols), 1) % col_period
    apart = jnp.abs(row - col)
    out = jnp.zeros((rows, cols), F32)
    for offset, value in enumerate(WHOLE):
        out = jnp.where(apart == offset, value, out)
    return out.astype(BF16)


def pieces(cells):
    high = cells.astype(BF16)
    return high, (cells - high.astype(F32)).astype(BF16)


def cross_diffs(planes, read, write_y, write_z, ny, nz):
    mat_y = band(ny, 2 * ny, ny, ny)
    mat_z = band(2 * nz, nz, nz, nz)
    for one, two in zip(planes[0::2], planes[1::2]):
        high_one, low_one = pieces(read(one))
        high_two, low_two = pieces(read(two))
        upper = jnp.concatenate([high_one, high_two], axis=1)
        lower = jnp.concatenate([low_one, low_two], axis=1)
        diff_y = jnp.dot(
            mat_y, jnp.concatenate([upper, lower], axis=0), preferred_element_type=F32
        )
        write_y(one, diff_y[:, :nz])
        write_y(two, diff_y[:, nz:])
        left = jnp.concatenate([high_one, low_one], axis=1)
        right = jnp.concatenate([high_two, low_two], axis=1)
        diff_z = jnp.dot(
            jnp.concatenate([left, right], axis=0), mat_z, preferred_element_type=F32
        )
        write_z(one, diff_z[:ny])
        write_z(two, diff_z[ny:])


def first_diff(cells, at):
    total = STENCIL[0] * cells[at]
    for offset in range(1, REACH + 1):
        above, below = cells.get(at + offset), cells.get(at - offset)
        if above is not None and below is not None:
            total = total + STENCIL[offset] * (above + below)
        elif above is not None:
            total = total + STENCIL[offset] * above
        elif below is not None:
            total = total + STENCIL[offset] * below
    return total


def outer_part(cells, at, positions):
    total = None
    for position in positions:
        offset = abs(position - at)
        if offset <= REACH:
            term = STENCIL[offset] * cells[position]
            total = term if total is None else total + term
    return total


def advance(cells, previous, memory, stiff, forcing, diffs, co, phase):
    rest = CENTRE_REST * cells
    diffs = [diffs[0], diffs[1] * (1.0 / SCALE) - rest, diffs[2] * (1.0 / SCALE) - rest]
    memory = [m + co(Q0 + d) * (diffs[d] - m) for d, m in enumerate(memory)]
    inner = sum(diffs[d] - co(B0 + d) * memory[d] for d in range(3))
    stiff = co(DECAY) * stiff + co(PAIR) * cells
    new = (
        co(AMP) * cells
        - co(BACK) * previous
        + co(KAPPA) * inner
        - co(STIFF) * stiff
        - (co(FORCE) * phase) * forcing
    )
    return new, memory, stiff


def coefficients(speed_square, bits):
    rates = [DAMP_PEAK * bit for bit in bits]
    damping = rates[0] + rates[1] + rates[2]
    pairing = rates[0] * rates[1] + rates[1] * rates[2] + rates[2] * rates[0]
    retention = [jnp.exp(-TIME_STEP * rate) for rate in rates]
    half = 0.5 * TIME_STEP * damping
    inverse = 1.0 / (1.0 + half)
    square = TIME_STEP * TIME_STEP
    kappa = square * speed_square * inverse
    return (
        kappa,
        kappa * retention[0],
        1.0 - retention[0],
        1.0 - retention[1],
        1.0 - retention[2],
        bits[0],
        bits[1],
        bits[2],
        jnp.exp(-TIME_STEP * damping),
        TIME_STEP * pairing,
        (2.0 - square * pairing) * inverse,
        (1.0 - half) * inverse,
        square * damping * inverse,
        square * inverse,
    )


def along_last(tiles, nz):
    row = lax.broadcasted_iota(jnp.int32, (nz, nz), 0)
    col = lax.broadcasted_iota(jnp.int32, (nz, nz), 1) // BLK
    along = (row == col).astype(F32).astype(BF16)
    return jnp.dot(tiles.astype(BF16), along, preferred_element_type=F32)


def squares(index, table):
    speed = jnp.zeros_like(index)
    for entry in range(table.shape[0]):
        speed = jnp.where(index == float(entry), table[entry], speed)
    return speed * speed


def bits_of(mask):
    mask = mask.astype(jnp.int32)
    return [((mask >> direction) & 1).astype(F32) for direction in range(3)]


def down_second(ref, lead, value, ny):
    for block in range(ny // BLK):
        rows = jnp.broadcast_to(value[block : block + 1], (BLK, value.shape[1]))
        ref[(*lead, pl.ds(block * BLK, BLK))] = rows


def fill_clock(clock, freq, start):
    steps = lax.broadcasted_iota(jnp.int32, clock.shape[1:], 0).astype(F32)
    cosine = jnp.cos(freq[0] * (start[0] + steps * TIME_STEP))
    weight = (TIME_STEP * freq[0] / math.pi) * (cosine - 0.25)
    for count in range(STEPS):
        clock[count] = jnp.broadcast_to(cosine[count : count + 1], cosine.shape)
        clock[STEPS + count] = jnp.broadcast_to(weight[count + 1 : count + 2], weight.shape)


def over_rows(ny, step):
    def one(block, carry):
        step(pl.multiple_of(block * BLK, BLK))
        return carry

    lax.fori_loop(0, ny // BLK, one, 0)


def is_even():
    return lax.axis_index("gx") % 2 == 0


def edge_planes(nx):
    return [*range(REACH), *range(nx - REACH, nx)]


def send_kernel(
    wave_in, layer_in, source_in, freq, start, table_in, index_in, mask_in,
    inside, across, coef, clock, edge, wave, layer, source,
    diff_y, diff_z, tags, index, mask, table, sems,
):
    _, nx, ny, nz = wave.shape
    n_block = nx // BLK
    edges = (0, nx - REACH)
    pieces_of = [(wave_in.at[0], wave.at[0])]
    for first, length in ((0, REACH), (nx - REACH, REACH), (REACH, nx - 2 * REACH)):
        at = pl.ds(first, length)
        pieces_of += [
            (wave_in.at[1, at], wave.at[1, at]),
            (layer_in.at[:, at], layer.at[:, at]),
            (source_in.at[at], source.at[at]),
        ]
    copies = [
        pltpu.make_async_copy(one, to, sems.at[number])
        for number, (one, to) in enumerate(pieces_of)
    ]
    small = [
        pltpu.make_async_copy(one, to, sems.at[len(copies) + number])
        for number, (one, to) in enumerate(
            ((index_in, index), (mask_in, mask), (table_in, table))
        )
    ]
    for copy in small + copies:
        copy.start()
    even = is_even()
    tags[...] = jnp.zeros_like(tags)
    fill_clock(clock, freq, start)
    phase = clock[0]
    for copy in small:
        copy.wait()
    rows = n_block * TAG_ROWS
    for block in range(n_block):
        at = pl.ds(block * TAG_ROWS, index.shape[0])
        tags[0, at, : index.shape[2]] = index[:, block].astype(F32)
        tags[1, at, : mask.shape[2]] = mask[:, block].astype(F32)
    wide = along_last(tags[...].reshape(2 * rows, nz), nz)
    square = squares(wide[:rows], table)
    masks = wide[rows:]
    values = coefficients(square, bits_of(masks))
    for entry, value in enumerate(values):
        for block in range(n_block):
            down_second(coef, (entry, block), value[block * TAG_ROWS : (block + 1) * TAG_ROWS], ny)
    for part, value in enumerate((square, masks)):
        to = pl.ds(2 * REACH * ny + part * TAG_ROWS, TAG_ROWS)
        left, right = value[:TAG_ROWS], value[rows - TAG_ROWS :]
        inside[to] = jnp.where(even, right, left)
        across[to] = jnp.where(even, left, right)
    copies[0].wait()
    planes = edge_planes(nx)
    slot = {plane: number for number, plane in enumerate(planes)}

    def put_y(plane, value):
        diff_y[slot[plane]] = value

    def put_z(plane, value):
        diff_z[slot[plane]] = value

    cross_diffs(planes, lambda plane: wave[0, plane], put_y, put_z, ny, nz)
    for copy in copies[1:7]:
        copy.wait()

    def step(rows):
        at = pl.ds(rows, BLK)
        sides = []
        for side in range(2):
            block = side * (n_block - 1)
            reach = range(2 * REACH) if side == 0 else range(nx - 2 * REACH, nx)
            cells = {plane: wave[0, plane, at] for plane in reach}
            values = []
            for number in range(REACH):
                plane = edges[side] + number
                new, memory, stiff = advance(
                    cells[plane],
                    wave[1, plane, at],
                    [layer[d, plane, at] for d in range(3)],
                    layer[3, plane, at],
                    source[plane, at],
                    [
                        first_diff(cells, plane),
                        diff_y[slot[plane], at],
                        diff_z[slot[plane], at],
                    ],
                    lambda entry, block=block: coef[entry, block, at],
                    phase,
                )
                for entry, value in enumerate((new, *memory, stiff)):
                    edge[side, entry, number, at] = value
                values.append((cells[plane], new))
            sides.append(values)
        for number in range(REACH):
            for part in range(2):
                to = pl.ds(pl.multiple_of((part * REACH + number) * ny + rows, BLK), BLK)
                left, right = sides[0][number][part], sides[1][number][part]
                inside[to] = jnp.where(even, right, left)
                across[to] = jnp.where(even, left, right)

    over_rows(ny, step)
    for copy in copies[7:]:
        copy.wait()


def local_kernel(
    wave, layer, source, coef, clock, edge,
    inside, across, first_out, second_out, run_out,
    fields, diff_y, diff_z,
):
    _, nx, ny, nz = wave.shape
    even = is_even()

    def put_y(plane, value):
        diff_y[plane] = value

    def put_z(plane, value):
        diff_z[plane] = value

    middle = range(REACH, nx - REACH)
    cross_diffs(middle, lambda plane: wave[0, plane], put_y, put_z, ny, nz)

    def read(entry, plane, at=slice(None)):
        if plane < REACH:
            return edge[0, entry, plane, at]
        if plane >= nx - REACH:
            return edge[1, entry, plane - nx + REACH, at]
        if entry == 0:
            return first_out[plane - REACH, at]
        return fields[entry - 1, plane - REACH, at]

    def first(rows):
        at = pl.ds(rows, BLK)
        cells = {plane: wave[0, plane, at] for plane in range(nx)}
        for plane in middle:
            new, memory, stiff = advance(
                cells[plane],
                wave[1, plane, at],
                [layer[d, plane, at] for d in range(3)],
                layer[3, plane, at],
                source[plane, at],
                [first_diff(cells, plane), diff_y[plane, at], diff_z[plane, at]],
                lambda entry, block=plane // BLK: coef[entry, block, at],
                clock[0],
            )
            first_out[plane - REACH, at] = new
            for entry, value in enumerate((*memory, stiff)):
                fields[entry, plane - REACH, at] = value

    over_rows(ny, first)
    cross_diffs(range(nx), lambda plane: read(0, plane), put_y, put_z, ny, nz)

    def second(rows):
        at = pl.ds(rows, BLK)
        cells = {plane: read(0, plane, at) for plane in range(nx)}
        values = {}
        for plane in range(nx):
            new, memory, stiff = advance(
                cells[plane],
                wave[0, plane, at],
                [read(1 + d, plane, at) for d in range(3)],
                read(4, plane, at),
                source[plane, at],
                [first_diff(cells, plane), diff_y[plane, at], diff_z[plane, at]],
                lambda entry, block=plane // BLK: coef[entry, block, at],
                clock[1],
            )
            values[plane] = new
            for entry, value in enumerate((new, *memory, stiff)):
                second_out[entry, plane, at] = value
            run_out[plane, at] = clock[STEPS] * cells[plane] + clock[STEPS + 1] * new
        for number in range(REACH):
            left, right = values[number], values[nx - REACH + number]
            inside[number, at] = jnp.where(even, right, left)
            across[number, at] = jnp.where(even, left, right)

    over_rows(ny, second)


def side_update(
    left, present, message, coef, clock, wave, running, edge, second_in, run_in,
    out_state, out_layer, out_filtered, ext, ghost,
    first, bump, push, ghost_coef, bump_y, bump_z,
):
    _, nx, ny, nz = wave.shape
    n_block = nx // BLK
    block = jnp.where(left, 0, n_block - 1)
    side = jnp.where(left, 0, 1)
    own = range(REACH)
    beyond = range(-1, -1 - REACH, -1)
    weights = [clock[STEPS + number] for number in range(2)]

    def plane_of(depth):
        return jnp.where(left, depth, nx - 1 - depth)

    def slot(depth):
        return depth if depth >= 0 else REACH - 1 - depth

    tag_at = 2 * REACH * ny
    square = message[pl.ds(tag_at, TAG_ROWS)] * present
    values = coefficients(square, bits_of(message[pl.ds(tag_at + TAG_ROWS, TAG_ROWS)]))
    for entry, value in enumerate(
        (
            values[KAPPA_R],
            values[Q0],
            values[KAPPA] * (1.0 - values[Q1]),
            values[KAPPA] * (1.0 - values[Q2]),
            values[AMP] - values[STIFF] * values[PAIR],
        )
    ):
        down_second(ghost_coef, (entry,), value, ny)

    def exchange(rows):
        at = pl.ds(rows, BLK)
        halo = {}
        sent = {}
        for depth in beyond:
            number = jnp.where(left, REACH + depth, -1 - depth)
            halo[depth] = message[pl.ds(pl.multiple_of(number * ny + rows, BLK), BLK)]
            number = number + REACH
            sent[depth] = message[pl.ds(pl.multiple_of(number * ny + rows, BLK), BLK)]
        mine = {depth: wave[0, plane_of(depth), at] for depth in own}
        kappa_r = coef[KAPPA_R, block, at]
        for depth in own:
            outer = outer_part(halo, depth, beyond)
            added = kappa_r * outer
            push[slot(depth), at] = outer
            bump[slot(depth), at] = added
            value = edge[side, 0, jnp.where(left, depth, REACH - 1 - depth), at] + added
            first[slot(depth), at] = value
            ext[jnp.where(left, depth, 2 * REACH - 1 - depth), at] = value
        kappa_r = ghost_coef[0, at]
        for depth in beyond:
            outer = outer_part(mine, depth, own)
            added = kappa_r * outer
            push[slot(depth), at] = outer
            bump[slot(depth), at] = added
            first[slot(depth), at] = sent[depth] + added

    over_rows(ny, exchange)

    def put_bump_y(plane, value):
        bump_y[plane] = value

    def put_bump_z(plane, value):
        bump_z[plane] = value

    cross_diffs(range(2 * REACH), lambda plane: bump[plane], put_bump_y, put_bump_z, ny, nz)

    def respond(added, true, depth, others, outer, q0, kappas, at):
        kappa_r, kappa_1, kappa_2, grown = kappas
        value = added[depth]
        rest = CENTRE_REST * value
        along = first_diff(added, depth) + outer_part(true, depth, others)
        side_y = bump_y[slot(depth), at] * (1.0 / SCALE) - rest
        side_z = bump_z[slot(depth), at] * (1.0 / SCALE) - rest
        gain = (
            grown * value + kappa_r * (along - q0 * outer) + kappa_1 * side_y + kappa_2 * side_z
        )
        return gain, along, side_y, side_z

    def second(rows):
        at = pl.ds(rows, BLK)
        true = {depth: first[slot(depth), at] for depth in (*own, *beyond)}
        added = {depth: bump[slot(depth), at] for depth in beyond}
        kappa_r, q0, kappa_1, kappa_2, grown = [ghost_coef[entry, at] for entry in range(5)]
        for depth in beyond:
            ghost[-1 - depth, at], _, _, _ = respond(
                added, true, depth, own, push[slot(depth), at], q0,
                (kappa_r, kappa_1, kappa_2, grown), at,
            )
        added = {depth: bump[slot(depth), at] for depth in own}
        kappa_r, kappa = coef[KAPPA_R, block, at], coef[KAPPA, block, at]
        q0, q1, q2 = [coef[entry, block, at] for entry in (Q0, Q1, Q2)]
        pair = coef[PAIR, block, at]
        kappas = (
            kappa_r,
            kappa * (1.0 - q1),
            kappa * (1.0 - q2),
            coef[AMP, block, at] - coef[STIFF, block, at] * pair,
        )
        for depth in own:
            plane = plane_of(depth)
            outer = push[slot(depth), at]
            gain, along, side_y, side_z = respond(
                added, true, depth, beyond, outer, q0, kappas, at
            )
            out_state[1, plane, at] = second_in[0, plane, at] + gain
            out_layer[0, plane, at] = second_in[1, plane, at] + q0 * (
                along + (1.0 - q0) * outer
            )
            out_layer[1, plane, at] = second_in[2, plane, at] + q1 * side_y
            out_layer[2, plane, at] = second_in[3, plane, at] + q2 * side_z
            out_layer[3, plane, at] = second_in[4, plane, at] + pair * added[depth]
            out_filtered[plane, at] = (
                running[plane, at]
                + run_in[plane, at]
                + weights[0] * added[depth]
                + weights[1] * gain
            )
        for depth in range(REACH, 2 * REACH):
            plane = plane_of(depth)
            along = outer_part(added, depth, own)
            gain = kappa_r * along
            out_state[1, plane, at] = second_in[0, plane, at] + gain
            out_layer[0, plane, at] = second_in[1, plane, at] + q0 * along
            out_filtered[plane, at] = running[plane, at] + run_in[plane, at] + weights[1] * gain

    over_rows(ny, second)


def inside_kernel(
    inside, coef, clock, wave, running, edge, second_in, run_in,
    out_state, out_layer, out_filtered, ext, ghost,
    *scratch,
):
    side_update(
        jnp.logical_not(is_even()), 1.0, inside, coef, clock, wave, running, edge, second_in,
        run_in, out_state, out_layer, out_filtered, ext, ghost, *scratch,
    )


def joint_kernel(
    across, coef, clock, wave, forcing, running, edge, first_in, second_in, run_in,
    state_in, layer_in, filtered_in, ext_in,
    out_state, out_layer, out_filtered, ext, ghost, partial,
    diff_y, diff_z, *scratch,
):
    del state_in, layer_in, filtered_in, ext_in
    _, nx, ny, nz = wave.shape
    count = lax.axis_size("gx")
    place = lax.axis_index("gx")
    even = is_even()
    weights = [clock[STEPS + number] for number in range(STEPS)]
    outermost = jnp.logical_or(place == 0, place == count - 1)
    side_update(
        even, jnp.where(outermost, 0.0, 1.0).astype(F32), across, coef, clock, wave, running,
        edge, second_in, run_in, out_state, out_layer, out_filtered, ext, ghost, *scratch,
    )
    if nx > 4 * REACH:

        def between(rows):
            at = pl.ds(rows, BLK)
            for plane in range(2 * REACH, nx - 2 * REACH):
                out_state[1, plane, at] = second_in[0, plane, at]
                out_layer[0, plane, at] = second_in[1, plane, at]
                out_filtered[plane, at] = running[plane, at] + run_in[plane, at]

        over_rows(ny, between)

    def put_y(plane, value):
        diff_y[plane] = value

    def put_z(plane, value):
        diff_z[plane] = value

    cross_diffs(range(nx), lambda plane: out_state[1, plane], put_y, put_z, ny, nz)
    partial[...] = jnp.zeros_like(partial)

    def third(rows):
        at = pl.ds(rows, BLK)
        cells = {plane: out_state[1, plane, at] for plane in range(nx)}
        total = partial[...]
        for plane in range(nx):
            at_edge = plane < REACH or plane >= nx - REACH
            if at_edge:
                previous = ext[plane if plane < REACH else plane - nx + 2 * REACH, at]
                fields = [out_layer[d, plane, at] for d in range(4)]
            else:
                previous = first_in[plane - REACH, at]
                fields = [out_layer[0, plane, at]]
                fields += [second_in[1 + d, plane, at] for d in range(1, 4)]
            value, memory, stiff = advance(
                cells[plane],
                previous,
                fields[:3],
                fields[3],
                forcing[plane, at],
                [first_diff(cells, plane), diff_y[plane, at], diff_z[plane, at]],
                lambda entry, block=plane // BLK: coef[entry, block, at],
                clock[2],
            )
            done = out_filtered[plane, at] + weights[2] * value
            for d in range(3):
                out_layer[d, plane, at] = memory[d]
            out_layer[3, plane, at] = stiff
            out_state[0, plane, at] = value
            out_filtered[plane, at] = done
            if not at_edge:
                total = total + done * done
        partial[...] = total

    over_rows(ny, third)


def finish_kernel(
    coef, clock, inside, across, across_late, ghost_inside, ghost_across, partial,
    state_in, layer_in, filtered_in,
    out_state, out_layer, out_filtered, total_out,
):
    _, nx, ny, _ = state_in.shape
    n_block = nx // BLK
    even = is_even()
    weight = clock[2 * STEPS - 1]
    total_out[...] = partial[...]
    ghosts = (range(-REACH, 0), range(nx, nx + REACH))
    owned = (range(REACH), range(nx - REACH, nx))

    def step(rows):
        at = pl.ds(rows, BLK)
        halo = {}
        for number in range(REACH):
            one = inside[number, at]
            two = across[number, at] + across_late[number, at]
            left = jnp.where(even, two, one)
            right = jnp.where(even, one, two)
            one, two = ghost_inside[REACH - 1 - number, at], ghost_across[REACH - 1 - number, at]
            halo[-REACH + number] = left + jnp.where(even, two, one)
            one, two = ghost_inside[number, at], ghost_across[number, at]
            halo[nx + number] = right + jnp.where(even, one, two)
        total = total_out[...]
        for side in range(2):
            block = side * (n_block - 1)
            kappa_r, q0 = coef[KAPPA_R, block, at], coef[Q0, block, at]
            for plane in owned[side]:
                outer = outer_part(halo, plane, ghosts[side])
                added = kappa_r * outer
                out_state[0, plane, at] = state_in[0, plane, at] + added
                out_layer[0, plane, at] = layer_in[0, plane, at] + q0 * outer
                done = filtered_in[plane, at] + weight * added
                out_filtered[plane, at] = done
                total = total + done * done
        total_out[...] = total

    over_rows(ny, step)


def store_kernel(parts, values, *refs):
    n = len(parts)
    arrays, outs, values_out, sems = refs[:n], refs[-n - 2 : -2], refs[-2], refs[-1]
    copies = [
        pltpu.make_async_copy(
            *((array, out) if at is None else (array.at[at], out.at[at])), sems.at[number]
        )
        for number, (at, array, out) in enumerate(zip(parts, arrays, outs))
    ]
    for copy in copies:
        copy.start()
    values_out[...] = values[...]
    for copy in copies:
        copy.wait()


def norm_kernel(cells, values, got, norm):
    total = jnp.sum(values[...] + got[...], axis=1, keepdims=True)
    total = jnp.sum(total, axis=0, keepdims=True)
    norm[...] = jnp.sqrt(total / cells + 1e-06)


SCALAR = pl.BlockSpec(memory_space=pltpu.SMEM)
HBM = pl.BlockSpec(memory_space=pltpu.HBM)
VEC = pl.BlockSpec(memory_space=pltpu.VMEM)


def held(*shape):
    return pltpu.VMEM(shape, F32)


def in_vmem(*arrays):
    return [pltpu.with_memory_space_constraint(array, pltpu.VMEM) for array in arrays]


def in_hbm(*arrays):
    return [pltpu.with_memory_space_constraint(array, pltpu.HBM) for array in arrays]


def call(kernel, name, in_specs, out_shape, out_specs, scratch, operands, micros, aliases=None):
    return pl.pallas_call(
        kernel,
        name=name,
        in_specs=in_specs,
        out_shape=out_shape,
        out_specs=out_specs,
        scratch_shapes=scratch,
        input_output_aliases=aliases or {},
        compiler_params=pltpu.CompilerParams(vmem_limit_bytes=VMEM_LIMIT),
        cost_estimate=pl.CostEstimate(
            flops=0, bytes_accessed=int(micros * 3.6e6), transcendentals=0
        ),
    )(*operands)


def swap_pairs(count):
    inside = [(i, i ^ 1) for i in range(count)]
    across = []
    for i in range(1, count - 1, 2):
        across += [(i, i + 1), (i + 1, i)]
    return inside, across


def halves(pairs):
    return [[pair for pair in pairs if min(pair) % 4 == first] for first in (1, 3)]


def store(values, parts, arrays, begun=()):
    n = len(arrays)
    outs = [jax.ShapeDtypeStruct(array.shape, F32) for array in arrays]
    *stored, values = call(
        functools.partial(store_kernel, parts),
        "store",
        [VEC] * (1 + n) + [HBM] * len(begun),
        [*outs, held(*values.shape)],
        [HBM] * n + [VEC],
        [pltpu.SemaphoreType.DMA((n,))],
        (*in_vmem(values, *arrays), *begun),
        1,
        {1 + n + number: n - len(begun) + number for number in range(len(begun))},
    )
    return values, stored


def norm_and_stores(values, state, layer, running, axis):
    count = lax.axis_size(axis)
    half = layer.shape[0] // 2
    stored = {}

    def first(values):
        values, (stored["state"],) = store(values, [None], [state])
        return values

    def second(values):
        values, (stored["layer"],) = store(values, [pl.ds(0, half)], [layer])
        return values

    def third(values):
        values, (stored["running"], stored["layer"]) = store(
            values, [None, pl.ds(half, half)], [running, layer], [stored["layer"]]
        )
        return values

    waiting = [first, second, third]
    hops = [] if count & (count - 1) else [1 << k for k in range(count.bit_length() - 1)]
    for number, hop in enumerate(hops):
        got = lax.ppermute(values, axis, [(i, i ^ hop) for i in range(count)])
        if waiting and number >= 1:
            values = waiting.pop(0)(values)
        if hop != hops[-1]:
            values = values + got
    for step in waiting:
        values = step(values)
    if not hops:
        values, got = lax.psum(values, axis), jnp.zeros_like(values)
    norm = call(
        functools.partial(norm_kernel, float(running.size * count)),
        "norm",
        [VEC] * 2,
        jax.ShapeDtypeStruct((1, 1), F32),
        VEC,
        [],
        in_vmem(values, got),
        1,
    )
    return norm.reshape(1), stored["state"], stored["layer"], stored["running"]


def body(
    wave_state, layer_fields, source, filtered, frequency, start_time, speed_table, speed_index,
    pml_mask,
):
    _, nx, ny, nz = wave_state.shape
    n_block = nx // BLK
    count = lax.axis_size("gx")
    pair_inside, pair_across = swap_pairs(count)
    brick = (nx, ny, nz)
    strip = (REACH, ny, nz)
    message = (2 * REACH * ny + 2 * TAG_ROWS, nz)
    dma = pltpu.SemaphoreType.DMA
    vec = lambda *shape: pltpu.VMEM(shape, F32)

    blocks = (speed_index.shape[1], n_block, speed_index.shape[2])
    index, mask = in_hbm(*(jnp.transpose(one, (1, 0, 2)) for one in (speed_index, pml_mask)))

    inside, across, coef, clock, edge, wave, layer, forcing = call(
        send_kernel,
        "strips",
        [HBM] * 3 + [SCALAR] * 2 + [HBM] * 3,
        [
            held(*message), held(*message), held(N_COEF, n_block, ny, nz),
            held(2 * STEPS, BLK, nz), held(2, 5, *strip), held(*wave_state.shape),
            held(*layer_fields.shape), held(*brick),
        ],
        [VEC] * 8,
        [
            vec(2 * REACH, ny, nz),
            vec(2 * REACH, ny, nz),
            vec(2, n_block * TAG_ROWS, nz),
            pltpu.VMEM(blocks, jnp.int32),
            pltpu.VMEM(blocks, jnp.int32),
            pltpu.SMEM(speed_table.shape, F32),
            dma((13,)),
        ],
        (
            *in_hbm(wave_state, layer_fields, source), frequency, start_time,
            *in_hbm(speed_table), index, mask,
        ),
        2.5,
    )
    got_inside = lax.ppermute(inside, "gx", pair_inside)
    got_across = lax.ppermute(across, "gx", pair_across)
    coef, clock, edge, wave, layer, forcing, running = in_vmem(
        coef, clock, edge, wave, layer, forcing, filtered
    )

    later_inside, later_across, first, second, run = call(
        local_kernel,
        "local",
        [VEC] * 6,
        [
            held(*strip), held(*strip), held(nx - 2 * REACH, ny, nz), held(5, *brick),
            held(*brick),
        ],
        [VEC] * 5,
        [vec(4, nx - 2 * REACH, ny, nz), vec(*brick), vec(*brick)],
        (wave, layer, forcing, coef, clock, edge),
        4,
    )
    last_inside = lax.ppermute(later_inside, "gx", pair_inside)
    early_pairs, late_pairs = halves(pair_across)
    last_across = lax.ppermute(later_across, "gx", early_pairs)
    out_types = [
        held(*wave_state.shape), held(*layer_fields.shape), held(*filtered.shape)
    ]
    edge_type = held(2 * REACH, ny, nz)
    side_scratch = [vec(2 * REACH, ny, nz)] * 3 + [vec(5, ny, nz)] + [vec(2 * REACH, ny, nz)] * 2
    later_across, got_inside = lax.optimization_barrier((later_across, got_inside))
    last_late = lax.ppermute(later_across, "gx", late_pairs)
    first, second, run = in_vmem(first, second, run)
    next_state, next_layer, next_filtered, ext, ghost_inside = call(
        inside_kernel,
        "inner_half",
        [VEC] * 8,
        out_types + [edge_type, held(*strip)],
        [VEC] * 5,
        side_scratch,
        (*in_vmem(got_inside), coef, clock, wave, running, edge, second, run),
        1.5,
    )
    next_state, next_layer, next_filtered, ext, ghost_across, partial = call(
        joint_kernel,
        "joint",
        [VEC] * 14,
        out_types + [edge_type, held(*strip), held(BLK, nz)],
        [VEC] * 6,
        [vec(*brick), vec(*brick), *side_scratch],
        (
            *in_vmem(got_across), coef, clock, wave, forcing, running, edge, first, second, run,
            *in_vmem(next_state, next_layer, next_filtered, ext),
        ),
        5,
        {10: 0, 11: 1, 12: 2, 13: 3},
    )
    next_state, next_layer, next_filtered, total = call(
        finish_kernel,
        "finish",
        [VEC] * 11,
        out_types + [held(BLK, nz)],
        [VEC] * 4,
        [],
        (
            coef, clock,
            *in_vmem(
                last_inside, last_across, last_late, ghost_inside, ghost_across, partial,
                next_state, next_layer, next_filtered,
            ),
        ),
        1,
        {8: 0, 9: 1, 10: 2},
    )
    filter_norm, next_state, next_layer, next_filtered = norm_and_stores(
        total, next_state, next_layer, next_filtered, "gx"
    )
    return next_state, next_layer, next_filtered, filter_norm


def solution(mesh):
    placed = (
        P("grp", "gx", None, None),
        P("grp", "gx", None, None),
        P(("grp", "gx"), None, None),
        P(("grp", "gx"), None, None),
        P("grp"),
        P("grp"),
        P(),
        P("gx", None, None),
        P("gx", None, None),
    )
    return jax.shard_map(
        body,
        mesh=mesh,
        in_specs=placed,
        out_specs=(
            P("grp", "gx", None, None),
            P("grp", "gx", None, None),
            P(("grp", "gx"), None, None),
            P("grp"),
        ),
        check_vma=False,
    )
```

```python
import functools
import math

import jax
import jax.numpy as jnp
from jax import lax
from jax.experimental import pallas as pl
from jax.experimental.pallas import tpu as pltpu
from jax.sharding import PartitionSpec as P

F32 = jnp.float32
BF16 = jnp.bfloat16
STEPS = 3
BLK = 8
REACH = 4
TIME_STEP = 0.25
DAMP_PEAK = 1.5
STENCIL = (-205.0 / 72.0, 8.0 / 5.0, -1.0 / 5.0, 8.0 / 315.0, -1.0 / 560.0)
SCALE = 5040.0
WHOLE = (-14336.0, 8064.0, -1008.0, 128.0, -9.0)
CENTRE_REST = 14.0 / SCALE
TAG_ROWS = 16
KAPPA, KAPPA_R, Q0, Q1, Q2, B0, B1, B2, DECAY, PAIR, AMP, BACK, STIFF, FORCE = range(14)
N_COEF = 14
VMEM_LIMIT = 30 * 1024 * 1024


def band(rows, cols, row_period, col_period):
    row = lax.broadcasted_iota(jnp.int32, (rows, cols), 0) % row_period
    col = lax.broadcasted_iota(jnp.int32, (rows, cols), 1) % col_period
    apart = jnp.abs(row - col)
    out = jnp.zeros((rows, cols), F32)
    for offset, value in enumerate(WHOLE):
        out = jnp.where(apart == offset, value, out)
    return out.astype(BF16)


def pieces(cells):
    high = cells.astype(BF16)
    return high, (cells - high.astype(F32)).astype(BF16)


def cross_diffs(planes, read, write_y, write_z, ny, nz):
    mat_y = band(ny, 2 * ny, ny, ny)
    mat_z = band(2 * nz, nz, nz, nz)
    for one, two in zip(planes[0::2], planes[1::2]):
        high_one, low_one = pieces(read(one))
        high_two, low_two = pieces(read(two))
        upper = jnp.concatenate([high_one, high_two], axis=1)
        lower = jnp.concatenate([low_one, low_two], axis=1)
        diff_y = jnp.dot(
            mat_y, jnp.concatenate([upper, lower], axis=0), preferred_element_type=F32
        )
        write_y(one, diff_y[:, :nz])
        write_y(two, diff_y[:, nz:])
        left = jnp.concatenate([high_one, low_one], axis=1)
        right = jnp.concatenate([high_two, low_two], axis=1)
        diff_z = jnp.dot(
            jnp.concatenate([left, right], axis=0), mat_z, preferred_element_type=F32
        )
        write_z(one, diff_z[:ny])
        write_z(two, diff_z[ny:])


def first_diff(cells, at):
    total = STENCIL[0] * cells[at]
    for offset in range(1, REACH + 1):
        above, below = cells.get(at + offset), cells.get(at - offset)
        if above is not None and below is not None:
            total = total + STENCIL[offset] * (above + below)
        elif above is not None:
            total = total + STENCIL[offset] * above
        elif below is not None:
            total = total + STENCIL[offset] * below
    return total


def outer_part(cells, at, positions):
    total = None
    for position in positions:
        offset = abs(position - at)
        if offset <= REACH:
            term = STENCIL[offset] * cells[position]
            total = term if total is None else total + term
    return total


def advance(cells, previous, memory, stiff, forcing, diffs, co, phase):
    rest = CENTRE_REST * cells
    diffs = [diffs[0], diffs[1] * (1.0 / SCALE) - rest, diffs[2] * (1.0 / SCALE) - rest]
    memory = [m + co(Q0 + d) * (diffs[d] - m) for d, m in enumerate(memory)]
    inner = sum(diffs[d] - co(B0 + d) * memory[d] for d in range(3))
    stiff = co(DECAY) * stiff + co(PAIR) * cells
    new = (
        co(AMP) * cells
        - co(BACK) * previous
        + co(KAPPA) * inner
        - co(STIFF) * stiff
        - (co(FORCE) * phase) * forcing
    )
    return new, memory, stiff


def coefficients(speed_square, bits):
    rates = [DAMP_PEAK * bit for bit in bits]
    damping = rates[0] + rates[1] + rates[2]
    pairing = rates[0] * rates[1] + rates[1] * rates[2] + rates[2] * rates[0]
    retention = [jnp.exp(-TIME_STEP * rate) for rate in rates]
    half = 0.5 * TIME_STEP * damping
    inverse = 1.0 / (1.0 + half)
    square = TIME_STEP * TIME_STEP
    kappa = square * speed_square * inverse
    return (
        kappa,
        kappa * retention[0],
        1.0 - retention[0],
        1.0 - retention[1],
        1.0 - retention[2],
        bits[0],
        bits[1],
        bits[2],
        jnp.exp(-TIME_STEP * damping),
        TIME_STEP * pairing,
        (2.0 - square * pairing) * inverse,
        (1.0 - half) * inverse,
        square * damping * inverse,
        square * inverse,
    )


def along_last(tiles, nz):
    row = lax.broadcasted_iota(jnp.int32, (nz, nz), 0)
    col = lax.broadcasted_iota(jnp.int32, (nz, nz), 1) // BLK
    along = (row == col).astype(F32).astype(BF16)
    return jnp.dot(tiles.astype(BF16), along, preferred_element_type=F32)


def tag_places(rows, lanes):
    return [
        (number * lanes, first, min(BLK, rows - first))
        for number, first in enumerate(range(0, rows, BLK))
    ]


def from_tag(tile, rows, lanes, nz):
    number = len(tag_places(rows, lanes))
    lane = lax.broadcasted_iota(jnp.int32, (nz, 2 * number * nz), 0)
    col = lax.broadcasted_iota(jnp.int32, (nz, 2 * number * nz), 1)
    along = (lane == col // nz * lanes + col % nz // BLK).astype(F32).astype(BF16)
    high = tile.astype(BF16).astype(F32)
    middle = (tile - high).astype(BF16).astype(F32)
    split = jnp.concatenate([high, middle, tile - high - middle, jnp.zeros_like(tile)], axis=0)
    wide = jnp.dot(split.astype(BF16), along, preferred_element_type=F32)
    wide = wide[:BLK] + wide[BLK : 2 * BLK] + wide[2 * BLK : 3 * BLK]
    columns = [wide[:, at * nz : (at + 1) * nz] for at in range(2 * number)]
    return [
        jnp.concatenate(columns[part * number : (part + 1) * number], axis=0) for part in range(2)
    ]


def squares(index, table):
    speed = jnp.zeros_like(index)
    for entry in range(table.shape[0]):
        speed = jnp.where(index == float(entry), table[entry], speed)
    return speed * speed


def bits_of(mask):
    mask = mask.astype(jnp.int32)
    return [((mask >> direction) & 1).astype(F32) for direction in range(3)]


def down_second(ref, lead, value, ny):
    for block in range(ny // BLK):
        rows = jnp.broadcast_to(value[block : block + 1], (BLK, value.shape[1]))
        ref[(*lead, pl.ds(block * BLK, BLK))] = rows


def fill_clock(clock, freq, start):
    steps = lax.broadcasted_iota(jnp.int32, clock.shape[1:], 0).astype(F32)
    cosine = jnp.cos(freq[0] * (start[0] + steps * TIME_STEP))
    weight = (TIME_STEP * freq[0] / math.pi) * (cosine - 0.25)
    for count in range(STEPS):
        clock[count] = jnp.broadcast_to(cosine[count : count + 1], cosine.shape)
        clock[STEPS + count] = jnp.broadcast_to(weight[count + 1 : count + 2], weight.shape)


def over_rows(ny, step):
    def one(block, carry):
        step(pl.multiple_of(block * BLK, BLK))
        return carry

    lax.fori_loop(0, ny // BLK, one, 0)


def is_even():
    return lax.axis_index("gx") % 2 == 0


def edge_planes(nx):
    return [*range(REACH), *range(nx - REACH, nx)]


def send_kernel(
    wave_in, layer_in, source_in, freq, start, table_in, index_in, mask_in,
    inside, across, coef, clock, edge, wave, layer, source,
    diff_y, diff_z, tags, tag_tiles, index, mask, table, sems,
):
    _, nx, ny, nz = wave.shape
    n_block = nx // BLK
    edges = (0, nx - REACH)
    pieces_of = [(wave_in.at[0], wave.at[0])]
    for first, length in ((0, REACH), (nx - REACH, REACH), (REACH, nx - 2 * REACH)):
        at = pl.ds(first, length)
        pieces_of += [
            (wave_in.at[1, at], wave.at[1, at]),
            (layer_in.at[:, at], layer.at[:, at]),
            (source_in.at[at], source.at[at]),
        ]
    copies = [
        pltpu.make_async_copy(one, to, sems.at[number])
        for number, (one, to) in enumerate(pieces_of)
    ]
    small = [
        pltpu.make_async_copy(one, to, sems.at[len(copies) + number])
        for number, (one, to) in enumerate(
            ((index_in, index), (mask_in, mask), (table_in, table))
        )
    ]
    for copy in small + copies:
        copy.start()
    even = is_even()
    tags[...] = jnp.zeros_like(tags)
    fill_clock(clock, freq, start)
    phase = clock[0]
    for copy in small:
        copy.wait()
    rows = n_block * TAG_ROWS
    for block in range(n_block):
        at = pl.ds(block * TAG_ROWS, index.shape[0])
        tags[0, at, : index.shape[2]] = index[:, block].astype(F32)
        tags[1, at, : mask.shape[2]] = mask[:, block].astype(F32)
    wide = along_last(tags[...].reshape(2 * rows, nz), nz)
    square = squares(wide[:rows], table)
    masks = wide[rows:]
    values = coefficients(square, bits_of(masks))
    for entry, value in enumerate(values):
        for block in range(n_block):
            down_second(coef, (entry, block), value[block * TAG_ROWS : (block + 1) * TAG_ROWS], ny)
    tag_tiles[...] = jnp.zeros_like(tag_tiles)
    places = tag_places(index.shape[0], index.shape[2])
    for side in range(2):
        block = side * (n_block - 1)
        speed = jnp.zeros(index.shape[::2], F32)
        for entry in range(table.shape[0]):
            speed = jnp.where(index[:, block] == entry, table[entry], speed)
        for part, value in enumerate((speed * speed, mask[:, block].astype(F32))):
            for lane, first, length in places:
                lane += part * len(places) * value.shape[1]
                tag_tiles[side, :length, lane : lane + value.shape[1]] = value[
                    first : first + length
                ]
    to = pl.ds(2 * REACH * ny, BLK)
    inside[to] = jnp.where(even, tag_tiles[1], tag_tiles[0])
    across[to] = jnp.where(even, tag_tiles[0], tag_tiles[1])
    copies[0].wait()
    planes = edge_planes(nx)
    slot = {plane: number for number, plane in enumerate(planes)}

    def put_y(plane, value):
        diff_y[slot[plane]] = value

    def put_z(plane, value):
        diff_z[slot[plane]] = value

    cross_diffs(planes, lambda plane: wave[0, plane], put_y, put_z, ny, nz)
    for copy in copies[1:7]:
        copy.wait()

    def step(rows):
        at = pl.ds(rows, BLK)
        sides = []
        for side in range(2):
            block = side * (n_block - 1)
            reach = range(2 * REACH) if side == 0 else range(nx - 2 * REACH, nx)
            cells = {plane: wave[0, plane, at] for plane in reach}
            values = []
            for number in range(REACH):
                plane = edges[side] + number
                new, memory, stiff = advance(
                    cells[plane],
                    wave[1, plane, at],
                    [layer[d, plane, at] for d in range(3)],
                    layer[3, plane, at],
                    source[plane, at],
                    [
                        first_diff(cells, plane),
                        diff_y[slot[plane], at],
                        diff_z[slot[plane], at],
                    ],
                    lambda entry, block=block: coef[entry, block, at],
                    phase,
                )
                for entry, value in enumerate((new, *memory, stiff)):
                    edge[side, entry, number, at] = value
                values.append((cells[plane], new))
            sides.append(values)
        for number in range(REACH):
            for part in range(2):
                to = pl.ds(pl.multiple_of((part * REACH + number) * ny + rows, BLK), BLK)
                left, right = sides[0][number][part], sides[1][number][part]
                inside[to] = jnp.where(even, right, left)
                across[to] = jnp.where(even, left, right)

    over_rows(ny, step)
    for copy in copies[7:]:
        copy.wait()


def local_kernel(
    wave, layer, source, coef, clock, edge,
    inside, across, first_out, second_out, run_out,
    fields, diff_y, diff_z,
):
    _, nx, ny, nz = wave.shape
    even = is_even()

    def put_y(plane, value):
        diff_y[plane] = value

    def put_z(plane, value):
        diff_z[plane] = value

    middle = range(REACH, nx - REACH)
    cross_diffs(middle, lambda plane: wave[0, plane], put_y, put_z, ny, nz)

    def read(entry, plane, at=slice(None)):
        if plane < REACH:
            return edge[0, entry, plane, at]
        if plane >= nx - REACH:
            return edge[1, entry, plane - nx + REACH, at]
        if entry == 0:
            return first_out[plane - REACH, at]
        return fields[entry - 1, plane - REACH, at]

    def first(rows):
        at = pl.ds(rows, BLK)
        cells = {plane: wave[0, plane, at] for plane in range(nx)}
        for plane in middle:
            new, memory, stiff = advance(
                cells[plane],
                wave[1, plane, at],
                [layer[d, plane, at] for d in range(3)],
                layer[3, plane, at],
                source[plane, at],
                [first_diff(cells, plane), diff_y[plane, at], diff_z[plane, at]],
                lambda entry, block=plane // BLK: coef[entry, block, at],
                clock[0],
            )
            first_out[plane - REACH, at] = new
            for entry, value in enumerate((*memory, stiff)):
                fields[entry, plane - REACH, at] = value

    over_rows(ny, first)
    cross_diffs(range(nx), lambda plane: read(0, plane), put_y, put_z, ny, nz)

    def second(rows):
        at = pl.ds(rows, BLK)
        cells = {plane: read(0, plane, at) for plane in range(nx)}
        values = {}
        for plane in range(nx):
            new, memory, stiff = advance(
                cells[plane],
                wave[0, plane, at],
                [read(1 + d, plane, at) for d in range(3)],
                read(4, plane, at),
                source[plane, at],
                [first_diff(cells, plane), diff_y[plane, at], diff_z[plane, at]],
                lambda entry, block=plane // BLK: coef[entry, block, at],
                clock[1],
            )
            values[plane] = new
            for entry, value in enumerate((new, *memory, stiff)):
                second_out[entry, plane, at] = value
            run_out[plane, at] = clock[STEPS] * cells[plane] + clock[STEPS + 1] * new
        for number in range(REACH):
            left, right = values[number], values[nx - REACH + number]
            inside[number, at] = jnp.where(even, right, left)
            across[number, at] = jnp.where(even, left, right)

    over_rows(ny, second)


def side_update(
    left, present, message, coef, clock, wave, running, edge, second_in, run_in,
    out_state, out_layer, out_filtered, ext, ghost,
    first, bump, push, ghost_coef, bump_y, bump_z,
):
    _, nx, ny, nz = wave.shape
    n_block = nx // BLK
    block = jnp.where(left, 0, n_block - 1)
    side = jnp.where(left, 0, 1)
    own = range(REACH)
    beyond = range(-1, -1 - REACH, -1)
    weights = [clock[STEPS + number] for number in range(2)]

    def plane_of(depth):
        return jnp.where(left, depth, nx - 1 - depth)

    def slot(depth):
        return depth if depth >= 0 else REACH - 1 - depth

    tag_at = 2 * REACH * ny
    tile = message[pl.ds(tag_at, BLK)]
    square, masks = from_tag(tile, ny // BLK, nz // BLK, nz)
    values = coefficients(square * present, bits_of(masks))
    for entry, value in enumerate(
        (
            values[KAPPA_R],
            values[Q0],
            values[KAPPA] * (1.0 - values[Q1]),
            values[KAPPA] * (1.0 - values[Q2]),
            values[AMP] - values[STIFF] * values[PAIR],
        )
    ):
        down_second(ghost_coef, (entry,), value, ny)

    def exchange(rows):
        at = pl.ds(rows, BLK)
        halo = {}
        sent = {}
        for depth in beyond:
            number = jnp.where(left, REACH + depth, -1 - depth)
            halo[depth] = message[pl.ds(pl.multiple_of(number * ny + rows, BLK), BLK)]
            number = number + REACH
            sent[depth] = message[pl.ds(pl.multiple_of(number * ny + rows, BLK), BLK)]
        mine = {depth: wave[0, plane_of(depth), at] for depth in own}
        kappa_r = coef[KAPPA_R, block, at]
        for depth in own:
            outer = outer_part(halo, depth, beyond)
            added = kappa_r * outer
            push[slot(depth), at] = outer
            bump[slot(depth), at] = added
            value = edge[side, 0, jnp.where(left, depth, REACH - 1 - depth), at] + added
            first[slot(depth), at] = value
            ext[jnp.where(left, depth, 2 * REACH - 1 - depth), at] = value
        kappa_r = ghost_coef[0, at]
        for depth in beyond:
            outer = outer_part(mine, depth, own)
            added = kappa_r * outer
            push[slot(depth), at] = outer
            bump[slot(depth), at] = added
            first[slot(depth), at] = sent[depth] + added

    over_rows(ny, exchange)

    def put_bump_y(plane, value):
        bump_y[plane] = value

    def put_bump_z(plane, value):
        bump_z[plane] = value

    cross_diffs(range(2 * REACH), lambda plane: bump[plane], put_bump_y, put_bump_z, ny, nz)

    def respond(added, true, depth, others, outer, q0, kappas, at):
        kappa_r, kappa_1, kappa_2, grown = kappas
        value = added[depth]
        rest = CENTRE_REST * value
        along = first_diff(added, depth) + outer_part(true, depth, others)
        side_y = bump_y[slot(depth), at] * (1.0 / SCALE) - rest
        side_z = bump_z[slot(depth), at] * (1.0 / SCALE) - rest
        gain = (
            grown * value + kappa_r * (along - q0 * outer) + kappa_1 * side_y + kappa_2 * side_z
        )
        return gain, along, side_y, side_z

    def second(rows):
        at = pl.ds(rows, BLK)
        true = {depth: first[slot(depth), at] for depth in (*own, *beyond)}
        added = {depth: bump[slot(depth), at] for depth in beyond}
        kappa_r, q0, kappa_1, kappa_2, grown = [ghost_coef[entry, at] for entry in range(5)]
        for depth in beyond:
            ghost[-1 - depth, at], _, _, _ = respond(
                added, true, depth, own, push[slot(depth), at], q0,
                (kappa_r, kappa_1, kappa_2, grown), at,
            )
        added = {depth: bump[slot(depth), at] for depth in own}
        kappa_r, kappa = coef[KAPPA_R, block, at], coef[KAPPA, block, at]
        q0, q1, q2 = [coef[entry, block, at] for entry in (Q0, Q1, Q2)]
        pair = coef[PAIR, block, at]
        kappas = (
            kappa_r,
            kappa * (1.0 - q1),
            kappa * (1.0 - q2),
            coef[AMP, block, at] - coef[STIFF, block, at] * pair,
        )
        for depth in own:
            plane = plane_of(depth)
            outer = push[slot(depth), at]
            gain, along, side_y, side_z = respond(
                added, true, depth, beyond, outer, q0, kappas, at
            )
            out_state[1, plane, at] = second_in[0, plane, at] + gain
            out_layer[0, plane, at] = second_in[1, plane, at] + q0 * (
                along + (1.0 - q0) * outer
            )
            out_layer[1, plane, at] = second_in[2, plane, at] + q1 * side_y
            out_layer[2, plane, at] = second_in[3, plane, at] + q2 * side_z
            out_layer[3, plane, at] = second_in[4, plane, at] + pair * added[depth]
            out_filtered[plane, at] = (
                running[plane, at]
                + run_in[plane, at]
                + weights[0] * added[depth]
                + weights[1] * gain
            )
        for depth in range(REACH, 2 * REACH):
            plane = plane_of(depth)
            along = outer_part(added, depth, own)
            gain = kappa_r * along
            out_state[1, plane, at] = second_in[0, plane, at] + gain
            out_layer[0, plane, at] = second_in[1, plane, at] + q0 * along
            out_filtered[plane, at] = running[plane, at] + run_in[plane, at] + weights[1] * gain

    over_rows(ny, second)


def inside_kernel(
    inside, coef, clock, wave, running, edge, second_in, run_in,
    out_state, out_layer, out_filtered, ext, ghost,
    *scratch,
):
    side_update(
        jnp.logical_not(is_even()), 1.0, inside, coef, clock, wave, running, edge, second_in,
        run_in, out_state, out_layer, out_filtered, ext, ghost, *scratch,
    )


def joint_kernel(
    across, coef, clock, wave, forcing, running, edge, first_in, second_in, run_in,
    state_in, layer_in, filtered_in, ext_in,
    out_state, out_layer, out_filtered, ext, ghost, partial,
    diff_y, diff_z, *scratch,
):
    del state_in, layer_in, filtered_in, ext_in
    _, nx, ny, nz = wave.shape
    count = lax.axis_size("gx")
    place = lax.axis_index("gx")
    even = is_even()
    weights = [clock[STEPS + number] for number in range(STEPS)]
    outermost = jnp.logical_or(place == 0, place == count - 1)
    side_update(
        even, jnp.where(outermost, 0.0, 1.0).astype(F32), across, coef, clock, wave, running,
        edge, second_in, run_in, out_state, out_layer, out_filtered, ext, ghost, *scratch,
    )
    if nx > 4 * REACH:

        def between(rows):
            at = pl.ds(rows, BLK)
            for plane in range(2 * REACH, nx - 2 * REACH):
                out_state[1, plane, at] = second_in[0, plane, at]
                out_layer[0, plane, at] = second_in[1, plane, at]
                out_filtered[plane, at] = running[plane, at] + run_in[plane, at]

        over_rows(ny, between)

    def put_y(plane, value):
        diff_y[plane] = value

    def put_z(plane, value):
        diff_z[plane] = value

    cross_diffs(range(nx), lambda plane: out_state[1, plane], put_y, put_z, ny, nz)
    partial[...] = jnp.zeros_like(partial)

    def third(rows):
        at = pl.ds(rows, BLK)
        cells = {plane: out_state[1, plane, at] for plane in range(nx)}
        total = partial[...]
        for plane in range(nx):
            at_edge = plane < REACH or plane >= nx - REACH
            if at_edge:
                previous = ext[plane if plane < REACH else plane - nx + 2 * REACH, at]
                fields = [out_layer[d, plane, at] for d in range(4)]
            else:
                previous = first_in[plane - REACH, at]
                fields = [out_layer[0, plane, at]]
                fields += [second_in[1 + d, plane, at] for d in range(1, 4)]
            value, memory, stiff = advance(
                cells[plane],
                previous,
                fields[:3],
                fields[3],
                forcing[plane, at],
                [first_diff(cells, plane), diff_y[plane, at], diff_z[plane, at]],
                lambda entry, block=plane // BLK: coef[entry, block, at],
                clock[2],
            )
            done = out_filtered[plane, at] + weights[2] * value
            for d in range(3):
                out_layer[d, plane, at] = memory[d]
            out_layer[3, plane, at] = stiff
            out_state[0, plane, at] = value
            out_filtered[plane, at] = done
            if not at_edge:
                total = total + done * done
        partial[...] = total

    over_rows(ny, third)


def finish_kernel(
    coef, clock, inside, across, across_late, ghost_inside, ghost_across, partial,
    state_in, layer_in, filtered_in,
    out_state, out_layer, out_filtered, total_out,
):
    _, nx, ny, _ = state_in.shape
    n_block = nx // BLK
    even = is_even()
    weight = clock[2 * STEPS - 1]
    total_out[...] = partial[...]
    ghosts = (range(-REACH, 0), range(nx, nx + REACH))
    owned = (range(REACH), range(nx - REACH, nx))

    def step(rows):
        at = pl.ds(rows, BLK)
        halo = {}
        for number in range(REACH):
            one = inside[number, at]
            two = across[number, at] + across_late[number, at]
            left = jnp.where(even, two, one)
            right = jnp.where(even, one, two)
            one, two = ghost_inside[REACH - 1 - number, at], ghost_across[REACH - 1 - number, at]
            halo[-REACH + number] = left + jnp.where(even, two, one)
            one, two = ghost_inside[number, at], ghost_across[number, at]
            halo[nx + number] = right + jnp.where(even, one, two)
        total = total_out[...]
        for side in range(2):
            block = side * (n_block - 1)
            kappa_r, q0 = coef[KAPPA_R, block, at], coef[Q0, block, at]
            for plane in owned[side]:
                outer = outer_part(halo, plane, ghosts[side])
                added = kappa_r * outer
                out_state[0, plane, at] = state_in[0, plane, at] + added
                out_layer[0, plane, at] = layer_in[0, plane, at] + q0 * outer
                done = filtered_in[plane, at] + weight * added
                out_filtered[plane, at] = done
                total = total + done * done
        total_out[...] = total

    over_rows(ny, step)


def store_kernel(parts, values, *refs):
    n = len(parts)
    arrays, outs, values_out, sems = refs[:n], refs[-n - 2 : -2], refs[-2], refs[-1]
    copies = [
        pltpu.make_async_copy(
            *((array, out) if at is None else (array.at[at], out.at[at])), sems.at[number]
        )
        for number, (at, array, out) in enumerate(zip(parts, arrays, outs))
    ]
    for copy in copies:
        copy.start()
    values_out[...] = values[...]
    for copy in copies:
        copy.wait()


def norm_kernel(cells, values, got, norm):
    total = jnp.sum(values[...] + got[...], axis=1, keepdims=True)
    total = jnp.sum(total, axis=0, keepdims=True)
    norm[...] = jnp.sqrt(total / cells + 1e-06)


SCALAR = pl.BlockSpec(memory_space=pltpu.SMEM)
HBM = pl.BlockSpec(memory_space=pltpu.HBM)
VEC = pl.BlockSpec(memory_space=pltpu.VMEM)


def held(*shape):
    return pltpu.VMEM(shape, F32)


def in_vmem(*arrays):
    return [pltpu.with_memory_space_constraint(array, pltpu.VMEM) for array in arrays]


def in_hbm(*arrays):
    return [pltpu.with_memory_space_constraint(array, pltpu.HBM) for array in arrays]


def call(kernel, name, in_specs, out_shape, out_specs, scratch, operands, micros, aliases=None):
    return pl.pallas_call(
        kernel,
        name=name,
        in_specs=in_specs,
        out_shape=out_shape,
        out_specs=out_specs,
        scratch_shapes=scratch,
        input_output_aliases=aliases or {},
        compiler_params=pltpu.CompilerParams(vmem_limit_bytes=VMEM_LIMIT),
        cost_estimate=pl.CostEstimate(
            flops=0, bytes_accessed=int(micros * 3.6e6), transcendentals=0
        ),
    )(*operands)


def swap_pairs(count):
    inside = [(i, i ^ 1) for i in range(count)]
    across = []
    for i in range(1, count - 1, 2):
        across += [(i, i + 1), (i + 1, i)]
    return inside, across


def halves(pairs):
    return [[pair for pair in pairs if min(pair) % 4 == first] for first in (1, 3)]


def store(values, parts, arrays, begun=()):
    n = len(arrays)
    outs = [jax.ShapeDtypeStruct(array.shape, F32) for array in arrays]
    *stored, values = call(
        functools.partial(store_kernel, parts),
        "store",
        [VEC] * (1 + n) + [HBM] * len(begun),
        [*outs, held(*values.shape)],
        [HBM] * n + [VEC],
        [pltpu.SemaphoreType.DMA((n,))],
        (*in_vmem(values, *arrays), *begun),
        1,
        {1 + n + number: n - len(begun) + number for number in range(len(begun))},
    )
    return values, stored


def norm_and_stores(values, state, layer, running, axis):
    count = lax.axis_size(axis)
    half = layer.shape[0] // 2
    stored = {}

    def first(values):
        values, (stored["state"],) = store(values, [None], [state])
        return values

    def second(values):
        values, (stored["layer"],) = store(values, [pl.ds(0, half)], [layer])
        return values

    def third(values):
        values, (stored["running"], stored["layer"]) = store(
            values, [None, pl.ds(half, half)], [running, layer], [stored["layer"]]
        )
        return values

    waiting = [first, second, third]
    hops = [] if count & (count - 1) else [1 << k for k in range(count.bit_length() - 1)]
    for number, hop in enumerate(hops):
        got = lax.ppermute(values, axis, [(i, i ^ hop) for i in range(count)])
        if waiting and number >= 1:
            values = waiting.pop(0)(values)
        if hop != hops[-1]:
            values = values + got
    for step in waiting:
        values = step(values)
    if not hops:
        values, got = lax.psum(values, axis), jnp.zeros_like(values)
    norm = call(
        functools.partial(norm_kernel, float(running.size * count)),
        "norm",
        [VEC] * 2,
        jax.ShapeDtypeStruct((1, 1), F32),
        VEC,
        [],
        in_vmem(values, got),
        1,
    )
    return norm.reshape(1), stored["state"], stored["layer"], stored["running"]


def body(
    wave_state, layer_fields, source, filtered, frequency, start_time, speed_table, speed_index,
    pml_mask,
):
    _, nx, ny, nz = wave_state.shape
    n_block = nx // BLK
    count = lax.axis_size("gx")
    pair_inside, pair_across = swap_pairs(count)
    brick = (nx, ny, nz)
    strip = (REACH, ny, nz)
    message = (2 * REACH * ny + BLK, nz)
    dma = pltpu.SemaphoreType.DMA
    vec = lambda *shape: pltpu.VMEM(shape, F32)

    blocks = (speed_index.shape[1], n_block, speed_index.shape[2])
    index, mask = in_hbm(*(jnp.transpose(one, (1, 0, 2)) for one in (speed_index, pml_mask)))

    inside, across, coef, clock, edge, wave, layer, forcing = call(
        send_kernel,
        "strips",
        [HBM] * 3 + [SCALAR] * 2 + [HBM] * 3,
        [
            held(*message), held(*message), held(N_COEF, n_block, ny, nz),
            held(2 * STEPS, BLK, nz), held(2, 5, *strip), held(*wave_state.shape),
            held(*layer_fields.shape), held(*brick),
        ],
        [VEC] * 8,
        [
            vec(2 * REACH, ny, nz),
            vec(2 * REACH, ny, nz),
            vec(2, n_block * TAG_ROWS, nz),
            vec(2, BLK, nz),
            pltpu.VMEM(blocks, jnp.int32),
            pltpu.VMEM(blocks, jnp.int32),
            pltpu.SMEM(speed_table.shape, F32),
            dma((13,)),
        ],
        (
            *in_hbm(wave_state, layer_fields, source), frequency, start_time,
            *in_hbm(speed_table), index, mask,
        ),
        2.5,
    )
    got_inside = lax.ppermute(inside, "gx", pair_inside)
    got_across = lax.ppermute(across, "gx", pair_across)
    coef, clock, edge, wave, layer, forcing, running = in_vmem(
        coef, clock, edge, wave, layer, forcing, filtered
    )

    later_inside, later_across, first, second, run = call(
        local_kernel,
        "local",
        [VEC] * 6,
        [
            held(*strip), held(*strip), held(nx - 2 * REACH, ny, nz), held(5, *brick),
            held(*brick),
        ],
        [VEC] * 5,
        [vec(4, nx - 2 * REACH, ny, nz), vec(*brick), vec(*brick)],
        (wave, layer, forcing, coef, clock, edge),
        4,
    )
    last_inside = lax.ppermute(later_inside, "gx", pair_inside)
    early_pairs, late_pairs = halves(pair_across)
    last_across = lax.ppermute(later_across, "gx", early_pairs)
    out_types = [
        held(*wave_state.shape), held(*layer_fields.shape), held(*filtered.shape)
    ]
    edge_type = held(2 * REACH, ny, nz)
    side_scratch = [vec(2 * REACH, ny, nz)] * 3 + [vec(5, ny, nz)] + [vec(2 * REACH, ny, nz)] * 2
    later_across, got_inside = lax.optimization_barrier((later_across, got_inside))
    last_late = lax.ppermute(later_across, "gx", late_pairs)
    first, second, run = in_vmem(first, second, run)
    next_state, next_layer, next_filtered, ext, ghost_inside = call(
        inside_kernel,
        "inner_half",
        [VEC] * 8,
        out_types + [edge_type, held(*strip)],
        [VEC] * 5,
        side_scratch,
        (*in_vmem(got_inside), coef, clock, wave, running, edge, second, run),
        1.5,
    )
    next_state, next_layer, next_filtered, ext, ghost_across, partial = call(
        joint_kernel,
        "joint",
        [VEC] * 14,
        out_types + [edge_type, held(*strip), held(BLK, nz)],
        [VEC] * 6,
        [vec(*brick), vec(*brick), *side_scratch],
        (
            *in_vmem(got_across), coef, clock, wave, forcing, running, edge, first, second, run,
            *in_vmem(next_state, next_layer, next_filtered, ext),
        ),
        5,
        {10: 0, 11: 1, 12: 2, 13: 3},
    )
    next_state, next_layer, next_filtered, total = call(
        finish_kernel,
        "finish",
        [VEC] * 11,
        out_types + [held(BLK, nz)],
        [VEC] * 4,
        [],
        (
            coef, clock,
            *in_vmem(
                last_inside, last_across, last_late, ghost_inside, ghost_across, partial,
                next_state, next_layer, next_filtered,
            ),
        ),
        1,
        {8: 0, 9: 1, 10: 2},
    )
    filter_norm, next_state, next_layer, next_filtered = norm_and_stores(
        total, next_state, next_layer, next_filtered, "gx"
    )
    return next_state, next_layer, next_filtered, filter_norm


def solution(mesh):
    placed = (
        P("grp", "gx", None, None),
        P("grp", "gx", None, None),
        P(("grp", "gx"), None, None),
        P(("grp", "gx"), None, None),
        P("grp"),
        P("grp"),
        P(),
        P("gx", None, None),
        P("gx", None, None),
    )
    return jax.shard_map(
        body,
        mesh=mesh,
        in_specs=placed,
        out_specs=(
            P("grp", "gx", None, None),
            P("grp", "gx", None, None),
            P(("grp", "gx"), None, None),
            P("grp"),
        ),
        check_vma=False,
    )
```

```python
import functools
import math

import jax
import jax.numpy as jnp
from jax import lax
from jax.experimental import pallas as pl
from jax.experimental.pallas import tpu as pltpu
from jax.sharding import PartitionSpec as P

F32 = jnp.float32
BF16 = jnp.bfloat16
STEPS = 3
BLK = 8
REACH = 4
TIME_STEP = 0.25
DAMP_PEAK = 1.5
STENCIL = (-205.0 / 72.0, 8.0 / 5.0, -1.0 / 5.0, 8.0 / 315.0, -1.0 / 560.0)
SCALE = 5040.0
WHOLE = (-14336.0, 8064.0, -1008.0, 128.0, -9.0)
CENTRE_REST = 14.0 / SCALE
TAG_ROWS = 16
KAPPA, KAPPA_R, Q0, Q1, Q2, B0, B1, B2, DECAY, PAIR, AMP, BACK, STIFF, FORCE, PUSH = range(15)
N_COEF = 14
VMEM_LIMIT = 30 * 1024 * 1024


def band(rows, cols, row_period, col_period):
    row = lax.broadcasted_iota(jnp.int32, (rows, cols), 0) % row_period
    col = lax.broadcasted_iota(jnp.int32, (rows, cols), 1) % col_period
    apart = jnp.abs(row - col)
    out = jnp.zeros((rows, cols), F32)
    for offset, value in enumerate(WHOLE):
        out = jnp.where(apart == offset, value, out)
    return out.astype(BF16)


def pieces(cells):
    high = cells.astype(BF16)
    return high, (cells - high.astype(F32)).astype(BF16)


def cross_diffs(planes, read, write_y, write_z, ny, nz):
    mat_y = band(ny, 2 * ny, ny, ny)
    mat_z = band(2 * nz, nz, nz, nz)
    for one, two in zip(planes[0::2], planes[1::2]):
        high_one, low_one = pieces(read(one))
        high_two, low_two = pieces(read(two))
        upper = jnp.concatenate([high_one, high_two], axis=1)
        lower = jnp.concatenate([low_one, low_two], axis=1)
        diff_y = jnp.dot(
            mat_y, jnp.concatenate([upper, lower], axis=0), preferred_element_type=F32
        )
        write_y(one, diff_y[:, :nz])
        write_y(two, diff_y[:, nz:])
        left = jnp.concatenate([high_one, low_one], axis=1)
        right = jnp.concatenate([high_two, low_two], axis=1)
        diff_z = jnp.dot(
            jnp.concatenate([left, right], axis=0), mat_z, preferred_element_type=F32
        )
        write_z(one, diff_z[:ny])
        write_z(two, diff_z[ny:])


def first_diff(cells, at):
    total = STENCIL[0] * cells[at]
    for offset in range(1, REACH + 1):
        above, below = cells.get(at + offset), cells.get(at - offset)
        if above is not None and below is not None:
            total = total + STENCIL[offset] * (above + below)
        elif above is not None:
            total = total + STENCIL[offset] * above
        elif below is not None:
            total = total + STENCIL[offset] * below
    return total


def outer_part(cells, at, positions):
    total = None
    for position in positions:
        offset = abs(position - at)
        if offset <= REACH:
            term = STENCIL[offset] * cells[position]
            total = term if total is None else total + term
    return total


def advance(cells, previous, memory, stiff, forcing, diffs, co):
    rest = CENTRE_REST * cells
    diffs = [diffs[0], diffs[1] * (1.0 / SCALE) - rest, diffs[2] * (1.0 / SCALE) - rest]
    memory = [m + co(Q0 + d) * (diffs[d] - m) for d, m in enumerate(memory)]
    inner = sum(diffs[d] - co(B0 + d) * memory[d] for d in range(3))
    stiff = co(DECAY) * stiff + co(PAIR) * cells
    new = (
        co(AMP) * cells
        - co(BACK) * previous
        + co(KAPPA) * inner
        - co(STIFF) * stiff
        - co(PUSH) * forcing
    )
    return new, memory, stiff


def loaded(coef, block, at, phase):
    have = {}

    def get(entry):
        if entry not in have:
            if entry == PUSH:
                have[entry] = coef[FORCE, block, at] * phase
            else:
                have[entry] = coef[entry, block, at]
        return have[entry]

    return get


def coefficients(speed_square, bits):
    rates = [DAMP_PEAK * bit for bit in bits]
    damping = rates[0] + rates[1] + rates[2]
    pairing = rates[0] * rates[1] + rates[1] * rates[2] + rates[2] * rates[0]
    retention = [jnp.exp(-TIME_STEP * rate) for rate in rates]
    half = 0.5 * TIME_STEP * damping
    inverse = 1.0 / (1.0 + half)
    square = TIME_STEP * TIME_STEP
    kappa = square * speed_square * inverse
    return (
        kappa,
        kappa * retention[0],
        1.0 - retention[0],
        1.0 - retention[1],
        1.0 - retention[2],
        bits[0],
        bits[1],
        bits[2],
        jnp.exp(-TIME_STEP * damping),
        TIME_STEP * pairing,
        (2.0 - square * pairing) * inverse,
        (1.0 - half) * inverse,
        square * damping * inverse,
        square * inverse,
    )


def along_last(tiles, nz):
    row = lax.broadcasted_iota(jnp.int32, (nz, nz), 0)
    col = lax.broadcasted_iota(jnp.int32, (nz, nz), 1) // BLK
    along = (row == col).astype(F32).astype(BF16)
    return jnp.dot(tiles.astype(BF16), along, preferred_element_type=F32)


def tag_places(rows, lanes):
    return [
        (number * lanes, first, min(BLK, rows - first))
        for number, first in enumerate(range(0, rows, BLK))
    ]


def from_tag(tile, rows, lanes, nz):
    number = len(tag_places(rows, lanes))
    lane = lax.broadcasted_iota(jnp.int32, (nz, 2 * number * nz), 0)
    col = lax.broadcasted_iota(jnp.int32, (nz, 2 * number * nz), 1)
    along = (lane == col // nz * lanes + col % nz // BLK).astype(F32).astype(BF16)
    high = tile.astype(BF16).astype(F32)
    middle = (tile - high).astype(BF16).astype(F32)
    split = jnp.concatenate([high, middle, tile - high - middle, jnp.zeros_like(tile)], axis=0)
    wide = jnp.dot(split.astype(BF16), along, preferred_element_type=F32)
    wide = wide[:BLK] + wide[BLK : 2 * BLK] + wide[2 * BLK : 3 * BLK]
    columns = [wide[:, at * nz : (at + 1) * nz] for at in range(2 * number)]
    return [
        jnp.concatenate(columns[part * number : (part + 1) * number], axis=0) for part in range(2)
    ]


def squares(index, table):
    speed = jnp.zeros_like(index)
    for entry in range(table.shape[0]):
        speed = jnp.where(index == float(entry), table[entry], speed)
    return speed * speed


def bits_of(mask):
    mask = mask.astype(jnp.int32)
    return [((mask >> direction) & 1).astype(F32) for direction in range(3)]


def down_second(ref, lead, value, ny):
    for block in range(ny // BLK):
        rows = jnp.broadcast_to(value[block : block + 1], (BLK, value.shape[1]))
        ref[(*lead, pl.ds(block * BLK, BLK))] = rows


def fill_clock(clock, freq, start):
    steps = lax.broadcasted_iota(jnp.int32, clock.shape[1:], 0).astype(F32)
    cosine = jnp.cos(freq[0] * (start[0] + steps * TIME_STEP))
    weight = (TIME_STEP * freq[0] / math.pi) * (cosine - 0.25)
    for count in range(STEPS):
        clock[count] = jnp.broadcast_to(cosine[count : count + 1], cosine.shape)
        clock[STEPS + count] = jnp.broadcast_to(weight[count + 1 : count + 2], weight.shape)


def over_rows(ny, step):
    def one(block, carry):
        step(pl.multiple_of(block * BLK, BLK))
        return carry

    lax.fori_loop(0, ny // BLK, one, 0, unroll=2)


def is_even():
    return lax.axis_index("gx") % 2 == 0


def edge_planes(nx):
    return [*range(REACH), *range(nx - REACH, nx)]


def send_kernel(
    wave_in, layer_in, source_in, freq, start, table_in, index_in, mask_in,
    inside, across, coef, clock, edge, wave, layer, source,
    diff_y, diff_z, tags, tag_tiles, index, mask, table, sems,
):
    _, nx, ny, nz = wave.shape
    n_block = nx // BLK
    edges = (0, nx - REACH)
    pieces_of = [(wave_in.at[0], wave.at[0])]
    for first, length in ((0, REACH), (nx - REACH, REACH), (REACH, nx - 2 * REACH)):
        at = pl.ds(first, length)
        pieces_of += [
            (wave_in.at[1, at], wave.at[1, at]),
            (layer_in.at[:, at], layer.at[:, at]),
            (source_in.at[at], source.at[at]),
        ]
    copies = [
        pltpu.make_async_copy(one, to, sems.at[number])
        for number, (one, to) in enumerate(pieces_of)
    ]
    small = [
        pltpu.make_async_copy(one, to, sems.at[len(copies) + number])
        for number, (one, to) in enumerate(
            ((index_in, index), (mask_in, mask), (table_in, table))
        )
    ]
    for copy in small + copies:
        copy.start()
    even = is_even()
    tags[...] = jnp.zeros_like(tags)
    fill_clock(clock, freq, start)
    phase = clock[0]
    for copy in small:
        copy.wait()
    rows = n_block * TAG_ROWS
    for block in range(n_block):
        at = pl.ds(block * TAG_ROWS, index.shape[0])
        tags[0, at, : index.shape[2]] = index[:, block].astype(F32)
        tags[1, at, : mask.shape[2]] = mask[:, block].astype(F32)
    wide = along_last(tags[...].reshape(2 * rows, nz), nz)
    square = squares(wide[:rows], table)
    masks = wide[rows:]
    values = coefficients(square, bits_of(masks))
    for entry, value in enumerate(values):
        for block in range(n_block):
            down_second(coef, (entry, block), value[block * TAG_ROWS : (block + 1) * TAG_ROWS], ny)
    tag_tiles[...] = jnp.zeros_like(tag_tiles)
    places = tag_places(index.shape[0], index.shape[2])
    for side in range(2):
        block = side * (n_block - 1)
        speed = jnp.zeros(index.shape[::2], F32)
        for entry in range(table.shape[0]):
            speed = jnp.where(index[:, block] == entry, table[entry], speed)
        for part, value in enumerate((speed * speed, mask[:, block].astype(F32))):
            for lane, first, length in places:
                lane += part * len(places) * value.shape[1]
                tag_tiles[side, :length, lane : lane + value.shape[1]] = value[
                    first : first + length
                ]
    to = pl.ds(2 * REACH * ny, BLK)
    inside[to] = jnp.where(even, tag_tiles[1], tag_tiles[0])
    across[to] = jnp.where(even, tag_tiles[0], tag_tiles[1])
    copies[0].wait()
    planes = edge_planes(nx)
    slot = {plane: number for number, plane in enumerate(planes)}

    def put_y(plane, value):
        diff_y[slot[plane]] = value

    def put_z(plane, value):
        diff_z[slot[plane]] = value

    cross_diffs(planes, lambda plane: wave[0, plane], put_y, put_z, ny, nz)
    for copy in copies[1:7]:
        copy.wait()

    def step(rows):
        at = pl.ds(rows, BLK)
        sides = []
        for side in range(2):
            block = side * (n_block - 1)
            reach = range(2 * REACH) if side == 0 else range(nx - 2 * REACH, nx)
            cells = {plane: wave[0, plane, at] for plane in reach}
            values = []
            co = loaded(coef, block, at, phase)
            for number in range(REACH):
                plane = edges[side] + number
                new, memory, stiff = advance(
                    cells[plane],
                    wave[1, plane, at],
                    [layer[d, plane, at] for d in range(3)],
                    layer[3, plane, at],
                    source[plane, at],
                    [
                        first_diff(cells, plane),
                        diff_y[slot[plane], at],
                        diff_z[slot[plane], at],
                    ],
                    co,
                )
                for entry, value in enumerate((new, *memory, stiff)):
                    edge[side, entry, number, at] = value
                values.append((cells[plane], new))
            sides.append(values)
        for number in range(REACH):
            for part in range(2):
                to = pl.ds(pl.multiple_of((part * REACH + number) * ny + rows, BLK), BLK)
                left, right = sides[0][number][part], sides[1][number][part]
                inside[to] = jnp.where(even, right, left)
                across[to] = jnp.where(even, left, right)

    over_rows(ny, step)
    for copy in copies[7:]:
        copy.wait()


def local_kernel(
    wave, layer, source, coef, clock, edge,
    inside, across, first_out, second_out, run_out,
    fields, diff_y, diff_z,
):
    _, nx, ny, nz = wave.shape
    even = is_even()

    def put_y(plane, value):
        diff_y[plane] = value

    def put_z(plane, value):
        diff_z[plane] = value

    middle = range(REACH, nx - REACH)
    cross_diffs(middle, lambda plane: wave[0, plane], put_y, put_z, ny, nz)

    def read(entry, plane, at=slice(None)):
        if plane < REACH:
            return edge[0, entry, plane, at]
        if plane >= nx - REACH:
            return edge[1, entry, plane - nx + REACH, at]
        if entry == 0:
            return first_out[plane - REACH, at]
        return fields[entry - 1, plane - REACH, at]

    def first(rows):
        at = pl.ds(rows, BLK)
        co = [loaded(coef, block, at, clock[0]) for block in range(nx // BLK)]
        cells = {plane: wave[0, plane, at] for plane in range(nx)}
        for plane in middle:
            new, memory, stiff = advance(
                cells[plane],
                wave[1, plane, at],
                [layer[d, plane, at] for d in range(3)],
                layer[3, plane, at],
                source[plane, at],
                [first_diff(cells, plane), diff_y[plane, at], diff_z[plane, at]],
                co[plane // BLK],
            )
            first_out[plane - REACH, at] = new
            for entry, value in enumerate((*memory, stiff)):
                fields[entry, plane - REACH, at] = value

    over_rows(ny, first)
    cross_diffs(range(nx), lambda plane: read(0, plane), put_y, put_z, ny, nz)

    def second(rows):
        at = pl.ds(rows, BLK)
        co = [loaded(coef, block, at, clock[1]) for block in range(nx // BLK)]
        cells = {plane: read(0, plane, at) for plane in range(nx)}
        values = {}
        for plane in range(nx):
            new, memory, stiff = advance(
                cells[plane],
                wave[0, plane, at],
                [read(1 + d, plane, at) for d in range(3)],
                read(4, plane, at),
                source[plane, at],
                [first_diff(cells, plane), diff_y[plane, at], diff_z[plane, at]],
                co[plane // BLK],
            )
            values[plane] = new
            for entry, value in enumerate((new, *memory, stiff)):
                second_out[entry, plane, at] = value
            run_out[plane, at] = clock[STEPS] * cells[plane] + clock[STEPS + 1] * new
        for number in range(REACH):
            left, right = values[number], values[nx - REACH + number]
            inside[number, at] = jnp.where(even, right, left)
            across[number, at] = jnp.where(even, left, right)

    over_rows(ny, second)


def side_update(
    left, present, message, coef, clock, wave, running, edge, second_in, run_in,
    out_state, out_layer, out_filtered, ext, ghost,
    first, bump, push, ghost_coef, bump_y, bump_z,
):
    _, nx, ny, nz = wave.shape
    n_block = nx // BLK
    block = jnp.where(left, 0, n_block - 1)
    side = jnp.where(left, 0, 1)
    own = range(REACH)
    beyond = range(-1, -1 - REACH, -1)
    weights = [clock[STEPS + number] for number in range(2)]

    def plane_of(depth):
        return jnp.where(left, depth, nx - 1 - depth)

    def slot(depth):
        return depth if depth >= 0 else REACH - 1 - depth

    tag_at = 2 * REACH * ny
    tile = message[pl.ds(tag_at, BLK)]
    square, masks = from_tag(tile, ny // BLK, nz // BLK, nz)
    values = coefficients(square * present, bits_of(masks))
    for entry, value in enumerate(
        (
            values[KAPPA_R],
            values[Q0],
            values[KAPPA] * (1.0 - values[Q1]),
            values[KAPPA] * (1.0 - values[Q2]),
            values[AMP] - values[STIFF] * values[PAIR],
        )
    ):
        down_second(ghost_coef, (entry,), value, ny)

    def exchange(rows):
        at = pl.ds(rows, BLK)
        halo = {}
        sent = {}
        for depth in beyond:
            number = jnp.where(left, REACH + depth, -1 - depth)
            halo[depth] = message[pl.ds(pl.multiple_of(number * ny + rows, BLK), BLK)]
            number = number + REACH
            sent[depth] = message[pl.ds(pl.multiple_of(number * ny + rows, BLK), BLK)]
        mine = {depth: wave[0, plane_of(depth), at] for depth in own}
        kappa_r = coef[KAPPA_R, block, at]
        for depth in own:
            outer = outer_part(halo, depth, beyond)
            added = kappa_r * outer
            push[slot(depth), at] = outer
            bump[slot(depth), at] = added
            value = edge[side, 0, jnp.where(left, depth, REACH - 1 - depth), at] + added
            first[slot(depth), at] = value
            ext[jnp.where(left, depth, 2 * REACH - 1 - depth), at] = value
        kappa_r = ghost_coef[0, at]
        for depth in beyond:
            outer = outer_part(mine, depth, own)
            added = kappa_r * outer
            push[slot(depth), at] = outer
            bump[slot(depth), at] = added
            first[slot(depth), at] = sent[depth] + added

    over_rows(ny, exchange)

    def put_bump_y(plane, value):
        bump_y[plane] = value

    def put_bump_z(plane, value):
        bump_z[plane] = value

    cross_diffs(range(2 * REACH), lambda plane: bump[plane], put_bump_y, put_bump_z, ny, nz)

    def respond(added, true, depth, others, outer, q0, kappas, at):
        kappa_r, kappa_1, kappa_2, grown = kappas
        value = added[depth]
        rest = CENTRE_REST * value
        along = first_diff(added, depth) + outer_part(true, depth, others)
        side_y = bump_y[slot(depth), at] * (1.0 / SCALE) - rest
        side_z = bump_z[slot(depth), at] * (1.0 / SCALE) - rest
        gain = (
            grown * value + kappa_r * (along - q0 * outer) + kappa_1 * side_y + kappa_2 * side_z
        )
        return gain, along, side_y, side_z

    def second(rows):
        at = pl.ds(rows, BLK)
        true = {depth: first[slot(depth), at] for depth in (*own, *beyond)}
        added = {depth: bump[slot(depth), at] for depth in beyond}
        kappa_r, q0, kappa_1, kappa_2, grown = [ghost_coef[entry, at] for entry in range(5)]
        for depth in beyond:
            ghost[-1 - depth, at], _, _, _ = respond(
                added, true, depth, own, push[slot(depth), at], q0,
                (kappa_r, kappa_1, kappa_2, grown), at,
            )
        added = {depth: bump[slot(depth), at] for depth in own}
        kappa_r, kappa = coef[KAPPA_R, block, at], coef[KAPPA, block, at]
        q0, q1, q2 = [coef[entry, block, at] for entry in (Q0, Q1, Q2)]
        pair = coef[PAIR, block, at]
        kappas = (
            kappa_r,
            kappa * (1.0 - q1),
            kappa * (1.0 - q2),
            coef[AMP, block, at] - coef[STIFF, block, at] * pair,
        )
        for depth in own:
            plane = plane_of(depth)
            outer = push[slot(depth), at]
            gain, along, side_y, side_z = respond(
                added, true, depth, beyond, outer, q0, kappas, at
            )
            out_state[1, plane, at] = second_in[0, plane, at] + gain
            out_layer[0, plane, at] = second_in[1, plane, at] + q0 * (
                along + (1.0 - q0) * outer
            )
            out_layer[1, plane, at] = second_in[2, plane, at] + q1 * side_y
            out_layer[2, plane, at] = second_in[3, plane, at] + q2 * side_z
            out_layer[3, plane, at] = second_in[4, plane, at] + pair * added[depth]
            out_filtered[plane, at] = (
                running[plane, at]
                + run_in[plane, at]
                + weights[0] * added[depth]
                + weights[1] * gain
            )
        for depth in range(REACH, 2 * REACH):
            plane = plane_of(depth)
            along = outer_part(added, depth, own)
            gain = kappa_r * along
            out_state[1, plane, at] = second_in[0, plane, at] + gain
            out_layer[0, plane, at] = second_in[1, plane, at] + q0 * along
            out_filtered[plane, at] = running[plane, at] + run_in[plane, at] + weights[1] * gain

    over_rows(ny, second)


def inside_kernel(
    inside, coef, clock, wave, running, edge, second_in, run_in,
    out_state, out_layer, out_filtered, ext, ghost,
    *scratch,
):
    side_update(
        jnp.logical_not(is_even()), 1.0, inside, coef, clock, wave, running, edge, second_in,
        run_in, out_state, out_layer, out_filtered, ext, ghost, *scratch,
    )


def joint_kernel(
    across, coef, clock, wave, forcing, running, edge, first_in, second_in, run_in,
    state_in, layer_in, filtered_in, ext_in,
    out_state, out_layer, out_filtered, ext, ghost, partial,
    diff_y, diff_z, *scratch,
):
    del state_in, layer_in, filtered_in, ext_in
    _, nx, ny, nz = wave.shape
    count = lax.axis_size("gx")
    place = lax.axis_index("gx")
    even = is_even()
    weights = [clock[STEPS + number] for number in range(STEPS)]
    outermost = jnp.logical_or(place == 0, place == count - 1)
    side_update(
        even, jnp.where(outermost, 0.0, 1.0).astype(F32), across, coef, clock, wave, running,
        edge, second_in, run_in, out_state, out_layer, out_filtered, ext, ghost, *scratch,
    )
    if nx > 4 * REACH:

        def between(rows):
            at = pl.ds(rows, BLK)
            for plane in range(2 * REACH, nx - 2 * REACH):
                out_state[1, plane, at] = second_in[0, plane, at]
                out_layer[0, plane, at] = second_in[1, plane, at]
                out_filtered[plane, at] = running[plane, at] + run_in[plane, at]

        over_rows(ny, between)

    def put_y(plane, value):
        diff_y[plane] = value

    def put_z(plane, value):
        diff_z[plane] = value

    cross_diffs(range(nx), lambda plane: out_state[1, plane], put_y, put_z, ny, nz)
    partial[...] = jnp.zeros_like(partial)

    def third(rows):
        at = pl.ds(rows, BLK)
        co = [loaded(coef, block, at, clock[2]) for block in range(nx // BLK)]
        cells = {plane: out_state[1, plane, at] for plane in range(nx)}
        total = partial[...]
        for plane in range(nx):
            at_edge = plane < REACH or plane >= nx - REACH
            if at_edge:
                previous = ext[plane if plane < REACH else plane - nx + 2 * REACH, at]
                fields = [out_layer[d, plane, at] for d in range(4)]
            else:
                previous = first_in[plane - REACH, at]
                fields = [out_layer[0, plane, at]]
                fields += [second_in[1 + d, plane, at] for d in range(1, 4)]
            value, memory, stiff = advance(
                cells[plane],
                previous,
                fields[:3],
                fields[3],
                forcing[plane, at],
                [first_diff(cells, plane), diff_y[plane, at], diff_z[plane, at]],
                co[plane // BLK],
            )
            done = out_filtered[plane, at] + weights[2] * value
            for d in range(3):
                out_layer[d, plane, at] = memory[d]
            out_layer[3, plane, at] = stiff
            out_state[0, plane, at] = value
            out_filtered[plane, at] = done
            if not at_edge:
                total = total + done * done
        partial[...] = total

    over_rows(ny, third)


def finish_kernel(
    coef, clock, across, inside, across_late, ghost_inside, ghost_across, partial,
    state_in, layer_in, filtered_in,
    out_state, out_layer, out_filtered, total_out,
):
    _, nx, ny, _ = state_in.shape
    n_block = nx // BLK
    even = is_even()
    weight = clock[2 * STEPS - 1]
    total_out[...] = partial[...]
    ghosts = (range(-REACH, 0), range(nx, nx + REACH))
    owned = (range(REACH), range(nx - REACH, nx))

    def step(rows):
        at = pl.ds(rows, BLK)
        halo = {}
        for number in range(REACH):
            one = inside[number, at]
            two = across[number, at] + across_late[number, at]
            left = jnp.where(even, two, one)
            right = jnp.where(even, one, two)
            one, two = ghost_inside[REACH - 1 - number, at], ghost_across[REACH - 1 - number, at]
            halo[-REACH + number] = left + jnp.where(even, two, one)
            one, two = ghost_inside[number, at], ghost_across[number, at]
            halo[nx + number] = right + jnp.where(even, one, two)
        total = total_out[...]
        for side in range(2):
            block = side * (n_block - 1)
            kappa_r, q0 = coef[KAPPA_R, block, at], coef[Q0, block, at]
            for plane in owned[side]:
                outer = outer_part(halo, plane, ghosts[side])
                added = kappa_r * outer
                out_state[0, plane, at] = state_in[0, plane, at] + added
                out_layer[0, plane, at] = layer_in[0, plane, at] + q0 * outer
                done = filtered_in[plane, at] + weight * added
                out_filtered[plane, at] = done
                total = total + done * done
        total_out[...] = total

    over_rows(ny, step)


def store_kernel(parts, values, *refs):
    n = len(parts)
    arrays, outs, values_out, sems = refs[:n], refs[-n - 2 : -2], refs[-2], refs[-1]
    copies = [
        pltpu.make_async_copy(
            *((array, out) if at is None else (array.at[at], out.at[at])), sems.at[number]
        )
        for number, (at, array, out) in enumerate(zip(parts, arrays, outs))
    ]
    for copy in copies:
        copy.start()
    values_out[...] = values[...]
    for copy in copies:
        copy.wait()


def norm_kernel(cells, values, got, norm):
    total = jnp.sum(values[...] + got[...], axis=1, keepdims=True)
    total = jnp.sum(total, axis=0, keepdims=True)
    norm[...] = jnp.sqrt(total / cells + 1e-06)


SCALAR = pl.BlockSpec(memory_space=pltpu.SMEM)
HBM = pl.BlockSpec(memory_space=pltpu.HBM)
VEC = pl.BlockSpec(memory_space=pltpu.VMEM)


def held(*shape):
    return pltpu.VMEM(shape, F32)


def in_vmem(*arrays):
    return [pltpu.with_memory_space_constraint(array, pltpu.VMEM) for array in arrays]


def in_hbm(*arrays):
    return [pltpu.with_memory_space_constraint(array, pltpu.HBM) for array in arrays]


def call(kernel, name, in_specs, out_shape, out_specs, scratch, operands, micros, aliases=None):
    return pl.pallas_call(
        kernel,
        name=name,
        in_specs=in_specs,
        out_shape=out_shape,
        out_specs=out_specs,
        scratch_shapes=scratch,
        input_output_aliases=aliases or {},
        compiler_params=pltpu.CompilerParams(vmem_limit_bytes=VMEM_LIMIT),
        cost_estimate=pl.CostEstimate(
            flops=0, bytes_accessed=int(micros * 3.6e6), transcendentals=0
        ),
    )(*operands)


def swap_pairs(count):
    inside = [(i, i ^ 1) for i in range(count)]
    across = []
    for i in range(1, count - 1, 2):
        across += [(i, i + 1), (i + 1, i)]
    return inside, across


def halves(pairs):
    return [[pair for pair in pairs if min(pair) % 4 == first] for first in (1, 3)]


def store(values, parts, arrays, begun=()):
    n = len(arrays)
    outs = [jax.ShapeDtypeStruct(array.shape, F32) for array in arrays]
    *stored, values = call(
        functools.partial(store_kernel, parts),
        "store",
        [VEC] * (1 + n) + [HBM] * len(begun),
        [*outs, held(*values.shape)],
        [HBM] * n + [VEC],
        [pltpu.SemaphoreType.DMA((n,))],
        (*in_vmem(values, *arrays), *begun),
        1,
        {1 + n + number: n - len(begun) + number for number in range(len(begun))},
    )
    return values, stored


def norm_and_stores(values, state, layer, running, axis):
    count = lax.axis_size(axis)
    half = layer.shape[0] // 2
    stored = {}

    def first(values):
        values, (stored["state"],) = store(values, [None], [state])
        return values

    def second(values):
        values, (stored["layer"],) = store(values, [pl.ds(0, half)], [layer])
        return values

    def third(values):
        values, (stored["running"], stored["layer"]) = store(
            values, [None, pl.ds(half, half)], [running, layer], [stored["layer"]]
        )
        return values

    waiting = [first, second, third]
    hops = [] if count & (count - 1) else [1 << k for k in range(count.bit_length() - 1)]
    for number, hop in enumerate(hops):
        got = lax.ppermute(values, axis, [(i, i ^ hop) for i in range(count)])
        if waiting and number >= 1:
            values = waiting.pop(0)(values)
        if hop != hops[-1]:
            values = values + got
    for step in waiting:
        values = step(values)
    if not hops:
        values, got = lax.psum(values, axis), jnp.zeros_like(values)
    norm = call(
        functools.partial(norm_kernel, float(running.size * count)),
        "norm",
        [VEC] * 2,
        jax.ShapeDtypeStruct((1, 1), F32),
        VEC,
        [],
        in_vmem(values, got),
        1,
    )
    return norm.reshape(1), stored["state"], stored["layer"], stored["running"]


def body(
    wave_state, layer_fields, source, filtered, frequency, start_time, speed_table, speed_index,
    pml_mask,
):
    _, nx, ny, nz = wave_state.shape
    n_block = nx // BLK
    count = lax.axis_size("gx")
    pair_inside, pair_across = swap_pairs(count)
    brick = (nx, ny, nz)
    strip = (REACH, ny, nz)
    message = (2 * REACH * ny + BLK, nz)
    dma = pltpu.SemaphoreType.DMA
    vec = lambda *shape: pltpu.VMEM(shape, F32)

    blocks = (speed_index.shape[1], n_block, speed_index.shape[2])
    index, mask = in_hbm(*(jnp.transpose(one, (1, 0, 2)) for one in (speed_index, pml_mask)))

    inside, across, coef, clock, edge, wave, layer, forcing = call(
        send_kernel,
        "strips",
        [HBM] * 3 + [SCALAR] * 2 + [HBM] * 3,
        [
            held(*message), held(*message), held(N_COEF, n_block, ny, nz),
            held(2 * STEPS, BLK, nz), held(2, 5, *strip), held(*wave_state.shape),
            held(*layer_fields.shape), held(*brick),
        ],
        [VEC] * 8,
        [
            vec(2 * REACH, ny, nz),
            vec(2 * REACH, ny, nz),
            vec(2, n_block * TAG_ROWS, nz),
            vec(2, BLK, nz),
            pltpu.VMEM(blocks, jnp.int32),
            pltpu.VMEM(blocks, jnp.int32),
            pltpu.SMEM(speed_table.shape, F32),
            dma((13,)),
        ],
        (
            *in_hbm(wave_state, layer_fields, source), frequency, start_time,
            *in_hbm(speed_table), index, mask,
        ),
        2.5,
    )
    got_inside = lax.ppermute(inside, "gx", pair_inside)
    got_across = lax.ppermute(across, "gx", pair_across)
    coef, clock, edge, wave, layer, forcing, running = in_vmem(
        coef, clock, edge, wave, layer, forcing, filtered
    )

    later_inside, later_across, first, second, run = call(
        local_kernel,
        "local",
        [VEC] * 6,
        [
            held(*strip), held(*strip), held(nx - 2 * REACH, ny, nz), held(5, *brick),
            held(*brick),
        ],
        [VEC] * 5,
        [vec(4, nx - 2 * REACH, ny, nz), vec(*brick), vec(*brick)],
        (wave, layer, forcing, coef, clock, edge),
        4,
    )
    last_inside = lax.ppermute(later_inside, "gx", pair_inside)
    early_pairs, late_pairs = halves(pair_across)
    last_across = lax.ppermute(later_across, "gx", early_pairs)
    out_types = [
        held(*wave_state.shape), held(*layer_fields.shape), held(*filtered.shape)
    ]
    edge_type = held(2 * REACH, ny, nz)
    side_scratch = [vec(2 * REACH, ny, nz)] * 3 + [vec(5, ny, nz)] + [vec(2 * REACH, ny, nz)] * 2
    later_across, got_inside = lax.optimization_barrier((later_across, got_inside))
    last_late = lax.ppermute(later_across, "gx", late_pairs)
    first, second, run = in_vmem(first, second, run)
    next_state, next_layer, next_filtered, ext, ghost_inside = call(
        inside_kernel,
        "inner_half",
        [VEC] * 8,
        out_types + [edge_type, held(*strip)],
        [VEC] * 5,
        side_scratch,
        (*in_vmem(got_inside), coef, clock, wave, running, edge, second, run),
        1.5,
    )
    next_state, next_layer, next_filtered, ext, ghost_across, partial = call(
        joint_kernel,
        "joint",
        [VEC] * 14,
        out_types + [edge_type, held(*strip), held(BLK, nz)],
        [VEC] * 6,
        [vec(*brick), vec(*brick), *side_scratch],
        (
            *in_vmem(got_across), coef, clock, wave, forcing, running, edge, first, second, run,
            *in_vmem(next_state, next_layer, next_filtered, ext),
        ),
        5,
        {10: 0, 11: 1, 12: 2, 13: 3},
    )
    next_state, next_layer, next_filtered, total = call(
        finish_kernel,
        "finish",
        [VEC] * 11,
        out_types + [held(BLK, nz)],
        [VEC] * 4,
        [],
        (
            coef, clock,
            *in_vmem(
                last_across, last_inside, last_late, ghost_inside, ghost_across, partial,
                next_state, next_layer, next_filtered,
            ),
        ),
        1,
        {8: 0, 9: 1, 10: 2},
    )
    filter_norm, next_state, next_layer, next_filtered = norm_and_stores(
        total, next_state, next_layer, next_filtered, "gx"
    )
    return next_state, next_layer, next_filtered, filter_norm


def solution(mesh):
    placed = (
        P("grp", "gx", None, None),
        P("grp", "gx", None, None),
        P(("grp", "gx"), None, None),
        P(("grp", "gx"), None, None),
        P("grp"),
        P("grp"),
        P(),
        P("gx", None, None),
        P("gx", None, None),
    )
    return jax.shard_map(
        body,
        mesh=mesh,
        in_specs=placed,
        out_specs=(
            P("grp", "gx", None, None),
            P("grp", "gx", None, None),
            P(("grp", "gx"), None, None),
            P("grp"),
        ),
        check_vma=False,
    )
```

```python
import functools
import math

import jax
import jax.numpy as jnp
from jax import lax
from jax.experimental import pallas as pl
from jax.experimental.pallas import tpu as pltpu
from jax.sharding import PartitionSpec as P

F32 = jnp.float32
BF16 = jnp.bfloat16
STEPS = 3
BLK = 8
REACH = 4
TIME_STEP = 0.25
DAMP_PEAK = 1.5
STENCIL = (-205.0 / 72.0, 8.0 / 5.0, -1.0 / 5.0, 8.0 / 315.0, -1.0 / 560.0)
SCALE = 5040.0
WHOLE = (-14336.0, 8064.0, -1008.0, 128.0, -9.0)
CENTRE_REST = 14.0 / SCALE
TAG_ROWS = 16
KAPPA, KAPPA_R, Q0, Q1, Q2, B0, B1, B2, DECAY, PAIR, AMP, BACK, STIFF, FORCE, PUSH = range(15)
N_COEF = 14
VMEM_LIMIT = 30 * 1024 * 1024


def band(rows, cols, row_period, col_period):
    row = lax.broadcasted_iota(jnp.int32, (rows, cols), 0) % row_period
    col = lax.broadcasted_iota(jnp.int32, (rows, cols), 1) % col_period
    apart = jnp.abs(row - col)
    out = jnp.zeros((rows, cols), F32)
    for offset, value in enumerate(WHOLE):
        out = jnp.where(apart == offset, value, out)
    return out.astype(BF16)


def pieces(cells):
    high = cells.astype(BF16)
    return high, (cells - high.astype(F32)).astype(BF16)


def cross_diffs(planes, read, write_y, write_z, ny, nz):
    mat_y = band(ny, 2 * ny, ny, ny)
    mat_z = band(2 * nz, nz, nz, nz)
    for one, two in zip(planes[0::2], planes[1::2]):
        high_one, low_one = pieces(read(one))
        high_two, low_two = pieces(read(two))
        upper = jnp.concatenate([high_one, high_two], axis=1)
        lower = jnp.concatenate([low_one, low_two], axis=1)
        diff_y = jnp.dot(
            mat_y, jnp.concatenate([upper, lower], axis=0), preferred_element_type=F32
        )
        write_y(one, diff_y[:, :nz])
        write_y(two, diff_y[:, nz:])
        left = jnp.concatenate([high_one, low_one], axis=1)
        right = jnp.concatenate([high_two, low_two], axis=1)
        diff_z = jnp.dot(
            jnp.concatenate([left, right], axis=0), mat_z, preferred_element_type=F32
        )
        write_z(one, diff_z[:ny])
        write_z(two, diff_z[ny:])


def first_diff(cells, at):
    total = STENCIL[0] * cells[at]
    for offset in range(1, REACH + 1):
        above, below = cells.get(at + offset), cells.get(at - offset)
        if above is not None and below is not None:
            total = total + STENCIL[offset] * (above + below)
        elif above is not None:
            total = total + STENCIL[offset] * above
        elif below is not None:
            total = total + STENCIL[offset] * below
    return total


def outer_part(cells, at, positions):
    total = None
    for position in positions:
        offset = abs(position - at)
        if offset <= REACH:
            term = STENCIL[offset] * cells[position]
            total = term if total is None else total + term
    return total


def advance(cells, previous, memory, stiff, forcing, diffs, co):
    rest = CENTRE_REST * cells
    diffs = [diffs[0], diffs[1] * (1.0 / SCALE) - rest, diffs[2] * (1.0 / SCALE) - rest]
    memory = [m + co(Q0 + d) * (diffs[d] - m) for d, m in enumerate(memory)]
    inner = sum(diffs[d] - co(B0 + d) * memory[d] for d in range(3))
    stiff = co(DECAY) * stiff + co(PAIR) * cells
    new = (
        co(AMP) * cells
        - co(BACK) * previous
        + co(KAPPA) * inner
        - co(STIFF) * stiff
        - co(PUSH) * forcing
    )
    return new, memory, stiff


def loaded(coef, block, at, phase):
    have = {}

    def get(entry):
        if entry not in have:
            if entry == PUSH:
                have[entry] = coef[FORCE, block, at] * phase
            else:
                have[entry] = coef[entry, block, at]
        return have[entry]

    return get


def coefficients(speed_square, bits):
    rates = [DAMP_PEAK * bit for bit in bits]
    damping = rates[0] + rates[1] + rates[2]
    pairing = rates[0] * rates[1] + rates[1] * rates[2] + rates[2] * rates[0]
    retention = [jnp.exp(-TIME_STEP * rate) for rate in rates]
    half = 0.5 * TIME_STEP * damping
    inverse = 1.0 / (1.0 + half)
    square = TIME_STEP * TIME_STEP
    kappa = square * speed_square * inverse
    return (
        kappa,
        kappa * retention[0],
        1.0 - retention[0],
        1.0 - retention[1],
        1.0 - retention[2],
        bits[0],
        bits[1],
        bits[2],
        jnp.exp(-TIME_STEP * damping),
        TIME_STEP * pairing,
        (2.0 - square * pairing) * inverse,
        (1.0 - half) * inverse,
        square * damping * inverse,
        square * inverse,
    )


def along_last(tiles, nz):
    row = lax.broadcasted_iota(jnp.int32, (nz, nz), 0)
    col = lax.broadcasted_iota(jnp.int32, (nz, nz), 1) // BLK
    along = (row == col).astype(F32).astype(BF16)
    return jnp.dot(tiles.astype(BF16), along, preferred_element_type=F32)


def tag_places(rows, lanes):
    return [
        (number * lanes, first, min(BLK, rows - first))
        for number, first in enumerate(range(0, rows, BLK))
    ]


def from_tag(tile, rows, lanes, nz):
    number = len(tag_places(rows, lanes))
    lane = lax.broadcasted_iota(jnp.int32, (nz, 2 * number * nz), 0)
    col = lax.broadcasted_iota(jnp.int32, (nz, 2 * number * nz), 1)
    along = (lane == col // nz * lanes + col % nz // BLK).astype(F32).astype(BF16)
    high = tile.astype(BF16).astype(F32)
    middle = (tile - high).astype(BF16).astype(F32)
    split = jnp.concatenate([high, middle, tile - high - middle, jnp.zeros_like(tile)], axis=0)
    wide = jnp.dot(split.astype(BF16), along, preferred_element_type=F32)
    wide = wide[:BLK] + wide[BLK : 2 * BLK] + wide[2 * BLK : 3 * BLK]
    columns = [wide[:, at * nz : (at + 1) * nz] for at in range(2 * number)]
    return [
        jnp.concatenate(columns[part * number : (part + 1) * number], axis=0) for part in range(2)
    ]


def squares(index, table):
    speed = jnp.zeros_like(index)
    for entry in range(table.shape[0]):
        speed = jnp.where(index == float(entry), table[entry], speed)
    return speed * speed


def bits_of(mask):
    mask = mask.astype(jnp.int32)
    return [((mask >> direction) & 1).astype(F32) for direction in range(3)]


def down_second(ref, lead, value, ny):
    for block in range(ny // BLK):
        rows = jnp.broadcast_to(value[block : block + 1], (BLK, value.shape[1]))
        ref[(*lead, pl.ds(block * BLK, BLK))] = rows


def fill_clock(clock, freq, start):
    steps = lax.broadcasted_iota(jnp.int32, clock.shape[1:], 0).astype(F32)
    cosine = jnp.cos(freq[0] * (start[0] + steps * TIME_STEP))
    weight = (TIME_STEP * freq[0] / math.pi) * (cosine - 0.25)
    for count in range(STEPS):
        clock[count] = jnp.broadcast_to(cosine[count : count + 1], cosine.shape)
        clock[STEPS + count] = jnp.broadcast_to(weight[count + 1 : count + 2], weight.shape)


def over_rows(ny, step):
    def one(block, carry):
        step(pl.multiple_of(block * BLK, BLK))
        return carry

    lax.fori_loop(0, ny // BLK, one, 0, unroll=2)


def is_even():
    return lax.axis_index("gx") % 2 == 0


def edge_planes(nx):
    return [*range(REACH), *range(nx - REACH, nx)]


def send_kernel(
    wave_in, layer_in, source_in, freq, start, table_in, index_in, mask_in,
    inside, across, coef, clock, edge, wave, layer, source,
    diff_y, diff_z, tags, tag_tiles, index, mask, table, sems,
):
    _, nx, ny, nz = wave.shape
    n_block = nx // BLK
    edges = (0, nx - REACH)
    pieces_of = [(wave_in.at[0], wave.at[0])]
    for first, length in ((0, REACH), (nx - REACH, REACH), (REACH, nx - 2 * REACH)):
        at = pl.ds(first, length)
        pieces_of += [
            (wave_in.at[1, at], wave.at[1, at]),
            (layer_in.at[:, at], layer.at[:, at]),
            (source_in.at[at], source.at[at]),
        ]
    copies = [
        pltpu.make_async_copy(one, to, sems.at[number])
        for number, (one, to) in enumerate(pieces_of)
    ]
    small = [
        pltpu.make_async_copy(one, to, sems.at[len(copies) + number])
        for number, (one, to) in enumerate(
            ((index_in, index), (mask_in, mask), (table_in, table))
        )
    ]
    for copy in small + copies:
        copy.start()
    even = is_even()
    tags[...] = jnp.zeros_like(tags)
    fill_clock(clock, freq, start)
    phase = clock[0]
    for copy in small:
        copy.wait()
    rows = n_block * TAG_ROWS
    for block in range(n_block):
        at = pl.ds(block * TAG_ROWS, index.shape[0])
        tags[0, at, : index.shape[2]] = index[:, block].astype(F32)
        tags[1, at, : mask.shape[2]] = mask[:, block].astype(F32)
    wide = along_last(tags[...].reshape(2 * rows, nz), nz)
    square = squares(wide[:rows], table)
    masks = wide[rows:]
    values = coefficients(square, bits_of(masks))
    for entry, value in enumerate(values):
        for block in range(n_block):
            down_second(coef, (entry, block), value[block * TAG_ROWS : (block + 1) * TAG_ROWS], ny)
    tag_tiles[...] = jnp.zeros_like(tag_tiles)
    places = tag_places(index.shape[0], index.shape[2])
    for side in range(2):
        block = side * (n_block - 1)
        speed = jnp.zeros(index.shape[::2], F32)
        for entry in range(table.shape[0]):
            speed = jnp.where(index[:, block] == entry, table[entry], speed)
        for part, value in enumerate((speed * speed, mask[:, block].astype(F32))):
            for lane, first, length in places:
                lane += part * len(places) * value.shape[1]
                tag_tiles[side, :length, lane : lane + value.shape[1]] = value[
                    first : first + length
                ]
    to = pl.ds(2 * REACH * ny, BLK)
    inside[to] = jnp.where(even, tag_tiles[1], tag_tiles[0])
    across[to] = jnp.where(even, tag_tiles[0], tag_tiles[1])
    copies[0].wait()
    planes = edge_planes(nx)
    slot = {plane: number for number, plane in enumerate(planes)}

    def put_y(plane, value):
        diff_y[slot[plane]] = value

    def put_z(plane, value):
        diff_z[slot[plane]] = value

    cross_diffs(planes, lambda plane: wave[0, plane], put_y, put_z, ny, nz)
    for copy in copies[1:7]:
        copy.wait()

    def step(rows):
        at = pl.ds(rows, BLK)
        sides = []
        for side in range(2):
            block = side * (n_block - 1)
            reach = range(2 * REACH) if side == 0 else range(nx - 2 * REACH, nx)
            cells = {plane: wave[0, plane, at] for plane in reach}
            values = []
            co = loaded(coef, block, at, phase)
            for number in range(REACH):
                plane = edges[side] + number
                new, memory, stiff = advance(
                    cells[plane],
                    wave[1, plane, at],
                    [layer[d, plane, at] for d in range(3)],
                    layer[3, plane, at],
                    source[plane, at],
                    [
                        first_diff(cells, plane),
                        diff_y[slot[plane], at],
                        diff_z[slot[plane], at],
                    ],
                    co,
                )
                for entry, value in enumerate((new, *memory, stiff)):
                    edge[side, entry, number, at] = value
                values.append((cells[plane], new))
            sides.append(values)
        for number in range(REACH):
            for part in range(2):
                to = pl.ds(pl.multiple_of((part * REACH + number) * ny + rows, BLK), BLK)
                left, right = sides[0][number][part], sides[1][number][part]
                inside[to] = jnp.where(even, right, left)
                across[to] = jnp.where(even, left, right)

    over_rows(ny, step)
    for copy in copies[7:]:
        copy.wait()


def local_kernel(
    wave, layer, source, coef, clock, edge,
    inside, across, first_out, second_out, run_out,
    fields, diff_y, diff_z,
):
    _, nx, ny, nz = wave.shape
    even = is_even()

    def put_y(plane, value):
        diff_y[plane] = value

    def put_z(plane, value):
        diff_z[plane] = value

    middle = range(REACH, nx - REACH)
    cross_diffs(middle, lambda plane: wave[0, plane], put_y, put_z, ny, nz)

    def read(entry, plane, at=slice(None)):
        if plane < REACH:
            return edge[0, entry, plane, at]
        if plane >= nx - REACH:
            return edge[1, entry, plane - nx + REACH, at]
        if entry == 0:
            return first_out[plane - REACH, at]
        return fields[entry - 1, plane - REACH, at]

    def first(rows):
        at = pl.ds(rows, BLK)
        co = [loaded(coef, block, at, clock[0]) for block in range(nx // BLK)]
        cells = {plane: wave[0, plane, at] for plane in range(nx)}
        for plane in middle:
            new, memory, stiff = advance(
                cells[plane],
                wave[1, plane, at],
                [layer[d, plane, at] for d in range(3)],
                layer[3, plane, at],
                source[plane, at],
                [first_diff(cells, plane), diff_y[plane, at], diff_z[plane, at]],
                co[plane // BLK],
            )
            first_out[plane - REACH, at] = new
            for entry, value in enumerate((*memory, stiff)):
                fields[entry, plane - REACH, at] = value

    over_rows(ny, first)
    cross_diffs(range(nx), lambda plane: read(0, plane), put_y, put_z, ny, nz)

    def second(rows):
        at = pl.ds(rows, BLK)
        co = [loaded(coef, block, at, clock[1]) for block in range(nx // BLK)]
        cells = {plane: read(0, plane, at) for plane in range(nx)}
        values = {}
        for plane in range(nx):
            new, memory, stiff = advance(
                cells[plane],
                wave[0, plane, at],
                [read(1 + d, plane, at) for d in range(3)],
                read(4, plane, at),
                source[plane, at],
                [first_diff(cells, plane), diff_y[plane, at], diff_z[plane, at]],
                co[plane // BLK],
            )
            values[plane] = new
            for entry, value in enumerate((new, *memory, stiff)):
                second_out[entry, plane, at] = value
            run_out[plane, at] = clock[STEPS] * cells[plane] + clock[STEPS + 1] * new
        for number in range(REACH):
            left, right = values[number], values[nx - REACH + number]
            inside[number, at] = jnp.where(even, right, left)
            across[number, at] = jnp.where(even, left, right)

    over_rows(ny, second)


def side_update(
    left, present, message, coef, clock, wave, running, edge, second_in, run_in,
    out_state, out_layer, out_filtered, ext, ghost,
    first, bump, push, ghost_coef, bump_y, bump_z,
):
    _, nx, ny, nz = wave.shape
    n_block = nx // BLK
    block = jnp.where(left, 0, n_block - 1)
    side = jnp.where(left, 0, 1)
    own = range(REACH)
    beyond = range(-1, -1 - REACH, -1)
    weights = [clock[STEPS + number] for number in range(2)]

    def plane_of(depth):
        return jnp.where(left, depth, nx - 1 - depth)

    def slot(depth):
        return depth if depth >= 0 else REACH - 1 - depth

    tag_at = 2 * REACH * ny
    tile = message[pl.ds(tag_at, BLK)]
    square, masks = from_tag(tile, ny // BLK, nz // BLK, nz)
    values = coefficients(square * present, bits_of(masks))
    for entry, value in enumerate(
        (
            values[KAPPA_R],
            values[Q0],
            values[KAPPA] * (1.0 - values[Q1]),
            values[KAPPA] * (1.0 - values[Q2]),
            values[AMP] - values[STIFF] * values[PAIR],
        )
    ):
        down_second(ghost_coef, (entry,), value, ny)

    def exchange(rows):
        at = pl.ds(rows, BLK)
        halo = {}
        sent = {}
        for depth in beyond:
            number = jnp.where(left, REACH + depth, -1 - depth)
            halo[depth] = message[pl.ds(pl.multiple_of(number * ny + rows, BLK), BLK)]
            number = number + REACH
            sent[depth] = message[pl.ds(pl.multiple_of(number * ny + rows, BLK), BLK)]
        mine = {depth: wave[0, plane_of(depth), at] for depth in own}
        kappa_r = coef[KAPPA_R, block, at]
        for depth in own:
            outer = outer_part(halo, depth, beyond)
            added = kappa_r * outer
            push[slot(depth), at] = outer
            bump[slot(depth), at] = added
            value = edge[side, 0, jnp.where(left, depth, REACH - 1 - depth), at] + added
            first[slot(depth), at] = value
            ext[jnp.where(left, depth, 2 * REACH - 1 - depth), at] = value
        kappa_r = ghost_coef[0, at]
        for depth in beyond:
            outer = outer_part(mine, depth, own)
            added = kappa_r * outer
            push[slot(depth), at] = outer
            bump[slot(depth), at] = added
            first[slot(depth), at] = sent[depth] + added

    over_rows(ny, exchange)

    def put_bump_y(plane, value):
        bump_y[plane] = value

    def put_bump_z(plane, value):
        bump_z[plane] = value

    cross_diffs(range(2 * REACH), lambda plane: bump[plane], put_bump_y, put_bump_z, ny, nz)

    def respond(added, true, depth, others, outer, q0, kappas, at):
        kappa_r, kappa_1, kappa_2, grown = kappas
        value = added[depth]
        rest = CENTRE_REST * value
        along = first_diff(added, depth) + outer_part(true, depth, others)
        side_y = bump_y[slot(depth), at] * (1.0 / SCALE) - rest
        side_z = bump_z[slot(depth), at] * (1.0 / SCALE) - rest
        gain = (
            grown * value + kappa_r * (along - q0 * outer) + kappa_1 * side_y + kappa_2 * side_z
        )
        return gain, along, side_y, side_z

    def second(rows):
        at = pl.ds(rows, BLK)
        true = {depth: first[slot(depth), at] for depth in (*own, *beyond)}
        added = {depth: bump[slot(depth), at] for depth in beyond}
        kappa_r, q0, kappa_1, kappa_2, grown = [ghost_coef[entry, at] for entry in range(5)]
        for depth in beyond:
            ghost[-1 - depth, at], _, _, _ = respond(
                added, true, depth, own, push[slot(depth), at], q0,
                (kappa_r, kappa_1, kappa_2, grown), at,
            )
        added = {depth: bump[slot(depth), at] for depth in own}
        kappa_r, kappa = coef[KAPPA_R, block, at], coef[KAPPA, block, at]
        q0, q1, q2 = [coef[entry, block, at] for entry in (Q0, Q1, Q2)]
        pair = coef[PAIR, block, at]
        kappas = (
            kappa_r,
            kappa * (1.0 - q1),
            kappa * (1.0 - q2),
            coef[AMP, block, at] - coef[STIFF, block, at] * pair,
        )
        for depth in own:
            plane = plane_of(depth)
            outer = push[slot(depth), at]
            gain, along, side_y, side_z = respond(
                added, true, depth, beyond, outer, q0, kappas, at
            )
            out_state[1, plane, at] = second_in[0, plane, at] + gain
            out_layer[0, plane, at] = second_in[1, plane, at] + q0 * (
                along + (1.0 - q0) * outer
            )
            out_layer[1, plane, at] = second_in[2, plane, at] + q1 * side_y
            out_layer[2, plane, at] = second_in[3, plane, at] + q2 * side_z
            out_layer[3, plane, at] = second_in[4, plane, at] + pair * added[depth]
            out_filtered[plane, at] = (
                running[plane, at]
                + run_in[plane, at]
                + weights[0] * added[depth]
                + weights[1] * gain
            )
        for depth in range(REACH, 2 * REACH):
            plane = plane_of(depth)
            along = outer_part(added, depth, own)
            gain = kappa_r * along
            out_state[1, plane, at] = second_in[0, plane, at] + gain
            out_layer[0, plane, at] = second_in[1, plane, at] + q0 * along
            out_filtered[plane, at] = running[plane, at] + run_in[plane, at] + weights[1] * gain

    over_rows(ny, second)


def inside_kernel(
    inside, coef, clock, wave, running, edge, second_in, run_in,
    out_state, out_layer, out_filtered, ext, ghost,
    *scratch,
):
    side_update(
        jnp.logical_not(is_even()), 1.0, inside, coef, clock, wave, running, edge, second_in,
        run_in, out_state, out_layer, out_filtered, ext, ghost, *scratch,
    )


def joint_kernel(
    across, coef, clock, wave, forcing, running, edge, first_in, second_in, run_in,
    state_in, layer_in, filtered_in, ext_in,
    out_state, out_layer, out_filtered, ext, ghost, partial,
    diff_y, diff_z, *scratch,
):
    del state_in, layer_in, filtered_in, ext_in
    _, nx, ny, nz = wave.shape
    count = lax.axis_size("gx")
    place = lax.axis_index("gx")
    even = is_even()
    weights = [clock[STEPS + number] for number in range(STEPS)]
    outermost = jnp.logical_or(place == 0, place == count - 1)
    side_update(
        even, jnp.where(outermost, 0.0, 1.0).astype(F32), across, coef, clock, wave, running,
        edge, second_in, run_in, out_state, out_layer, out_filtered, ext, ghost, *scratch,
    )
    if nx > 4 * REACH:

        def between(rows):
            at = pl.ds(rows, BLK)
            for plane in range(2 * REACH, nx - 2 * REACH):
                out_state[1, plane, at] = second_in[0, plane, at]
                out_layer[0, plane, at] = second_in[1, plane, at]
                out_filtered[plane, at] = running[plane, at] + run_in[plane, at]

        over_rows(ny, between)

    def put_y(plane, value):
        diff_y[plane] = value

    def put_z(plane, value):
        diff_z[plane] = value

    cross_diffs(range(nx), lambda plane: out_state[1, plane], put_y, put_z, ny, nz)
    partial[...] = jnp.zeros_like(partial)

    def third(rows):
        at = pl.ds(rows, BLK)
        co = [loaded(coef, block, at, clock[2]) for block in range(nx // BLK)]
        cells = {plane: out_state[1, plane, at] for plane in range(nx)}
        total = partial[...]
        for plane in range(nx):
            at_edge = plane < REACH or plane >= nx - REACH
            if at_edge:
                previous = ext[plane if plane < REACH else plane - nx + 2 * REACH, at]
                fields = [out_layer[d, plane, at] for d in range(4)]
            else:
                previous = first_in[plane - REACH, at]
                fields = [out_layer[0, plane, at]]
                fields += [second_in[1 + d, plane, at] for d in range(1, 4)]
            value, memory, stiff = advance(
                cells[plane],
                previous,
                fields[:3],
                fields[3],
                forcing[plane, at],
                [first_diff(cells, plane), diff_y[plane, at], diff_z[plane, at]],
                co[plane // BLK],
            )
            done = out_filtered[plane, at] + weights[2] * value
            for d in range(3):
                out_layer[d, plane, at] = memory[d]
            out_layer[3, plane, at] = stiff
            out_state[0, plane, at] = value
            out_filtered[plane, at] = done
            if not at_edge:
                total = total + done * done
        partial[...] = total

    over_rows(ny, third)


def finish_kernel(
    coef, clock, across, inside, across_late, ghost_inside, ghost_across, partial,
    state_in, layer_in, filtered_in,
    out_state, out_layer, out_filtered, total_out,
    gathered,
):
    _, nx, ny, _ = state_in.shape
    n_block = nx // BLK
    even = is_even()
    weight = clock[2 * STEPS - 1]
    gathered[...] = partial[...]
    ghosts = (range(-REACH, 0), range(nx, nx + REACH))
    owned = (range(REACH), range(nx - REACH, nx))

    def step(rows):
        at = pl.ds(rows, BLK)
        halo = {}
        for number in range(REACH):
            one = inside[number, at]
            two = across[number, at] + across_late[number, at]
            left = jnp.where(even, two, one)
            right = jnp.where(even, one, two)
            one, two = ghost_inside[REACH - 1 - number, at], ghost_across[REACH - 1 - number, at]
            halo[-REACH + number] = left + jnp.where(even, two, one)
            one, two = ghost_inside[number, at], ghost_across[number, at]
            halo[nx + number] = right + jnp.where(even, one, two)
        total = gathered[...]
        for side in range(2):
            block = side * (n_block - 1)
            kappa_r, q0 = coef[KAPPA_R, block, at], coef[Q0, block, at]
            for plane in owned[side]:
                outer = outer_part(halo, plane, ghosts[side])
                added = kappa_r * outer
                out_state[0, plane, at] = state_in[0, plane, at] + added
                out_layer[0, plane, at] = layer_in[0, plane, at] + q0 * outer
                done = filtered_in[plane, at] + weight * added
                out_filtered[plane, at] = done
                total = total + done * done
        gathered[...] = total

    over_rows(ny, step)
    total_out[...] = jnp.sum(gathered[...], axis=0, keepdims=True)


def store_kernel(parts, values, *refs):
    n = len(parts)
    arrays, outs, values_out, sems = refs[:n], refs[-n - 2 : -2], refs[-2], refs[-1]
    copies = [
        pltpu.make_async_copy(
            *((array, out) if at is None else (array.at[at], out.at[at])), sems.at[number]
        )
        for number, (at, array, out) in enumerate(zip(parts, arrays, outs))
    ]
    for copy in copies:
        copy.start()
    values_out[...] = values[...]
    for copy in copies:
        copy.wait()


def norm_kernel(cells, values, got, norm):
    total = jnp.sum(values[...] + got[...], axis=1, keepdims=True)
    total = jnp.sum(total, axis=0, keepdims=True)
    norm[...] = jnp.sqrt(total / cells + 1e-06)


SCALAR = pl.BlockSpec(memory_space=pltpu.SMEM)
HBM = pl.BlockSpec(memory_space=pltpu.HBM)
VEC = pl.BlockSpec(memory_space=pltpu.VMEM)


def held(*shape):
    return pltpu.VMEM(shape, F32)


def in_vmem(*arrays):
    return [pltpu.with_memory_space_constraint(array, pltpu.VMEM) for array in arrays]


def in_hbm(*arrays):
    return [pltpu.with_memory_space_constraint(array, pltpu.HBM) for array in arrays]


def call(kernel, name, in_specs, out_shape, out_specs, scratch, operands, micros, aliases=None):
    return pl.pallas_call(
        kernel,
        name=name,
        in_specs=in_specs,
        out_shape=out_shape,
        out_specs=out_specs,
        scratch_shapes=scratch,
        input_output_aliases=aliases or {},
        compiler_params=pltpu.CompilerParams(vmem_limit_bytes=VMEM_LIMIT),
        cost_estimate=pl.CostEstimate(
            flops=0, bytes_accessed=int(micros * 3.6e6), transcendentals=0
        ),
    )(*operands)


def swap_pairs(count):
    inside = [(i, i ^ 1) for i in range(count)]
    across = []
    for i in range(1, count - 1, 2):
        across += [(i, i + 1), (i + 1, i)]
    return inside, across


def halves(pairs):
    return [[pair for pair in pairs if min(pair) % 4 == first] for first in (1, 3)]


def store(values, parts, arrays, begun=()):
    n = len(arrays)
    outs = [jax.ShapeDtypeStruct(array.shape, F32) for array in arrays]
    *stored, values = call(
        functools.partial(store_kernel, parts),
        "store",
        [VEC] * (1 + n) + [HBM] * len(begun),
        [*outs, held(*values.shape)],
        [HBM] * n + [VEC],
        [pltpu.SemaphoreType.DMA((n,))],
        (*in_vmem(values, *arrays), *begun),
        1,
        {1 + n + number: n - len(begun) + number for number in range(len(begun))},
    )
    return values, stored


def norm_and_stores(values, state, layer, running, axis):
    count = lax.axis_size(axis)
    half = layer.shape[0] // 2
    stored = {}

    def first(values):
        values, (stored["state"],) = store(values, [None], [state])
        return values

    def second(values):
        values, (stored["layer"],) = store(values, [pl.ds(0, half)], [layer])
        return values

    def third(values):
        values, (stored["running"], stored["layer"]) = store(
            values, [None, pl.ds(half, half)], [running, layer], [stored["layer"]]
        )
        return values

    waiting = [first, second, third]
    hops = [] if count & (count - 1) else [1 << k for k in range(count.bit_length() - 1)]
    for number, hop in enumerate(hops):
        got = lax.ppermute(values, axis, [(i, i ^ hop) for i in range(count)])
        if waiting and number >= 1:
            values = waiting.pop(0)(values)
        if hop != hops[-1]:
            values = values + got
    for step in waiting:
        values = step(values)
    if not hops:
        values, got = lax.psum(values, axis), jnp.zeros_like(values)
    norm = call(
        functools.partial(norm_kernel, float(running.size * count)),
        "norm",
        [VEC] * 2,
        jax.ShapeDtypeStruct((1, 1), F32),
        VEC,
        [],
        in_vmem(values, got),
        1,
    )
    return norm.reshape(1), stored["state"], stored["layer"], stored["running"]


def body(
    wave_state, layer_fields, source, filtered, frequency, start_time, speed_table, speed_index,
    pml_mask,
):
    _, nx, ny, nz = wave_state.shape
    n_block = nx // BLK
    count = lax.axis_size("gx")
    pair_inside, pair_across = swap_pairs(count)
    brick = (nx, ny, nz)
    strip = (REACH, ny, nz)
    message = (2 * REACH * ny + BLK, nz)
    dma = pltpu.SemaphoreType.DMA
    vec = lambda *shape: pltpu.VMEM(shape, F32)

    blocks = (speed_index.shape[1], n_block, speed_index.shape[2])
    index, mask = in_hbm(*(jnp.transpose(one, (1, 0, 2)) for one in (speed_index, pml_mask)))

    inside, across, coef, clock, edge, wave, layer, forcing = call(
        send_kernel,
        "strips",
        [HBM] * 3 + [SCALAR] * 2 + [HBM] * 3,
        [
            held(*message), held(*message), held(N_COEF, n_block, ny, nz),
            held(2 * STEPS, BLK, nz), held(2, 5, *strip), held(*wave_state.shape),
            held(*layer_fields.shape), held(*brick),
        ],
        [VEC] * 8,
        [
            vec(2 * REACH, ny, nz),
            vec(2 * REACH, ny, nz),
            vec(2, n_block * TAG_ROWS, nz),
            vec(2, BLK, nz),
            pltpu.VMEM(blocks, jnp.int32),
            pltpu.VMEM(blocks, jnp.int32),
            pltpu.SMEM(speed_table.shape, F32),
            dma((13,)),
        ],
        (
            *in_hbm(wave_state, layer_fields, source), frequency, start_time,
            *in_hbm(speed_table), index, mask,
        ),
        2.5,
    )
    got_inside = lax.ppermute(inside, "gx", pair_inside)
    got_across = lax.ppermute(across, "gx", pair_across)
    coef, clock, edge, wave, layer, forcing, running = in_vmem(
        coef, clock, edge, wave, layer, forcing, filtered
    )

    later_inside, later_across, first, second, run = call(
        local_kernel,
        "local",
        [VEC] * 6,
        [
            held(*strip), held(*strip), held(nx - 2 * REACH, ny, nz), held(5, *brick),
            held(*brick),
        ],
        [VEC] * 5,
        [vec(4, nx - 2 * REACH, ny, nz), vec(*brick), vec(*brick)],
        (wave, layer, forcing, coef, clock, edge),
        4,
    )
    last_inside = lax.ppermute(later_inside, "gx", pair_inside)
    early_pairs, late_pairs = halves(pair_across)
    last_across = lax.ppermute(later_across, "gx", early_pairs)
    out_types = [
        held(*wave_state.shape), held(*layer_fields.shape), held(*filtered.shape)
    ]
    edge_type = held(2 * REACH, ny, nz)
    side_scratch = [vec(2 * REACH, ny, nz)] * 3 + [vec(5, ny, nz)] + [vec(2 * REACH, ny, nz)] * 2
    later_across, got_inside = lax.optimization_barrier((later_across, got_inside))
    last_late = lax.ppermute(later_across, "gx", late_pairs)
    first, second, run = in_vmem(first, second, run)
    next_state, next_layer, next_filtered, ext, ghost_inside = call(
        inside_kernel,
        "inner_half",
        [VEC] * 8,
        out_types + [edge_type, held(*strip)],
        [VEC] * 5,
        side_scratch,
        (*in_vmem(got_inside), coef, clock, wave, running, edge, second, run),
        1.5,
    )
    next_state, next_layer, next_filtered, ext, ghost_across, partial = call(
        joint_kernel,
        "joint",
        [VEC] * 14,
        out_types + [edge_type, held(*strip), held(BLK, nz)],
        [VEC] * 6,
        [vec(*brick), vec(*brick), *side_scratch],
        (
            *in_vmem(got_across), coef, clock, wave, forcing, running, edge, first, second, run,
            *in_vmem(next_state, next_layer, next_filtered, ext),
        ),
        5,
        {10: 0, 11: 1, 12: 2, 13: 3},
    )
    next_state, next_layer, next_filtered, total = call(
        finish_kernel,
        "finish",
        [VEC] * 11,
        out_types + [held(1, nz)],
        [VEC] * 4,
        [vec(BLK, nz)],
        (
            coef, clock,
            *in_vmem(
                last_across, last_inside, last_late, ghost_inside, ghost_across, partial,
                next_state, next_layer, next_filtered,
            ),
        ),
        1,
        {8: 0, 9: 1, 10: 2},
    )
    filter_norm, next_state, next_layer, next_filtered = norm_and_stores(
        total, next_state, next_layer, next_filtered, "gx"
    )
    return next_state, next_layer, next_filtered, filter_norm


def solution(mesh):
    placed = (
        P("grp", "gx", None, None),
        P("grp", "gx", None, None),
        P(("grp", "gx"), None, None),
        P(("grp", "gx"), None, None),
        P("grp"),
        P("grp"),
        P(),
        P("gx", None, None),
        P("gx", None, None),
    )
    return jax.shard_map(
        body,
        mesh=mesh,
        in_specs=placed,
        out_specs=(
            P("grp", "gx", None, None),
            P("grp", "gx", None, None),
            P(("grp", "gx"), None, None),
            P("grp"),
        ),
        check_vma=False,
    )
```

```python
import functools
import math

import jax
import jax.numpy as jnp
from jax import lax
from jax.experimental import pallas as pl
from jax.experimental.pallas import tpu as pltpu
from jax.sharding import PartitionSpec as P

F32 = jnp.float32
BF16 = jnp.bfloat16
STEPS = 3
BLK = 8
REACH = 4
TIME_STEP = 0.25
DAMP_PEAK = 1.5
STENCIL = (-205.0 / 72.0, 8.0 / 5.0, -1.0 / 5.0, 8.0 / 315.0, -1.0 / 560.0)
SCALE = 5040.0
WHOLE = (-14336.0, 8064.0, -1008.0, 128.0, -9.0)
CENTRE_REST = 14.0 / SCALE
TAG_ROWS = 16
KAPPA, KAPPA_R, Q0, Q1, Q2, B0, B1, B2, DECAY, PAIR, AMP, BACK, STIFF, FORCE, PUSH = range(15)
N_COEF = 14
VMEM_LIMIT = 30 * 1024 * 1024


def band(rows, cols, row_period, col_period):
    row = lax.broadcasted_iota(jnp.int32, (rows, cols), 0) % row_period
    col = lax.broadcasted_iota(jnp.int32, (rows, cols), 1) % col_period
    apart = jnp.abs(row - col)
    out = jnp.zeros((rows, cols), F32)
    for offset, value in enumerate(WHOLE):
        out = jnp.where(apart == offset, value, out)
    return out.astype(BF16)


def pieces(cells):
    high = cells.astype(BF16)
    return high, (cells - high.astype(F32)).astype(BF16)


def cross_diffs(planes, read, write_y, write_z, ny, nz):
    mat_y = band(ny, 2 * ny, ny, ny)
    mat_z = band(2 * nz, nz, nz, nz)
    for one, two in zip(planes[0::2], planes[1::2]):
        high_one, low_one = pieces(read(one))
        high_two, low_two = pieces(read(two))
        upper = jnp.concatenate([high_one, high_two], axis=1)
        lower = jnp.concatenate([low_one, low_two], axis=1)
        diff_y = jnp.dot(
            mat_y, jnp.concatenate([upper, lower], axis=0), preferred_element_type=F32
        )
        write_y(one, diff_y[:, :nz])
        write_y(two, diff_y[:, nz:])
        left = jnp.concatenate([high_one, low_one], axis=1)
        right = jnp.concatenate([high_two, low_two], axis=1)
        diff_z = jnp.dot(
            jnp.concatenate([left, right], axis=0), mat_z, preferred_element_type=F32
        )
        write_z(one, diff_z[:ny])
        write_z(two, diff_z[ny:])


def first_diff(cells, at):
    total = STENCIL[0] * cells[at]
    for offset in range(1, REACH + 1):
        above, below = cells.get(at + offset), cells.get(at - offset)
        if above is not None and below is not None:
            total = total + STENCIL[offset] * (above + below)
        elif above is not None:
            total = total + STENCIL[offset] * above
        elif below is not None:
            total = total + STENCIL[offset] * below
    return total


def outer_part(cells, at, positions):
    total = None
    for position in positions:
        offset = abs(position - at)
        if offset <= REACH:
            term = STENCIL[offset] * cells[position]
            total = term if total is None else total + term
    return total


def advance(cells, previous, memory, stiff, forcing, diffs, co):
    rest = CENTRE_REST * cells
    diffs = [diffs[0], diffs[1] * (1.0 / SCALE) - rest, diffs[2] * (1.0 / SCALE) - rest]
    memory = [m + co(Q0 + d) * (diffs[d] - m) for d, m in enumerate(memory)]
    inner = sum(diffs[d] - co(B0 + d) * memory[d] for d in range(3))
    stiff = co(DECAY) * stiff + co(PAIR) * cells
    new = (
        co(AMP) * cells
        - co(BACK) * previous
        + co(KAPPA) * inner
        - co(STIFF) * stiff
        - co(PUSH) * forcing
    )
    return new, memory, stiff


def loaded(coef, block, at, phase):
    have = {}

    def get(entry):
        if entry not in have:
            if entry == PUSH:
                have[entry] = coef[FORCE, block, at] * phase
            else:
                have[entry] = coef[entry, block, at]
        return have[entry]

    return get


def coefficients(speed_square, bits):
    rates = [DAMP_PEAK * bit for bit in bits]
    damping = rates[0] + rates[1] + rates[2]
    pairing = rates[0] * rates[1] + rates[1] * rates[2] + rates[2] * rates[0]
    retention = [jnp.exp(-TIME_STEP * rate) for rate in rates]
    half = 0.5 * TIME_STEP * damping
    inverse = 1.0 / (1.0 + half)
    square = TIME_STEP * TIME_STEP
    kappa = square * speed_square * inverse
    return (
        kappa,
        kappa * retention[0],
        1.0 - retention[0],
        1.0 - retention[1],
        1.0 - retention[2],
        bits[0],
        bits[1],
        bits[2],
        jnp.exp(-TIME_STEP * damping),
        TIME_STEP * pairing,
        (2.0 - square * pairing) * inverse,
        (1.0 - half) * inverse,
        square * damping * inverse,
        square * inverse,
    )


def along_last(tiles, nz):
    row = lax.broadcasted_iota(jnp.int32, (nz, nz), 0)
    col = lax.broadcasted_iota(jnp.int32, (nz, nz), 1) // BLK
    along = (row == col).astype(F32).astype(BF16)
    return jnp.dot(tiles.astype(BF16), along, preferred_element_type=F32)


def tag_places(rows, lanes):
    return [
        (number * lanes, first, min(BLK, rows - first))
        for number, first in enumerate(range(0, rows, BLK))
    ]


def from_tag(tile, rows, lanes, nz):
    number = len(tag_places(rows, lanes))
    lane = lax.broadcasted_iota(jnp.int32, (nz, 2 * number * nz), 0)
    col = lax.broadcasted_iota(jnp.int32, (nz, 2 * number * nz), 1)
    along = (lane == col // nz * lanes + col % nz // BLK).astype(F32).astype(BF16)
    high = tile.astype(BF16).astype(F32)
    middle = (tile - high).astype(BF16).astype(F32)
    split = jnp.concatenate([high, middle, tile - high - middle, jnp.zeros_like(tile)], axis=0)
    wide = jnp.dot(split.astype(BF16), along, preferred_element_type=F32)
    wide = wide[:BLK] + wide[BLK : 2 * BLK] + wide[2 * BLK : 3 * BLK]
    columns = [wide[:, at * nz : (at + 1) * nz] for at in range(2 * number)]
    return [
        jnp.concatenate(columns[part * number : (part + 1) * number], axis=0) for part in range(2)
    ]


def squares(index, table):
    speed = jnp.zeros_like(index)
    for entry in range(table.shape[0]):
        speed = jnp.where(index == float(entry), table[entry], speed)
    return speed * speed


def bits_of(mask):
    mask = mask.astype(jnp.int32)
    return [((mask >> direction) & 1).astype(F32) for direction in range(3)]


def down_second(ref, lead, value, ny):
    for block in range(ny // BLK):
        rows = jnp.broadcast_to(value[block : block + 1], (BLK, value.shape[1]))
        ref[(*lead, pl.ds(block * BLK, BLK))] = rows


def fill_clock(clock, freq, start):
    steps = lax.broadcasted_iota(jnp.int32, clock.shape[1:], 0).astype(F32)
    cosine = jnp.cos(freq[0] * (start[0] + steps * TIME_STEP))
    weight = (TIME_STEP * freq[0] / math.pi) * (cosine - 0.25)
    for count in range(STEPS):
        clock[count] = jnp.broadcast_to(cosine[count : count + 1], cosine.shape)
        clock[STEPS + count] = jnp.broadcast_to(weight[count + 1 : count + 2], weight.shape)


def over_rows(ny, step):
    def one(block, carry):
        step(pl.multiple_of(block * BLK, BLK))
        return carry

    lax.fori_loop(0, ny // BLK, one, 0, unroll=4)


def is_even():
    return lax.axis_index("gx") % 2 == 0


def edge_planes(nx):
    return [*range(REACH), *range(nx - REACH, nx)]


def send_kernel(
    wave_in, layer_in, source_in, freq, start, table_in, index_in, mask_in,
    inside, across, coef, clock, edge, wave, layer, source,
    diff_y, diff_z, tags, tag_tiles, index, mask, table, sems,
):
    _, nx, ny, nz = wave.shape
    n_block = nx // BLK
    edges = (0, nx - REACH)
    pieces_of = [(wave_in.at[0], wave.at[0])]
    for first, length in ((0, REACH), (nx - REACH, REACH), (REACH, nx - 2 * REACH)):
        at = pl.ds(first, length)
        pieces_of += [
            (wave_in.at[1, at], wave.at[1, at]),
            (layer_in.at[:, at], layer.at[:, at]),
            (source_in.at[at], source.at[at]),
        ]
    copies = [
        pltpu.make_async_copy(one, to, sems.at[number])
        for number, (one, to) in enumerate(pieces_of)
    ]
    small = [
        pltpu.make_async_copy(one, to, sems.at[len(copies) + number])
        for number, (one, to) in enumerate(
            ((index_in, index), (mask_in, mask), (table_in, table))
        )
    ]
    for copy in small + copies:
        copy.start()
    even = is_even()
    tags[...] = jnp.zeros_like(tags)
    fill_clock(clock, freq, start)
    phase = clock[0]
    for copy in small:
        copy.wait()
    rows = n_block * TAG_ROWS
    for block in range(n_block):
        at = pl.ds(block * TAG_ROWS, index.shape[0])
        tags[0, at, : index.shape[2]] = index[:, block].astype(F32)
        tags[1, at, : mask.shape[2]] = mask[:, block].astype(F32)
    wide = along_last(tags[...].reshape(2 * rows, nz), nz)
    square = squares(wide[:rows], table)
    masks = wide[rows:]
    values = coefficients(square, bits_of(masks))
    for entry, value in enumerate(values):
        for block in range(n_block):
            down_second(coef, (entry, block), value[block * TAG_ROWS : (block + 1) * TAG_ROWS], ny)
    tag_tiles[...] = jnp.zeros_like(tag_tiles)
    places = tag_places(index.shape[0], index.shape[2])
    for side in range(2):
        block = side * (n_block - 1)
        speed = jnp.zeros(index.shape[::2], F32)
        for entry in range(table.shape[0]):
            speed = jnp.where(index[:, block] == entry, table[entry], speed)
        for part, value in enumerate((speed * speed, mask[:, block].astype(F32))):
            for lane, first, length in places:
                lane += part * len(places) * value.shape[1]
                tag_tiles[side, :length, lane : lane + value.shape[1]] = value[
                    first : first + length
                ]
    to = pl.ds(2 * REACH * ny, BLK)
    inside[to] = jnp.where(even, tag_tiles[1], tag_tiles[0])
    across[to] = jnp.where(even, tag_tiles[0], tag_tiles[1])
    copies[0].wait()
    planes = edge_planes(nx)
    slot = {plane: number for number, plane in enumerate(planes)}

    def put_y(plane, value):
        diff_y[slot[plane]] = value

    def put_z(plane, value):
        diff_z[slot[plane]] = value

    cross_diffs(planes, lambda plane: wave[0, plane], put_y, put_z, ny, nz)
    for copy in copies[1:7]:
        copy.wait()

    def step(rows):
        at = pl.ds(rows, BLK)
        sides = []
        for side in range(2):
            block = side * (n_block - 1)
            reach = range(2 * REACH) if side == 0 else range(nx - 2 * REACH, nx)
            cells = {plane: wave[0, plane, at] for plane in reach}
            values = []
            co = loaded(coef, block, at, phase)
            for number in range(REACH):
                plane = edges[side] + number
                new, memory, stiff = advance(
                    cells[plane],
                    wave[1, plane, at],
                    [layer[d, plane, at] for d in range(3)],
                    layer[3, plane, at],
                    source[plane, at],
                    [
                        first_diff(cells, plane),
                        diff_y[slot[plane], at],
                        diff_z[slot[plane], at],
                    ],
                    co,
                )
                for entry, value in enumerate((new, *memory, stiff)):
                    edge[side, entry, number, at] = value
                values.append((cells[plane], new))
            sides.append(values)
        for number in range(REACH):
            for part in range(2):
                to = pl.ds(pl.multiple_of((part * REACH + number) * ny + rows, BLK), BLK)
                left, right = sides[0][number][part], sides[1][number][part]
                inside[to] = jnp.where(even, right, left)
                across[to] = jnp.where(even, left, right)

    over_rows(ny, step)
    for copy in copies[7:]:
        copy.wait()


def local_kernel(
    wave, layer, source, coef, clock, edge,
    inside, across, first_out, second_out, run_out,
    fields, diff_y, diff_z,
):
    _, nx, ny, nz = wave.shape
    even = is_even()

    def put_y(plane, value):
        diff_y[plane] = value

    def put_z(plane, value):
        diff_z[plane] = value

    middle = range(REACH, nx - REACH)
    cross_diffs(middle, lambda plane: wave[0, plane], put_y, put_z, ny, nz)

    def read(entry, plane, at=slice(None)):
        if plane < REACH:
            return edge[0, entry, plane, at]
        if plane >= nx - REACH:
            return edge[1, entry, plane - nx + REACH, at]
        if entry == 0:
            return first_out[plane - REACH, at]
        return fields[entry - 1, plane - REACH, at]

    def first(rows):
        at = pl.ds(rows, BLK)
        co = [loaded(coef, block, at, clock[0]) for block in range(nx // BLK)]
        cells = {plane: wave[0, plane, at] for plane in range(nx)}
        for plane in middle:
            new, memory, stiff = advance(
                cells[plane],
                wave[1, plane, at],
                [layer[d, plane, at] for d in range(3)],
                layer[3, plane, at],
                source[plane, at],
                [first_diff(cells, plane), diff_y[plane, at], diff_z[plane, at]],
                co[plane // BLK],
            )
            first_out[plane - REACH, at] = new
            for entry, value in enumerate((*memory, stiff)):
                fields[entry, plane - REACH, at] = value

    over_rows(ny, first)
    cross_diffs(range(nx), lambda plane: read(0, plane), put_y, put_z, ny, nz)

    def second(rows):
        at = pl.ds(rows, BLK)
        co = [loaded(coef, block, at, clock[1]) for block in range(nx // BLK)]
        cells = {plane: read(0, plane, at) for plane in range(nx)}
        values = {}
        for plane in range(nx):
            new, memory, stiff = advance(
                cells[plane],
                wave[0, plane, at],
                [read(1 + d, plane, at) for d in range(3)],
                read(4, plane, at),
                source[plane, at],
                [first_diff(cells, plane), diff_y[plane, at], diff_z[plane, at]],
                co[plane // BLK],
            )
            values[plane] = new
            for entry, value in enumerate((new, *memory, stiff)):
                second_out[entry, plane, at] = value
            run_out[plane, at] = clock[STEPS] * cells[plane] + clock[STEPS + 1] * new
        for number in range(REACH):
            left, right = values[number], values[nx - REACH + number]
            inside[number, at] = jnp.where(even, right, left)
            across[number, at] = jnp.where(even, left, right)

    over_rows(ny, second)


def side_update(
    left, present, message, coef, clock, wave, running, edge, second_in, run_in,
    out_state, out_layer, out_filtered, ext, ghost,
    first, bump, push, ghost_coef, bump_y, bump_z,
):
    _, nx, ny, nz = wave.shape
    n_block = nx // BLK
    block = jnp.where(left, 0, n_block - 1)
    side = jnp.where(left, 0, 1)
    own = range(REACH)
    beyond = range(-1, -1 - REACH, -1)
    weights = [clock[STEPS + number] for number in range(2)]

    def plane_of(depth):
        return jnp.where(left, depth, nx - 1 - depth)

    def slot(depth):
        return depth if depth >= 0 else REACH - 1 - depth

    tag_at = 2 * REACH * ny
    tile = message[pl.ds(tag_at, BLK)]
    square, masks = from_tag(tile, ny // BLK, nz // BLK, nz)
    values = coefficients(square * present, bits_of(masks))
    for entry, value in enumerate(
        (
            values[KAPPA_R],
            values[Q0],
            values[KAPPA] * (1.0 - values[Q1]),
            values[KAPPA] * (1.0 - values[Q2]),
            values[AMP] - values[STIFF] * values[PAIR],
        )
    ):
        down_second(ghost_coef, (entry,), value, ny)

    def exchange(rows):
        at = pl.ds(rows, BLK)
        halo = {}
        sent = {}
        for depth in beyond:
            number = jnp.where(left, REACH + depth, -1 - depth)
            halo[depth] = message[pl.ds(pl.multiple_of(number * ny + rows, BLK), BLK)]
            number = number + REACH
            sent[depth] = message[pl.ds(pl.multiple_of(number * ny + rows, BLK), BLK)]
        mine = {depth: wave[0, plane_of(depth), at] for depth in own}
        kappa_r = coef[KAPPA_R, block, at]
        for depth in own:
            outer = outer_part(halo, depth, beyond)
            added = kappa_r * outer
            push[slot(depth), at] = outer
            bump[slot(depth), at] = added
            value = edge[side, 0, jnp.where(left, depth, REACH - 1 - depth), at] + added
            first[slot(depth), at] = value
            ext[jnp.where(left, depth, 2 * REACH - 1 - depth), at] = value
        kappa_r = ghost_coef[0, at]
        for depth in beyond:
            outer = outer_part(mine, depth, own)
            added = kappa_r * outer
            push[slot(depth), at] = outer
            bump[slot(depth), at] = added
            first[slot(depth), at] = sent[depth] + added

    over_rows(ny, exchange)

    def put_bump_y(plane, value):
        bump_y[plane] = value

    def put_bump_z(plane, value):
        bump_z[plane] = value

    cross_diffs(range(2 * REACH), lambda plane: bump[plane], put_bump_y, put_bump_z, ny, nz)

    def respond(added, true, depth, others, outer, q0, kappas, at):
        kappa_r, kappa_1, kappa_2, grown = kappas
        value = added[depth]
        rest = CENTRE_REST * value
        along = first_diff(added, depth) + outer_part(true, depth, others)
        side_y = bump_y[slot(depth), at] * (1.0 / SCALE) - rest
        side_z = bump_z[slot(depth), at] * (1.0 / SCALE) - rest
        gain = (
            grown * value + kappa_r * (along - q0 * outer) + kappa_1 * side_y + kappa_2 * side_z
        )
        return gain, along, side_y, side_z

    def second(rows):
        at = pl.ds(rows, BLK)
        true = {depth: first[slot(depth), at] for depth in (*own, *beyond)}
        added = {depth: bump[slot(depth), at] for depth in beyond}
        kappa_r, q0, kappa_1, kappa_2, grown = [ghost_coef[entry, at] for entry in range(5)]
        for depth in beyond:
            ghost[-1 - depth, at], _, _, _ = respond(
                added, true, depth, own, push[slot(depth), at], q0,
                (kappa_r, kappa_1, kappa_2, grown), at,
            )
        added = {depth: bump[slot(depth), at] for depth in own}
        kappa_r, kappa = coef[KAPPA_R, block, at], coef[KAPPA, block, at]
        q0, q1, q2 = [coef[entry, block, at] for entry in (Q0, Q1, Q2)]
        pair = coef[PAIR, block, at]
        kappas = (
            kappa_r,
            kappa * (1.0 - q1),
            kappa * (1.0 - q2),
            coef[AMP, block, at] - coef[STIFF, block, at] * pair,
        )
        for depth in own:
            plane = plane_of(depth)
            outer = push[slot(depth), at]
            gain, along, side_y, side_z = respond(
                added, true, depth, beyond, outer, q0, kappas, at
            )
            out_state[1, plane, at] = second_in[0, plane, at] + gain
            out_layer[0, plane, at] = second_in[1, plane, at] + q0 * (
                along + (1.0 - q0) * outer
            )
            out_layer[1, plane, at] = second_in[2, plane, at] + q1 * side_y
            out_layer[2, plane, at] = second_in[3, plane, at] + q2 * side_z
            out_layer[3, plane, at] = second_in[4, plane, at] + pair * added[depth]
            out_filtered[plane, at] = (
                running[plane, at]
                + run_in[plane, at]
                + weights[0] * added[depth]
                + weights[1] * gain
            )
        for depth in range(REACH, 2 * REACH):
            plane = plane_of(depth)
            along = outer_part(added, depth, own)
            gain = kappa_r * along
            out_state[1, plane, at] = second_in[0, plane, at] + gain
            out_layer[0, plane, at] = second_in[1, plane, at] + q0 * along
            out_filtered[plane, at] = running[plane, at] + run_in[plane, at] + weights[1] * gain

    over_rows(ny, second)


def inside_kernel(
    inside, coef, clock, wave, running, edge, second_in, run_in,
    out_state, out_layer, out_filtered, ext, ghost,
    *scratch,
):
    side_update(
        jnp.logical_not(is_even()), 1.0, inside, coef, clock, wave, running, edge, second_in,
        run_in, out_state, out_layer, out_filtered, ext, ghost, *scratch,
    )


def joint_kernel(
    across, coef, clock, wave, forcing, running, edge, first_in, second_in, run_in,
    state_in, layer_in, filtered_in, ext_in,
    out_state, out_layer, out_filtered, ext, ghost, partial,
    diff_y, diff_z, *scratch,
):
    del state_in, layer_in, filtered_in, ext_in
    _, nx, ny, nz = wave.shape
    count = lax.axis_size("gx")
    place = lax.axis_index("gx")
    even = is_even()
    weights = [clock[STEPS + number] for number in range(STEPS)]
    outermost = jnp.logical_or(place == 0, place == count - 1)
    side_update(
        even, jnp.where(outermost, 0.0, 1.0).astype(F32), across, coef, clock, wave, running,
        edge, second_in, run_in, out_state, out_layer, out_filtered, ext, ghost, *scratch,
    )
    if nx > 4 * REACH:

        def between(rows):
            at = pl.ds(rows, BLK)
            for plane in range(2 * REACH, nx - 2 * REACH):
                out_state[1, plane, at] = second_in[0, plane, at]
                out_layer[0, plane, at] = second_in[1, plane, at]
                out_filtered[plane, at] = running[plane, at] + run_in[plane, at]

        over_rows(ny, between)

    def put_y(plane, value):
        diff_y[plane] = value

    def put_z(plane, value):
        diff_z[plane] = value

    cross_diffs(range(nx), lambda plane: out_state[1, plane], put_y, put_z, ny, nz)
    partial[...] = jnp.zeros_like(partial)

    def third(rows):
        at = pl.ds(rows, BLK)
        co = [loaded(coef, block, at, clock[2]) for block in range(nx // BLK)]
        cells = {plane: out_state[1, plane, at] for plane in range(nx)}
        total = partial[...]
        for plane in range(nx):
            at_edge = plane < REACH or plane >= nx - REACH
            if at_edge:
                previous = ext[plane if plane < REACH else plane - nx + 2 * REACH, at]
                fields = [out_layer[d, plane, at] for d in range(4)]
            else:
                previous = first_in[plane - REACH, at]
                fields = [out_layer[0, plane, at]]
                fields += [second_in[1 + d, plane, at] for d in range(1, 4)]
            value, memory, stiff = advance(
                cells[plane],
                previous,
                fields[:3],
                fields[3],
                forcing[plane, at],
                [first_diff(cells, plane), diff_y[plane, at], diff_z[plane, at]],
                co[plane // BLK],
            )
            done = out_filtered[plane, at] + weights[2] * value
            for d in range(3):
                out_layer[d, plane, at] = memory[d]
            out_layer[3, plane, at] = stiff
            out_state[0, plane, at] = value
            out_filtered[plane, at] = done
            if not at_edge:
                total = total + done * done
        partial[...] = total

    over_rows(ny, third)


def finish_kernel(
    coef, clock, across, inside, across_late, ghost_inside, ghost_across, partial,
    state_in, layer_in, filtered_in,
    out_state, out_layer, out_filtered, total_out,
    gathered,
):
    _, nx, ny, _ = state_in.shape
    n_block = nx // BLK
    even = is_even()
    weight = clock[2 * STEPS - 1]
    gathered[...] = partial[...]
    ghosts = (range(-REACH, 0), range(nx, nx + REACH))
    owned = (range(REACH), range(nx - REACH, nx))

    def step(rows):
        at = pl.ds(rows, BLK)
        halo = {}
        for number in range(REACH):
            one = inside[number, at]
            two = across[number, at] + across_late[number, at]
            left = jnp.where(even, two, one)
            right = jnp.where(even, one, two)
            one, two = ghost_inside[REACH - 1 - number, at], ghost_across[REACH - 1 - number, at]
            halo[-REACH + number] = left + jnp.where(even, two, one)
            one, two = ghost_inside[number, at], ghost_across[number, at]
            halo[nx + number] = right + jnp.where(even, one, two)
        total = gathered[...]
        for side in range(2):
            block = side * (n_block - 1)
            kappa_r, q0 = coef[KAPPA_R, block, at], coef[Q0, block, at]
            for plane in owned[side]:
                outer = outer_part(halo, plane, ghosts[side])
                added = kappa_r * outer
                out_state[0, plane, at] = state_in[0, plane, at] + added
                out_layer[0, plane, at] = layer_in[0, plane, at] + q0 * outer
                done = filtered_in[plane, at] + weight * added
                out_filtered[plane, at] = done
                total = total + done * done
        gathered[...] = total

    over_rows(ny, step)
    total_out[...] = jnp.sum(gathered[...], axis=0, keepdims=True)


def store_kernel(parts, values, *refs):
    n = len(parts)
    arrays, outs, values_out, sems = refs[:n], refs[-n - 2 : -2], refs[-2], refs[-1]
    copies = [
        pltpu.make_async_copy(
            *((array, out) if at is None else (array.at[at], out.at[at])), sems.at[number]
        )
        for number, (at, array, out) in enumerate(zip(parts, arrays, outs))
    ]
    for copy in copies:
        copy.start()
    values_out[...] = values[...]
    for copy in copies:
        copy.wait()


def norm_kernel(cells, values, got, norm):
    total = jnp.sum(values[...] + got[...], axis=1, keepdims=True)
    total = jnp.sum(total, axis=0, keepdims=True)
    norm[...] = jnp.sqrt(total / cells + 1e-06)


SCALAR = pl.BlockSpec(memory_space=pltpu.SMEM)
HBM = pl.BlockSpec(memory_space=pltpu.HBM)
VEC = pl.BlockSpec(memory_space=pltpu.VMEM)


def held(*shape):
    return pltpu.VMEM(shape, F32)


def in_vmem(*arrays):
    return [pltpu.with_memory_space_constraint(array, pltpu.VMEM) for array in arrays]


def in_hbm(*arrays):
    return [pltpu.with_memory_space_constraint(array, pltpu.HBM) for array in arrays]


def call(kernel, name, in_specs, out_shape, out_specs, scratch, operands, micros, aliases=None):
    return pl.pallas_call(
        kernel,
        name=name,
        in_specs=in_specs,
        out_shape=out_shape,
        out_specs=out_specs,
        scratch_shapes=scratch,
        input_output_aliases=aliases or {},
        compiler_params=pltpu.CompilerParams(vmem_limit_bytes=VMEM_LIMIT),
        cost_estimate=pl.CostEstimate(
            flops=0, bytes_accessed=int(micros * 3.6e6), transcendentals=0
        ),
    )(*operands)


def swap_pairs(count):
    inside = [(i, i ^ 1) for i in range(count)]
    across = []
    for i in range(1, count - 1, 2):
        across += [(i, i + 1), (i + 1, i)]
    return inside, across


def halves(pairs):
    return [[pair for pair in pairs if min(pair) % 4 == first] for first in (1, 3)]


def store(values, parts, arrays, begun=()):
    n = len(arrays)
    outs = [jax.ShapeDtypeStruct(array.shape, F32) for array in arrays]
    *stored, values = call(
        functools.partial(store_kernel, parts),
        "store",
        [VEC] * (1 + n) + [HBM] * len(begun),
        [*outs, held(*values.shape)],
        [HBM] * n + [VEC],
        [pltpu.SemaphoreType.DMA((n,))],
        (*in_vmem(values, *arrays), *begun),
        1,
        {1 + n + number: n - len(begun) + number for number in range(len(begun))},
    )
    return values, stored


def norm_and_stores(values, state, layer, running, axis):
    count = lax.axis_size(axis)
    half = layer.shape[0] // 2
    stored = {}

    def first(values):
        values, (stored["state"],) = store(values, [None], [state])
        return values

    def second(values):
        values, (stored["layer"],) = store(values, [pl.ds(0, half)], [layer])
        return values

    def third(values):
        values, (stored["running"], stored["layer"]) = store(
            values, [None, pl.ds(half, half)], [running, layer], [stored["layer"]]
        )
        return values

    waiting = [first, second, third]
    hops = [] if count & (count - 1) else [1 << k for k in range(count.bit_length() - 1)]
    for number, hop in enumerate(hops):
        got = lax.ppermute(values, axis, [(i, i ^ hop) for i in range(count)])
        if waiting and number >= 1:
            values = waiting.pop(0)(values)
        if hop != hops[-1]:
            values = values + got
    for step in waiting:
        values = step(values)
    if not hops:
        values, got = lax.psum(values, axis), jnp.zeros_like(values)
    norm = call(
        functools.partial(norm_kernel, float(running.size * count)),
        "norm",
        [VEC] * 2,
        jax.ShapeDtypeStruct((1, 1), F32),
        VEC,
        [],
        in_vmem(values, got),
        1,
    )
    return norm.reshape(1), stored["state"], stored["layer"], stored["running"]


def body(
    wave_state, layer_fields, source, filtered, frequency, start_time, speed_table, speed_index,
    pml_mask,
):
    _, nx, ny, nz = wave_state.shape
    n_block = nx // BLK
    count = lax.axis_size("gx")
    pair_inside, pair_across = swap_pairs(count)
    brick = (nx, ny, nz)
    strip = (REACH, ny, nz)
    message = (2 * REACH * ny + BLK, nz)
    dma = pltpu.SemaphoreType.DMA
    vec = lambda *shape: pltpu.VMEM(shape, F32)

    blocks = (speed_index.shape[1], n_block, speed_index.shape[2])
    index, mask = in_hbm(*(jnp.transpose(one, (1, 0, 2)) for one in (speed_index, pml_mask)))

    inside, across, coef, clock, edge, wave, layer, forcing = call(
        send_kernel,
        "strips",
        [HBM] * 3 + [SCALAR] * 2 + [HBM] * 3,
        [
            held(*message), held(*message), held(N_COEF, n_block, ny, nz),
            held(2 * STEPS, BLK, nz), held(2, 5, *strip), held(*wave_state.shape),
            held(*layer_fields.shape), held(*brick),
        ],
        [VEC] * 8,
        [
            vec(2 * REACH, ny, nz),
            vec(2 * REACH, ny, nz),
            vec(2, n_block * TAG_ROWS, nz),
            vec(2, BLK, nz),
            pltpu.VMEM(blocks, jnp.int32),
            pltpu.VMEM(blocks, jnp.int32),
            pltpu.SMEM(speed_table.shape, F32),
            dma((13,)),
        ],
        (
            *in_hbm(wave_state, layer_fields, source), frequency, start_time,
            *in_hbm(speed_table), index, mask,
        ),
        2.5,
    )
    got_inside = lax.ppermute(inside, "gx", pair_inside)
    got_across = lax.ppermute(across, "gx", pair_across)
    coef, clock, edge, wave, layer, forcing, running = in_vmem(
        coef, clock, edge, wave, layer, forcing, filtered
    )

    later_inside, later_across, first, second, run = call(
        local_kernel,
        "local",
        [VEC] * 6,
        [
            held(*strip), held(*strip), held(nx - 2 * REACH, ny, nz), held(5, *brick),
            held(*brick),
        ],
        [VEC] * 5,
        [vec(4, nx - 2 * REACH, ny, nz), vec(*brick), vec(*brick)],
        (wave, layer, forcing, coef, clock, edge),
        4,
    )
    last_inside = lax.ppermute(later_inside, "gx", pair_inside)
    early_pairs, late_pairs = halves(pair_across)
    last_across = lax.ppermute(later_across, "gx", early_pairs)
    out_types = [
        held(*wave_state.shape), held(*layer_fields.shape), held(*filtered.shape)
    ]
    edge_type = held(2 * REACH, ny, nz)
    side_scratch = [vec(2 * REACH, ny, nz)] * 3 + [vec(5, ny, nz)] + [vec(2 * REACH, ny, nz)] * 2
    later_across, got_inside = lax.optimization_barrier((later_across, got_inside))
    last_late = lax.ppermute(later_across, "gx", late_pairs)
    first, second, run = in_vmem(first, second, run)
    next_state, next_layer, next_filtered, ext, ghost_inside = call(
        inside_kernel,
        "inner_half",
        [VEC] * 8,
        out_types + [edge_type, held(*strip)],
        [VEC] * 5,
        side_scratch,
        (*in_vmem(got_inside), coef, clock, wave, running, edge, second, run),
        1.5,
    )
    next_state, next_layer, next_filtered, ext, ghost_across, partial = call(
        joint_kernel,
        "joint",
        [VEC] * 14,
        out_types + [edge_type, held(*strip), held(BLK, nz)],
        [VEC] * 6,
        [vec(*brick), vec(*brick), *side_scratch],
        (
            *in_vmem(got_across), coef, clock, wave, forcing, running, edge, first, second, run,
            *in_vmem(next_state, next_layer, next_filtered, ext),
        ),
        5,
        {10: 0, 11: 1, 12: 2, 13: 3},
    )
    next_state, next_layer, next_filtered, total = call(
        finish_kernel,
        "finish",
        [VEC] * 11,
        out_types + [held(1, nz)],
        [VEC] * 4,
        [vec(BLK, nz)],
        (
            coef, clock,
            *in_vmem(
                last_across, last_inside, last_late, ghost_inside, ghost_across, partial,
                next_state, next_layer, next_filtered,
            ),
        ),
        1,
        {8: 0, 9: 1, 10: 2},
    )
    filter_norm, next_state, next_layer, next_filtered = norm_and_stores(
        total, next_state, next_layer, next_filtered, "gx"
    )
    return next_state, next_layer, next_filtered, filter_norm


def solution(mesh):
    placed = (
        P("grp", "gx", None, None),
        P("grp", "gx", None, None),
        P(("grp", "gx"), None, None),
        P(("grp", "gx"), None, None),
        P("grp"),
        P("grp"),
        P(),
        P("gx", None, None),
        P("gx", None, None),
    )
    return jax.shard_map(
        body,
        mesh=mesh,
        in_specs=placed,
        out_specs=(
            P("grp", "gx", None, None),
            P("grp", "gx", None, None),
            P(("grp", "gx"), None, None),
            P("grp"),
        ),
        check_vma=False,
    )
```
